128 devices in a mesh: expert: 32 (over z, y, core), head: 4 (over x).
Axes of the slice: x: 4, y: 4, z: 4, core: 2. Of those that a mesh axis runs over, the one named last changes fastest.
Arguments:
- tokens: bfloat16 [16384, 1024], P('expert'), may hold values from -6 to 6
- segment_ids: int32 [32, 512], P('expert'), may hold values from 0 to 3, never falling along the last dimension, each value on 1 to 256 neighbouring positions
- expert_of: int32 [16384, 1], P('expert'), may hold values from 0 to 63; in each aligned block of 512 rows (0 to 511, 512 to 1023, ...) at most 16 rows name the same one
- norm1_gain: float32 [1024], replicated, may hold values from 0.5 to 1.5
- norm1_bias: float32 [1024], replicated, may hold values from -0.6 to 0.6
- norm2_gain: float32 [1024], replicated, may hold values from 0.5 to 1.5
- norm2_bias: float32 [1024], replicated, may hold values from -0.6 to 0.6
- w_qkv: bfloat16 [3, 1024, 1024], P(None, None, 'head'), may hold values from -0.1875 to 0.1875
- w_out: bfloat16 [1024, 1024], P('head'), may hold values from -0.75 to 0.75
- w_in: bfloat16 [64, 1024, 4096], P('expert', None, 'head'), may hold values from -0.1875 to 0.1875
- w_back: bfloat16 [64, 4096, 1024], P('expert', 'head'), may hold values from -0.09375 to 0.09375
- cotangent: float32 [16384, 1024], P('expert'), may hold values from -6 to 6
Outputs:
- output: float32 [16384, 1024], P('expert')
- grad_tokens: float32 [16384, 1024], P('expert')
- grad_norm1_gain: float32 [1024], replicated
- grad_norm1_bias: float32 [1024], replicated
- grad_norm2_gain: float32 [1024], replicated
- grad_norm2_bias: float32 [1024], replicated
- grad_w_qkv: float32 [3, 1024, 1024], P(None, None, 'head')
- grad_w_out: float32 [1024, 1024], P('head')
- grad_w_in: float32 [64, 1024, 4096], P('expert', None, 'head')
- grad_w_back: float32 [64, 4096, 1024], P('expert', 'head')
The draws below stay inside these ranges and needn't reach their ends.
Inputs may be any that keep to these rules, and one draw needn't show every extreme that they name: `expert_of`: of the 512 tokens of one sequence, at most 16 have the same expert, and exactly 16 do for some expert in some sequence. `segment_ids`: along each sequence the segment numbers never fall; each segment covers 1 to 256 positions.
All inputs are finite; a program needn't handle non-finite values.
Results may differ from the reference program's by a relative error of at most 0.03.
Values may be sent and summed in bfloat16 or wider, within the bound.
A program may use at most 128 MiB of HBM per device.

```python
import math
import jax
import jax.numpy as jnp
import numpy as np
from jax import lax

D = 1024
HEADS = 16
HEAD_DIM = 64
FF = 4096
EXPERTS = 64
TOK_DEV = 512
SEQS = 32
TOKENS = 16384
MOST = 16
CAPACITY = 512
SEGMENTS = 4


def steps_of(own_key, extent, shards, low, high):
    level = 1.0
    for axis_at, shards_of in shards:
        steps = jax.random.uniform(jax.random.fold_in(jax.random.fold_in(own_key, 6), axis_at), (shards_of,), jnp.float32, low / len(shards), high / len(shards))
        level = level * jnp.repeat(jnp.exp(steps), extent[axis_at] // shards_of).reshape((-1,) + (1,) * (len(extent) - 1 - axis_at))
    return level


def length_profile(number_of, total, most, lean):
    loads = [(1 << 20) // math.isqrt(standing ** lean) + 1 for standing in range(2, number_of + 1)]
    spare, given = total - most - (number_of - 1), [1] * (number_of - 1)
    while spare > 0:
        movable = [i for i in range(number_of - 1) if given[i] < most]
        pool, left = sum([loads[i] for i in movable]), spare
        for i in movable:
            addition = min(most - given[i], max(1, left * loads[i] // pool), spare)
            given[i] = given[i] + addition
            spare = spare - addition
    return np.array([most] + given)


def uneven(stream_key, number_of, total, limit, slope):
    if number_of == 2:
        one = jax.random.randint(stream_key, (), max(1, total - limit), min(limit, total - 1) + 1)
        return jnp.stack([one, total - one])
    lengths = jnp.asarray(length_profile(number_of, total, limit, slope), jnp.int32)
    couples = (number_of - 1) // 2
    source_of, taker = lengths[1:1 + 2 * couples:2], lengths[2:2 + 2 * couples:2]
    margin = jnp.minimum(source_of - 1, limit - taker)
    moved = jax.random.randint(jax.random.fold_in(stream_key, 1), (couples,), 0, 1 << 20) % (margin + 1)
    lengths = lengths.at[1:1 + 2 * couples:2].set(source_of - moved).at[2:2 + 2 * couples:2].set(taker + moved)
    return lengths[jax.random.permutation(jax.random.fold_in(stream_key, 2), number_of)]


def assign_block(key, own, number, rows, count, top, most, skew):
    order = jax.random.permutation(key, count)
    heavy_load, usual = load_shares(count, rows * top, most, skew, True), load_shares(count, rows * top, most, skew, False)
    places = jnp.arange(count)

    def named(tallies, offset_by):
        used = int((tallies > 0).sum())
        fixed = max(1, used // 4)
        shifted = fixed + (places - fixed + offset_by * (used - fixed)) % max(1, count - fixed)
        return jnp.zeros((count,), jnp.int32).at[order[jnp.where(places < fixed, places, shifted)]].set(jnp.asarray(tallies, jnp.int32))

    tallies = jnp.where(number % 4 == 0, named(heavy_load, number // 4), named(usual, number - number // 4 - 1))
    mixed = jax.random.permutation(jax.random.fold_in(own, 3), count)
    donor, sink = mixed[0:count // 2 * 2:2], mixed[1:count // 2 * 2:2]
    slack = jnp.minimum(tallies[donor] - 1, most - tallies[sink]) // 2
    slack = jnp.where((donor == order[0]) | (sink == order[0]) | (tallies[sink] == 0), 0, jnp.maximum(slack, 0))
    shifted = jax.random.randint(jax.random.fold_in(own, 4), (count // 2,), 0, 1 << 20) % (slack + 1)
    tallies = tallies.at[donor].add(-shifted).at[sink].add(shifted)
    members = jnp.searchsorted(jnp.cumsum(tallies), jnp.arange(rows * top), side="right").astype(jnp.int32)
    table = members.reshape(top, rows).T
    table = table[jax.random.permutation(jax.random.fold_in(own, 1), rows)]
    offset_by = jax.random.randint(jax.random.fold_in(own, 2), (rows, 1), 0, top)
    return jnp.take_along_axis(table, (jnp.arange(top)[None, :] + offset_by) % top, axis=1)


def load_shares(amount, total, limit, lean, full):
    loads = [(1 << 20) // math.isqrt(standing ** lean) + 1 for standing in range(1, amount + 1)]
    largest = limit if full else min(limit, max(-(-total // amount), total * loads[0] // sum(loads)))
    least = 1 if total - largest >= amount - 1 else 0
    counts, surplus = [largest] + [least] * (amount - 1), total - largest - least * (amount - 1)
    while surplus > 0:
        candidates = [i for i in range(1, amount) if counts[i] < largest] or [i for i in range(1, amount) if counts[i] < limit]
        whole, left = sum([loads[i] for i in candidates]), surplus
        for i in candidates:
            addition = min(limit - counts[i], max(1, left * loads[i] // whole), surplus)
            counts[i] = counts[i] + addition
            surplus = surplus - addition
    return np.array(counts)


def normal_values(own_key, extent, scale, limit, split=(), held_as=jnp.bfloat16):
    drawn = scale * jax.random.normal(own_key, extent, jnp.float32)
    if split:
        drawn = drawn * steps_of(own_key, extent, split, -0.22, 0.18)
    return jnp.clip(drawn, -limit, limit).astype(held_as)


def setup_inputs(seed: int = 0) -> dict:
    keys = jax.random.split(jax.random.key(seed), 13)
    tokens = normal_values(keys[0], (TOKENS, D), 1.0, 6.0, ((0, 32),))
    segment_ids = jax.vmap(lambda own: jnp.searchsorted(jnp.cumsum(uneven(own, SEGMENTS, TOK_DEV, TOK_DEV // 2, 0)), jnp.arange(TOK_DEV), side="right"))(jax.random.split(keys[1], SEQS)).reshape((SEQS, TOK_DEV)).astype(jnp.int32)
    expert_of_keys = jax.random.split(jax.random.fold_in(keys[2], 1), TOKENS // TOK_DEV)
    expert_of_turns = jax.random.permutation(jax.random.fold_in(keys[2], 3), TOKENS // TOK_DEV)
    expert_of = jax.vmap(lambda own, number: assign_block(jax.random.fold_in(keys[2], 2), own, number, TOK_DEV, EXPERTS, 1, MOST, 2))(expert_of_keys, expert_of_turns).reshape((TOKENS, 1))
    norm1_gain = jnp.clip(1.0 + 0.1 * jax.random.normal(keys[3], (D,), jnp.float32), 0.5, 1.5)
    norm1_bias = normal_values(keys[4], (D,), 0.1, 0.6, (), jnp.float32)
    norm2_gain = jnp.clip(1.0 + 0.1 * jax.random.normal(keys[5], (D,), jnp.float32), 0.5, 1.5)
    norm2_bias = normal_values(keys[6], (D,), 0.1, 0.6, (), jnp.float32)
    w_qkv = normal_values(keys[7], (3, D, D), D ** -0.5, 0.1875, ((2, 4),))
    w_out = normal_values(keys[8], (D, D), (D // 16) ** -0.5, 0.75, ((0, 4),))
    w_in = normal_values(keys[9], (EXPERTS, D, FF), D ** -0.5, 0.1875, ((0, 32), (2, 4)))
    w_back = normal_values(keys[10], (EXPERTS, FF, D), FF ** -0.5, 0.09375, ((0, 32), (1, 4)))
    cotangent = normal_values(keys[11], (TOKENS, D), 1.0, 6.0, ((0, 32),), jnp.float32)
    return dict(tokens=tokens, segment_ids=segment_ids, expert_of=expert_of, norm1_gain=norm1_gain, norm1_bias=norm1_bias, norm2_gain=norm2_gain, norm2_bias=norm2_bias, w_qkv=w_qkv, w_out=w_out, w_in=w_in, w_back=w_back, cotangent=cotangent)


@jax.custom_vjp
def low(v):
    return lax.optimization_barrier(v.astype(jnp.bfloat16)).astype(jnp.float32)

@jax.custom_vjp
def low_back(v):
    return v

def low_keep(v):
    return (low(v), None)

def low_pass(kept, grad):
    return (grad,)

def back_keep(v):
    return (v, None)

def back_low(kept, grad):
    return (low(grad),)
low.defvjp(low_keep, low_pass)
low_back.defvjp(back_keep, back_low)
HIGH = lax.Precision.HIGHEST

def layer_norm(stream, gain, bias):
    center = stream - lax.optimization_barrier(jnp.mean(stream, axis=-1, keepdims=True))
    spread = lax.optimization_barrier(jnp.mean(center * center, axis=-1, keepdims=True))
    return center * lax.rsqrt(spread + 1e-05) * gain + bias

def activate(values):
    return jax.nn.gelu(values, approximate=True)

def attend(packed):
    triple, segment = packed
    query = triple[0].reshape(TOK_DEV, HEADS, HEAD_DIM)
    key_rows = triple[1].reshape(TOK_DEV, HEADS, HEAD_DIM)
    value_rows = triple[2].reshape(TOK_DEV, HEADS, HEAD_DIM)
    scores = low_back(jnp.einsum('qhd,khd->hqk', query, key_rows, precision=HIGH) * HEAD_DIM ** (-0.5))
    position = jnp.arange(TOK_DEV, dtype=jnp.int32)
    allowed = (position[:, None] >= position[None, :]) & (segment[:, None] == segment[None, :])
    scores = jnp.where(allowed[None], scores, -1e+30)
    row_top = lax.optimization_barrier(jnp.max(scores, axis=-1, keepdims=True))
    exponent = jnp.exp(scores - row_top)
    chances = exponent / lax.optimization_barrier(jnp.sum(exponent, axis=-1, keepdims=True))
    mixed = jnp.einsum('hqk,khd->qhd', low(chances), value_rows, precision=HIGH)
    return mixed.reshape(TOK_DEV, D)

def expert_apply(packed):
    rows_in, first, second = packed
    pre_act = low_back(jnp.dot(rows_in, first, precision=HIGH))
    hidden = low(activate(pre_act))
    return jnp.dot(hidden, second, precision=HIGH)

def reference(tokens, segment_ids, expert_of, norm1_gain, norm1_bias, norm2_gain, norm2_bias, w_qkv, w_out, w_in, w_back, cotangent):
    route = expert_of[:, 0].astype(jnp.int32)
    onehot = (route[:, None] == jnp.arange(EXPERTS, dtype=jnp.int32)[None, :]).astype(jnp.int32)
    earlier = jnp.cumsum(onehot, axis=0) - onehot
    rank = lax.optimization_barrier(jnp.sum(earlier * onehot, axis=1))
    slot_index = route * CAPACITY + rank

    def forward(stream, gain1, bias1, gain2, bias2, proj_qkv, proj_out, first, second):
        normed = low(layer_norm(stream, gain1, bias1))
        qkv = low_back(low(jnp.einsum('td,cdf->ctf', normed, proj_qkv, precision=HIGH)))
        per_seq = qkv.reshape(3, SEQS, TOK_DEV, D).transpose(1, 0, 2, 3)
        mixed = lax.map(jax.checkpoint(attend), (per_seq, segment_ids)).reshape(TOKENS, D)
        mixed = low_back(low(mixed))
        attended = low_back(jnp.dot(mixed, proj_out, precision=HIGH))
        resid = stream + attended
        normed2 = low_back(low(layer_norm(resid, gain2, bias2)))
        buffer = jnp.zeros((EXPERTS * CAPACITY, D), jnp.float32).at[slot_index].set(normed2)
        buffer = buffer.reshape(EXPERTS, CAPACITY, D)
        outs = lax.map(jax.checkpoint(expert_apply), (buffer, first, second)).reshape(EXPERTS * CAPACITY, D)
        expert_out = low_back(low(outs[slot_index]))
        return resid + expert_out
    primals = (tokens.astype(jnp.float32), norm1_gain, norm1_bias, norm2_gain, norm2_bias, w_qkv.astype(jnp.float32), w_out.astype(jnp.float32), w_in.astype(jnp.float32), w_back.astype(jnp.float32))
    output, pullback = jax.vjp(forward, *primals)
    grads = pullback(cotangent)
    return (output, grads[0], grads[1], grads[2], grads[3], grads[4], grads[5], grads[6], grads[7], grads[8])
```

```python
import functools

import jax
import jax.numpy as jnp
from jax import lax
from jax.experimental import pallas as pl
from jax.experimental.pallas import tpu as pltpu
from jax.sharding import PartitionSpec as P

f32 = jnp.float32
bf16 = jnp.bfloat16
i32 = jnp.int32
MESH = pl.DeviceIdType.MESH

T = 512
D = 1024
G = 32
H = 4
Q = T // H
HALF = D // 2
EPS = 1e-5


def mm(a, b):
    return lax.dot_general(a, b, (((1,), (0,)), ((), ())), preferred_element_type=f32)


def mm_nt(a, b):
    return lax.dot_general(a, b, (((1,), (1,)), ((), ())), preferred_element_type=f32)


def iota(shape, dim):
    return lax.broadcasted_iota(i32, shape, dim)


def hot(cond):
    return jnp.where(cond, 1.0, 0.0).astype(bf16)


def rem4(v):
    return lax.rem(v, 4)


def remote(src, dst, send_sem, recv_sem, device):
    return pltpu.make_async_remote_copy(
        src_ref=src,
        dst_ref=dst,
        send_sem=send_sem,
        recv_sem=recv_sem,
        device_id=device,
        device_id_type=MESH,
    )


def columns(ref, rows):
    half = ref.shape[1] // 2
    return lambda b, hf: ref.at[pl.ds(pl.multiple_of(b * rows, rows), rows), pl.ds(hf * half, half)]


class ReduceScatter:
    def __init__(self, ring, part, relay, total, arrived, send, recv):
        self.me, right, left = ring
        self.right, self.left = rem4(self.me + 1), rem4(self.me + 3)
        far = rem4(self.me + 2)
        self.part, self.relay, self.total, self.arrived = part, relay, total, arrived
        self.far = [
            remote(part(far, 0), relay(0), send.at[0], recv.at[0], left),
            remote(part(far, 1), relay(1), send.at[1], recv.at[1], right),
        ]
        self.near = [
            remote(part(self.left, 1), arrived(1, 1), send.at[2], recv.at[2], left),
            remote(part(self.right, 0), arrived(0, 0), send.at[3], recv.at[3], right),
        ]
        self.last = [
            remote(total(0), arrived(1, 0), send.at[4], recv.at[4], left),
            remote(total(1), arrived(0, 1), send.at[5], recv.at[5], right),
        ]

    def send_far(self, hf):
        self.far[hf].start()

    def send_near(self, side):
        self.near[side].start()

    def pass_on(self):
        for hf, owner in ((0, self.left), (1, self.right)):
            self.far[hf].wait_recv()
            mine = self.part(owner, hf)[...].astype(f32)
            self.total(hf)[...] = (mine + self.relay(hf)[...].astype(f32)).astype(bf16)
            self.last[hf].start()

    def wait(self):
        for copy in self.near + self.last:
            copy.wait_recv()

    def value(self, hf):
        mine = self.part(self.me, hf)[...].astype(f32)
        return mine + self.arrived(0, hf)[...].astype(f32) + self.arrived(1, hf)[...].astype(f32)

    def wait_sent(self):
        for copy in self.far + self.near + self.last:
            copy.wait_send()


class Gather:
    def __init__(self, ring, block, send, recv):
        me, right, left = ring
        on_right, on_left = rem4(me + 1), rem4(me + 3)

        def copy(b, hf, i, device):
            return remote(block(b, hf), block(b, hf), send.at[i], recv.at[i], device)

        self.first = [copy(me, 0, 0, right), copy(me, 1, 1, left)]
        self.second = [copy(me, 0, 2, left), copy(me, 1, 3, right)]
        self.third = [copy(on_left, 0, 4, right), copy(on_right, 1, 5, left)]

    def start(self):
        for copy in self.first + self.second:
            copy.start()

    def pass_on(self, hf):
        self.first[hf].wait_recv()
        self.third[hf].start()

    def wait_second(self, hf):
        self.second[hf].wait_recv()

    def wait_third(self, hf):
        self.third[hf].wait_recv()

    def finish(self):
        self.pass_on(0)
        self.pass_on(1)
        for copy in self.second + self.third:
            copy.wait_recv()

    def wait_sent(self):
        for copy in self.first + self.second + self.third:
            copy.wait_send()


def norm_parts(x):
    center = x - jnp.mean(x, axis=-1, keepdims=True)
    r = lax.rsqrt(jnp.mean(center * center, axis=-1, keepdims=True) + EPS)
    return center * r, r


def norm_back(g, xhat, r):
    return r * (
        g - jnp.mean(g, axis=-1, keepdims=True) - xhat * jnp.mean(g * xhat, axis=-1, keepdims=True)
    )


def gelu_parts(v):
    c = 0.7978845608028654
    v2 = v * v
    t = jnp.tanh(c * v * (1.0 + 0.044715 * v2))
    half = 0.5 * (1.0 + t)
    grad = half + 0.5 * v * (1.0 - t * t) * c * (1.0 + 3.0 * 0.044715 * v2)
    return v * half, grad


def as_tile(row):
    return jnp.concatenate([row[:, i * 128 : (i + 1) * 128] for i in range(8)], axis=0)


def layer_kernel(
    seg_ref, route_ref, g1_ref, b1_ref, g2_ref, b2_ref,
    tok_hbm, wqkv_hbm, wout_hbm, win_hbm, wbk_hbm, cot_hbm,
    x_out, g_out, hid_out, dpre_out, u_out, gt_out, w_out, nrm_out,
    tok, wqkv, wout, win, wbk, cotw, cot_low,
    pm, pmt, code_c, code_r, slot_c, slot_r,
    csend, crecv, gal,
    xp, normed, normed_t, qkv, q_t, chs, mixed, mixed_t,
    apart, a_rel, a_sum, a_arr,
    nsend, nrecv, xall, hid, dpre, n2p,
    e_rel, e_sum, e_arr, esend, erecv,
    o_rel, o_sum, o_arr, osend, orecv, outall,
    datt, dmx, dm_t, dqkv,
    d_rel, d_sum, d_arr, gtall,
    wpart, wx, ws,
    w0, w0_rel, w0_sum, w0_arr, w1, w1_rel, w1_sum, w1_arr,
    w2_rel, w2_sum, w2_arr, w3_rel, w3_sum, w3_arr,
    nv, nrx, nye,
    loc, cs, cr, ns, nr, es, er, os_, or_, rss, rsr, ags, agr, xs, xr, vs, vr, vys, vyr,
):
    me = lax.axis_index("expert")
    h = lax.axis_index("head")
    core = lax.rem(me, 2)
    chip = me // 2
    y = lax.rem(chip, 4)
    z = chip // 4

    def at_yz(yy, zz, cc):
        return {"expert": (rem4(zz) * 4 + rem4(yy)) * 2 + cc}

    ring_x = (h, {"head": rem4(h + 1)}, {"head": rem4(h + 3)})
    ring_y = (y, at_yz(y + 1, z, core), at_yz(y + 3, z, core))
    ring_z = (z, at_yz(y, z + 1, core), at_yz(y, z + 3, core))
    sibling = {"expert": chip * 2 + 1 - core}
    left, right, far = rem4(h + 3), rem4(h + 1), rem4(h + 2)

    att_q, dres = cotw.at[pl.ds(0, Q), :], cotw.at[pl.ds(Q, Q), :]
    npart = tok
    dss = [tok.at[:, pl.ds(0, T)], tok.at[:, pl.ds(T, T)]]

    def outp(q, e):
        return csend.at[e, pl.ds(pl.multiple_of(q * Q, Q), Q), :]

    loads = {}
    for i, (name, src, dst) in enumerate(
        (
            ("cot", cot_hbm, cotw),
            ("tok", tok_hbm, tok),
            ("wqkv", wqkv_hbm, wqkv),
            ("wout", wout_hbm, wout),
            ("win", win_hbm, win),
            ("wbk", wbk_hbm, wbk),
        )
    ):
        loads[name] = pltpu.make_async_copy(src, dst, loc.at[i])
        loads[name].start()

    barrier = pltpu.get_barrier_semaphore()

    @pl.loop(1, G)
    def _(k):
        pl.semaphore_signal(
            barrier, inc=1, device_id={"expert": lax.rem(me + k, G)}, device_id_type=MESH
        )

    for k in range(1, H):
        pl.semaphore_signal(barrier, inc=1, device_id={"head": rem4(h + k)}, device_id_type=MESH)

    route_c = route_ref[...]
    eye = iota((T, T), 0) == iota((T, T), 1)

    def to_row(col):
        return jnp.sum(jnp.where(eye, col.astype(f32), 0.0), axis=0, keepdims=True)

    onehot = jnp.where(iota((T, 128), 1) == route_c, 1.0, 0.0)
    before = hot(iota((T, T), 1) < iota((T, T), 0))
    rank = jnp.sum(mm(before, onehot.astype(bf16)) * onehot, axis=1, keepdims=True)
    count = jnp.broadcast_to(jnp.sum(onehot, axis=0, keepdims=True), (8, 128)).astype(bf16)
    first = mm(count, hot(iota((128, 128), 0) < iota((128, 128), 1)))[0:1]
    place = (jnp.sum(onehot * first, axis=1, keepdims=True) + rank).astype(i32)
    rank4 = rank.astype(i32) >> 2
    quarter = place & 3
    pos_c = quarter * Q + (place >> 2)
    slot4 = route_c * 4 + rank4
    key = (route_c & 1) * T + (route_c >> 1) * 16 + quarter * 4 + rank4
    pos_r = to_row(pos_c).astype(i32)
    key_r = to_row(key).astype(i32)
    perm = iota((T, T), 0) == pos_r
    perm_t = iota((T, T), 1) == pos_c
    pm[...] = hot(perm)
    pmt[...] = hot(perm_t)
    code = (seg_ref[...] * 1024 + iota((1, T), 1)).astype(f32)
    code_pc = jnp.sum(jnp.where(perm, code, 0.0), axis=1, keepdims=True)
    code_c[...] = code_pc.astype(i32)
    code_r[...] = to_row(code_pc).astype(i32)
    own_t = iota((T, Q), 1) + h * Q == pos_c
    slot_row = jnp.sum(jnp.where(own_t, slot4.astype(f32), 0.0), axis=0, keepdims=True)
    slot_r[...] = slot_row.astype(i32)
    eye_q = iota((Q, Q), 0) == iota((Q, Q), 1)
    slot_c[...] = jnp.sum(jnp.where(eye_q, slot_row, 0.0), axis=1, keepdims=True).astype(i32)

    pl.semaphore_wait(barrier, G - 1 + H - 1)

    loads["cot"].wait()
    cot_low[...] = cotw[...].astype(bf16)

    def cot_copy(d):
        return remote(
            csend.at[:, pl.ds(pl.multiple_of(d * 16, 16), 16), :],
            crecv.at[:, pl.ds(pl.multiple_of(me * 16, 16), 16), :],
            cs.at[d], cr.at[me], {"expert": d},
        )

    def cot_arrived(d):
        return remote(
            csend.at[:, pl.ds(pl.multiple_of(d * 16, 16), 16), :],
            crecv.at[:, pl.ds(pl.multiple_of(d * 16, 16), 16), :],
            cs.at[d], cr.at[d], {"expert": d},
        )

    def row_copy(src, dst, send, recv):
        def to(d):
            return remote(
                src.at[pl.ds(pl.multiple_of(d * 16, 16), 16), :],
                dst.at[pl.ds(pl.multiple_of(me * 16, 16), 16), :],
                send.at[d], recv.at[me], {"expert": d},
            )

        def arrived(d):
            return remote(
                src.at[pl.ds(pl.multiple_of(d * 16, 16), 16), :],
                dst.at[pl.ds(pl.multiple_of(d * 16, 16), 16), :],
                send.at[d], recv.at[d], {"expert": d},
            )

        return to, arrived

    def start_chunk(to, chunk):
        @pl.loop(0, 8)
        def _(k):
            d = chunk * 8 + lax.rem(me + k, 8)

            @pl.when(d != me)
            def _():
                to(d).start()

    def others(act):
        @pl.loop(1, G)
        def _(k):
            act(lax.rem(me + k, G))

    @pl.loop(0, 4)
    def _(c):
        chunk = rem4(me // 8 + c)
        row0 = pl.multiple_of(chunk * 128, 128)
        for e in range(2):
            sel = hot(iota((128, T), 0) + (row0 + e * T) == key_r)
            csend[e, pl.ds(row0, 128), :] = mm(sel, cot_low[...]).astype(bf16)
        start_chunk(cot_copy, chunk)

    own16 = pl.ds(pl.multiple_of(me * 16, 16), 16)
    crecv[:, own16, :] = csend[:, own16, :]

    loads["tok"].wait()

    @pl.loop(0, 4)
    def _(rb):
        rows = pl.ds(pl.multiple_of(rb * Q, Q), Q)
        x = mm(pm[rows, :], tok[...])
        xp[rows, :] = x.astype(bf16)
        xhat, _r = norm_parts(x)
        normed[rows, :] = (xhat * g1_ref[...] + b1_ref[...]).astype(bf16)

    loads["wqkv"].wait()

    @pl.loop(0, 3)
    def _(c):
        qkv[c] = mm(normed[...], wqkv[c]).astype(bf16)

    for hp in range(2):
        pair = slice(hp * 128, hp * 128 + 128)

        @pl.loop(0, 4)
        def _(rb):
            rows = pl.ds(pl.multiple_of(rb * Q, Q), Q)
            codes = code_c[rows, :]
            keys = code_r[...]
            allowed = (keys <= codes) & (keys >= ((codes >> 10) << 10))
            outs = []
            for hh in range(2):
                lanes = slice(hp * 128 + hh * 64, hp * 128 + hh * 64 + 64)
                s = mm_nt(qkv[0, rows, lanes], qkv[1, :, lanes]) * 0.125
                s = jnp.where(allowed, s, -1e30)
                e = jnp.exp(s - jnp.max(s, axis=-1, keepdims=True))
                ch = (e * (1.0 / jnp.sum(e, axis=-1, keepdims=True))).astype(bf16)
                chs[hp * 2 + hh, rows, :] = ch
                outs.append(mm(ch, qkv[2, :, lanes]))
            mixed[rows, pair] = jnp.concatenate(outs, axis=1).astype(bf16)

    loads["wout"].wait()
    halves = lambda ref: (lambda hf: ref.at[hf])
    sides = lambda ref: (lambda side, hf: ref.at[side, hf])
    rs_a = ReduceScatter(
        ring_x, columns(apart, Q), halves(a_rel), halves(a_sum), sides(a_arr), rss.at[0], rsr.at[0]
    )

    def project(b):
        rows = pl.ds(pl.multiple_of(b * Q, Q), Q)
        apart[rows, :] = mm(mixed[rows, :], wout[...]).astype(bf16)

    project(far)
    rs_a.send_far(0)
    rs_a.send_far(1)
    project(left)
    rs_a.send_near(0)
    project(right)
    rs_a.send_near(1)
    project(h)
    own_rows = pl.ds(pl.multiple_of(h * Q, Q), Q)

    rs_a.pass_on()
    q_t[...] = qkv[0].astype(f32).T.astype(bf16)
    mixed_t[...] = mixed[...].astype(f32).T.astype(bf16)

    @pl.loop(0, 4)
    def _(c):
        cols = pl.ds(pl.multiple_of(c * 256, 256), 256)
        normed_t[cols, :] = normed[:, cols].astype(f32).T.astype(bf16)

    rs_a.wait()
    att_q[...] = jnp.concatenate([rs_a.value(0), rs_a.value(1)], axis=1)

    def resid_norm():
        return norm_parts(xp[own_rows, :].astype(f32) + att_q[...])

    xhat2, _r2 = resid_norm()
    normed2 = (xhat2 * g2_ref[...] + b2_ref[...]).astype(bf16)
    n_to, n_arrived = row_copy(nsend, nrecv, ns, nr)

    def pick_halves(full, row0):
        low_half = ((iota((128, HALF), 0) + row0) & 8) == 0
        return jnp.where(low_half, full[:, :HALF], full[:, HALF:]).astype(bf16)

    for c in range(4):
        chunk = rem4(me // 8 + c)
        row0 = pl.multiple_of(chunk * 128, 128)
        r = iota((128, Q), 0) + row0
        sel = hot((r >> 4) * 8 + (r & 7) == slot_r[...])
        nsend[pl.ds(row0, 128), :] = pick_halves(mm(sel, normed2), row0)
        start_chunk(n_to, chunk)
    nrecv[own16, :] = nsend[own16, :]

    others(lambda d: cot_arrived(d).wait_recv())

    @pl.loop(0, 4)
    def _(q):
        i = iota((128, T), 0)
        sel = hot((i >> 2) * 16 + (i & 3) + q * 4 == iota((128, T), 1))
        for e in range(2):
            gal[q, e] = mm(sel, crecv[e]).astype(bf16)

    others(lambda d: n_arrived(d).wait_recv())
    ag_x = Gather(ring_x, lambda b, hf: xall.at[b, hf], ags.at[0], agr.at[0])
    for e in range(2):
        i = iota((128, T), 0)
        target = (i >> 2) * 16 + e * 4 + (i & 3)
        for hf in range(2):
            sel = hot(iota((128, T), 1) == target + hf * 8)
            xall[h, e, :, hf * HALF : (hf + 1) * HALF] = mm(sel, nrecv[...]).astype(bf16)
    ag_x.start()

    loads["win"].wait()
    loads["wbk"].wait()
    others(lambda d: cot_copy(d).wait_send())

    def unit(q, e):
        @pl.loop(0, 4)
        def _(c):
            cols = pl.ds(pl.multiple_of(c * 256, 256), 256)
            act, slope = gelu_parts(mm(xall[q, e], win[e, :, cols]))
            hid[q, e, :, cols] = act.astype(bf16)
            dpre[q, e, :, cols] = (mm_nt(gal[q, e], wbk[e, cols, :]) * slope).astype(bf16)

    def unit_n2(q, e):
        @pl.loop(0, 4)
        def _(c):
            cols = pl.ds(pl.multiple_of(c * 256, 256), 256)
            n2p[q, e, :, cols] = mm_nt(dpre[q, e], win[e, cols, :]).astype(bf16)

    def unit_out(q, e):
        @pl.loop(0, 4)
        def _(c):
            cols = pl.ds(pl.multiple_of(c * 256, 256), 256)
            outp(q, e)[:, cols] = mm(hid[q, e], wbk[e, :, cols]).astype(bf16)

    rs_e = ReduceScatter(
        ring_x, lambda b, hf: n2p.at[b, hf], halves(e_rel), halves(e_sum), sides(e_arr),
        rss.at[1], rsr.at[1],
    )
    rs_o = ReduceScatter(
        ring_x, outp, halves(o_rel), halves(o_sum), sides(o_arr),
        rss.at[2], rsr.at[2],
    )

    def whole(q, e):
        unit(q, e)
        unit_n2(q, e)
        unit_out(q, e)

    whole(h, 0)
    whole(h, 1)
    ag_x.pass_on(0)
    ag_x.pass_on(1)
    whole(left, 0)
    whole(right, 1)
    ag_x.wait_second(0)
    whole(right, 0)
    rs_e.send_near(1)
    ag_x.wait_second(1)
    whole(left, 1)
    rs_e.send_near(0)
    ag_x.wait_third(0)
    unit(far, 0)
    unit_n2(far, 0)
    rs_e.send_far(0)
    ag_x.wait_third(1)
    unit(far, 1)
    unit_n2(far, 1)
    rs_e.send_far(1)
    unit_out(far, 0)
    unit_out(far, 1)

    outs = [(xall, x_out), (gal, g_out), (hid, hid_out), (dpre, dpre_out)]
    stores = [pltpu.make_async_copy(a, b, loc.at[6 + i]) for i, (a, b) in enumerate(outs)]
    for copy in stores:
        copy.start()

    rs_e.pass_on()
    rs_e.wait()
    rs_o.send_far(0)
    rs_o.send_far(1)
    rs_o.send_near(0)
    rs_o.send_near(1)

    def send_back(rs, buf, to):
        value = jnp.concatenate([rs.value(0), rs.value(1)], axis=0).astype(bf16)
        for c in range(4):
            chunk = rem4(me // 8 + c)
            row0 = pl.multiple_of(chunk * 128, 128)
            r = iota((128, 256), 0) + row0
            sel = hot(((r >> 2) & 1) * 128 + (r >> 4) * 4 + (r & 3) == iota((128, 256), 1))
            buf[pl.ds(row0, 128), :] = pick_halves(mm(sel, value), row0)
            start_chunk(to, chunk)

    def to_tokens(buf):
        slots = slot_c[...]
        target = (slots >> 3) * 16 + (slots & 7)
        lanes = iota((Q, T), 1)
        low = mm(hot(lanes == target), buf[...])
        return jnp.concatenate([low, mm(hot(lanes == target + 8), buf[...])], axis=1)

    e_to, e_arrived = row_copy(esend, erecv, es, er)
    o_to, o_arrived = row_copy(osend, orecv, os_, or_)
    send_back(rs_e, esend, e_to)
    erecv[own16, :] = esend[own16, :]

    sel_own = hot(iota((Q, T), 0) + h * Q == iota((Q, T), 1))
    cot_q = mm(mm(sel_own, pm[...]).astype(bf16), cot_low[...])
    others(lambda d: e_arrived(d).wait_recv())
    dn2 = to_tokens(erecv)
    xhat2, r2 = resid_norm()
    nv[2] = as_tile(jnp.sum(dn2 * xhat2, axis=0, keepdims=True))
    nv[3] = as_tile(jnp.sum(dn2, axis=0, keepdims=True))
    d_resid = cot_q + norm_back(dn2 * g2_ref[...], xhat2, r2)
    dres[...] = d_resid
    datt[own_rows, :] = d_resid.astype(bf16)
    ag_d = Gather(ring_x, columns(datt, Q), ags.at[1], agr.at[1])
    ag_d.start()
    ag_d.finish()

    dmx[...] = mm_nt(datt[...], wout[...]).astype(bf16)
    dm_t[...] = dmx[...].astype(f32).T.astype(bf16)

    @pl.loop(0, 4)
    def _(c):
        cols = pl.ds(pl.multiple_of(c * 256, 256), 256)
        rows = pl.ds(pl.multiple_of(c * 256, 256), 256)
        wpart[rows, 768:1024] = mm(mixed_t[...], datt[:, cols]).astype(bf16)

    rs_o.pass_on()

    for hp in range(2):
        pair = slice(hp * 128, hp * 128 + 128)

        @pl.loop(0, 4)
        def _(rb):
            rows = pl.ds(pl.multiple_of(rb * Q, Q), Q)
            dqs = []
            for hh in range(2):
                lanes = slice(hp * 128 + hh * 64, hp * 128 + hh * 64 + 64)
                dch = mm_nt(dmx[rows, lanes], qkv[2, :, lanes])
                ch = chs[hp * 2 + hh, rows, :].astype(f32)
                inner = jnp.sum(ch * dch, axis=-1, keepdims=True)
                ds = (ch * (dch - inner)).astype(bf16)
                dss[hh][rows, :] = ds
                dqs.append(mm(ds, qkv[1, :, lanes]) * 0.125)
            dqkv[0, rows, pair] = jnp.concatenate(dqs, axis=1).astype(bf16)

        dks, dvs = [], []
        for hh in range(2):
            lanes = slice(hp * 128 + hh * 64, hp * 128 + hh * 64 + 64)
            dks.append(mm(q_t[lanes, :], dss[hh][...]) * 0.125)
            dvs.append(mm(dm_t[lanes, :], chs[hp * 2 + hh]))
        dqkv[1, :, pair] = jnp.concatenate(dks, axis=0).T.astype(bf16)
        dqkv[2, :, pair] = jnp.concatenate(dvs, axis=0).T.astype(bf16)
        if hp == 0:
            rs_o.wait()
            send_back(rs_o, osend, o_to)
            orecv[own16, :] = osend[own16, :]

    rs_d = ReduceScatter(
        ring_x, columns(npart, Q), halves(d_rel), halves(d_sum), sides(d_arr), rss.at[3], rsr.at[3]
    )

    def input_grad(b):
        rows = pl.ds(pl.multiple_of(b * Q, Q), Q)
        total = mm_nt(dqkv[0, rows, :], wqkv[0])
        for c in (1, 2):
            total += mm_nt(dqkv[c, rows, :], wqkv[c])
        npart[rows, :] = total.astype(bf16)

    input_grad(far)
    rs_d.send_far(0)
    rs_d.send_far(1)
    input_grad(left)
    rs_d.send_near(0)
    input_grad(right)
    rs_d.send_near(1)
    input_grad(h)

    for c in range(3):
        wpart[:, c * 256 : (c + 1) * 256] = mm(normed_t[...], dqkv[c]).astype(bf16)

    core_rows = pl.ds(pl.multiple_of(core * T, T), T)
    other_rows = pl.ds(pl.multiple_of((1 - core) * T, T), T)
    swap = remote(wpart.at[other_rows, :], wx, xs.at[0], xr.at[0], sibling)
    swap.start()
    rs_d.pass_on()
    swap.wait_recv()
    ws[...] = (wpart[core_rows, :].astype(f32) + wx[...].astype(f32)).astype(bf16)
    ws0, ws1 = ws.at[pl.ds(0, 256), :], ws.at[pl.ds(256, 256), :]
    rs_w0 = ReduceScatter(
        ring_y, columns(ws0, 64), halves(w0_rel), halves(w0_sum), sides(w0_arr), rss.at[4], rsr.at[4]
    )
    rs_w1 = ReduceScatter(
        ring_z, columns(ws1, 64), halves(w1_rel), halves(w1_sum), sides(w1_arr), rss.at[5], rsr.at[5]
    )
    rs_w2 = ReduceScatter(
        ring_z, columns(w0, 16), halves(w2_rel), halves(w2_sum), sides(w2_arr), rss.at[6], rsr.at[6]
    )
    rs_w3 = ReduceScatter(
        ring_y, columns(w1, 16), halves(w3_rel), halves(w3_sum), sides(w3_arr), rss.at[7], rsr.at[7]
    )

    def start_all(rs):
        rs.send_far(0)
        rs.send_far(1)
        rs.send_near(0)
        rs.send_near(1)

    start_all(rs_w0)
    start_all(rs_w1)

    others(lambda d: o_arrived(d).wait_recv())
    outall[own_rows, :] = (att_q[...] + to_tokens(orecv)).astype(bf16)
    ag_o = Gather(ring_x, columns(outall, Q), ags.at[2], agr.at[2])

    rs_d.wait()
    dn1 = jnp.concatenate([rs_d.value(0), rs_d.value(1)], axis=1)
    xhat1, r1 = norm_parts(xp[own_rows, :].astype(f32))
    gtall[own_rows, :] = (dres[...] + norm_back(dn1 * g1_ref[...], xhat1, r1)).astype(bf16)
    ag_g = Gather(ring_x, columns(gtall, Q), ags.at[3], agr.at[3])
    ag_g.start()
    ag_o.start()
    nv[0] = as_tile(jnp.sum(dn1 * xhat1, axis=0, keepdims=True))
    nv[1] = as_tile(jnp.sum(dn1, axis=0, keepdims=True))

    nx = [remote(nv.at[rem4(h + k)], nrx.at[h], vs.at[k], vr.at[h], {"head": rem4(h + k)})
          for k in (1, 2, 3)]
    nx_in = [remote(nv.at[0], nrx.at[rem4(h + k)], vs.at[k], vr.at[rem4(h + k)], {"head": rem4(h + k)})
             for k in (1, 2, 3)]
    for copy in nx:
        copy.start()

    rs_w0.pass_on()
    rs_w1.pass_on()
    ag_g.pass_on(0)
    ag_g.pass_on(1)

    for copy in nx_in:
        copy.wait_recv()
    nye[me] = nv[h] + nrx[rem4(h + 1)] + nrx[rem4(h + 2)] + nrx[rem4(h + 3)]

    def n_all(d):
        return remote(nye.at[me], nye.at[me], vys.at[d], vyr.at[me], {"expert": d})

    def n_all_in(d):
        return remote(nye.at[me], nye.at[d], vys.at[d], vyr.at[d], {"expert": d})

    others(lambda d: n_all(d).start())

    rs_w0.wait()
    w0[...] = jnp.concatenate([rs_w0.value(0), rs_w0.value(1)], axis=1).astype(bf16)
    start_all(rs_w2)
    rs_w1.wait()
    w1[...] = jnp.concatenate([rs_w1.value(0), rs_w1.value(1)], axis=1).astype(bf16)
    start_all(rs_w3)
    ag_o.pass_on(0)
    ag_o.pass_on(1)
    rs_w2.pass_on()
    rs_w3.pass_on()

    base = core * T
    row_y = pl.multiple_of(base + y * 64, 64)
    row_z = pl.multiple_of(base + 256 + z * 64, 64)
    ag_w2 = Gather(ring_z, columns(w_out.at[pl.ds(row_y, 64), :], 16), ags.at[4], agr.at[4])
    ag_w3 = Gather(ring_y, columns(w_out.at[pl.ds(row_z, 64), :], 16), ags.at[5], agr.at[5])
    ag_w0 = Gather(
        ring_y, columns(w_out.at[pl.ds(pl.multiple_of(base, 256), 256), :], 64), ags.at[6], agr.at[6]
    )
    ag_w1 = Gather(
        ring_z, columns(w_out.at[pl.ds(pl.multiple_of(base + 256, 256), 256), :], 64), ags.at[7], agr.at[7]
    )
    rs_w2.wait()
    w_out[pl.ds(pl.multiple_of(row_y + z * 16, 16), 16), :] = jnp.concatenate(
        [rs_w2.value(0), rs_w2.value(1)], axis=1
    ).astype(bf16)
    ag_w2.start()
    rs_w3.wait()
    w_out[pl.ds(pl.multiple_of(row_z + y * 16, 16), 16), :] = jnp.concatenate(
        [rs_w3.value(0), rs_w3.value(1)], axis=1
    ).astype(bf16)
    ag_w3.start()

    others(lambda d: n_all_in(d).wait_recv())
    nrm_out[h] = jnp.sum(nye[...], axis=0)
    nf = [remote(nrm_out.at[h], nrm_out.at[h], vs.at[3 + k], vr.at[4 + h], {"head": rem4(h + k)})
          for k in (1, 2, 3)]
    nf_in = [
        remote(nrm_out.at[h], nrm_out.at[rem4(h + k)], vs.at[3 + k], vr.at[4 + rem4(h + k)],
               {"head": rem4(h + k)})
        for k in (1, 2, 3)
    ]
    for copy in nf:
        copy.start()

    ag_w2.finish()
    ag_w0.start()
    ag_w3.finish()
    ag_w1.start()

    for hf in range(2):
        ag_g.wait_second(hf)
        ag_g.wait_third(hf)

    def restore(dst, src):
        @pl.loop(0, 4)
        def _(c):
            cols = pl.ds(pl.multiple_of(c * 256, 256), 256)
            dst[:, cols] = mm(pmt[...], src[:, cols]).astype(bf16)

    restore(xp, gtall)
    gt_store = pltpu.make_async_copy(xp, gt_out, loc.at[10])
    gt_store.start()
    ag_w0.finish()
    ag_w1.finish()
    both = remote(w_out.at[core_rows, :], w_out.at[core_rows, :], xs.at[1], xr.at[1], sibling)
    both_in = remote(w_out.at[core_rows, :], w_out.at[other_rows, :], xs.at[1], xr.at[1], sibling)
    both.start()
    for hf in range(2):
        ag_o.wait_second(hf)
        ag_o.wait_third(hf)
    restore(normed, outall)
    u_store = pltpu.make_async_copy(normed, u_out, loc.at[11])
    u_store.start()
    both_in.wait_recv()
    for copy in nf_in:
        copy.wait_recv()

    others(lambda d: n_to(d).wait_send())
    others(lambda d: e_to(d).wait_send())
    others(lambda d: o_to(d).wait_send())
    others(lambda d: n_all(d).wait_send())
    for group in (rs_a, rs_e, rs_o, rs_d, rs_w0, rs_w1, rs_w2, rs_w3,
                  ag_x, ag_d, ag_o, ag_g, ag_w0, ag_w1, ag_w2, ag_w3):
        group.wait_sent()
    swap.wait_send()
    both.wait_send()
    for copy in nx + nf:
        copy.wait_send()
    for copy in stores + [gt_store, u_store]:
        copy.wait()


def layer(seg, route, g1, b1, g2, b2, tok, wqkv, wout, win, wbk, cot):
    vmem = pl.BlockSpec(memory_space=pltpu.VMEM)
    hbm = pl.BlockSpec(memory_space=pl.ANY)
    V = pltpu.VMEM
    DMA = pltpu.SemaphoreType.DMA

    def rs_bufs(rows, cols):
        return [V((2, rows, cols), bf16), V((2, rows, cols), bf16), V((2, 2, rows, cols), bf16)]

    scratch = [
        V((T, D), bf16), V((3, D, 256), bf16), V((256, D), bf16), V((2, D, D), bf16),
        V((2, D, D), bf16), V((T, D), f32), V((T, D), bf16),
        V((T, T), bf16), V((T, T), bf16), V((T, 1), i32), V((1, T), i32), V((Q, 1), i32),
        V((1, Q), i32),
        V((2, T, D), bf16), V((2, T, D), bf16), V((4, 2, Q, D), bf16),
        V((T, D), bf16), V((T, D), bf16), V((D, T), bf16), V((3, T, 256), bf16),
        V((256, T), bf16), V((4, T, T), bf16), V((T, 256), bf16), V((256, T), bf16),
        V((T, D), bf16), *rs_bufs(Q, HALF),
        V((T, HALF), bf16), V((T, HALF), bf16), *[V((4, 2, Q, D), bf16)] * 4,
        *rs_bufs(Q, D), V((T, HALF), bf16), V((T, HALF), bf16),
        *rs_bufs(Q, D), V((T, HALF), bf16), V((T, HALF), bf16), V((T, D), bf16),
        V((T, D), bf16), V((T, 256), bf16), V((256, T), bf16), V((3, T, 256), bf16),
        *rs_bufs(Q, HALF), V((T, D), bf16),
        V((D, D), bf16), V((T, D), bf16), V((T, D), bf16),
        V((64, D), bf16), *rs_bufs(64, HALF), V((64, D), bf16), *rs_bufs(64, HALF),
        *rs_bufs(16, HALF), *rs_bufs(16, HALF),
        V((4, 8, 128), f32), V((4, 8, 128), f32), V((G, 8, 128), f32),
        DMA((12,)), *[DMA((G,))] * 8, *[DMA((8, 6))] * 4, DMA((2,)), DMA((2,)),
        DMA((8,)), DMA((8,)), DMA((G,)), DMA((G,)),
    ]
    S = jax.ShapeDtypeStruct
    quarters = S((4, 2, Q, D), bf16)
    return pl.pallas_call(
        layer_kernel,
        name="layer",
        out_shape=[quarters] * 4
        + [S((T, D), bf16), S((T, D), bf16), S((D, D), bf16), S((4, 8, 128), f32)],
        in_specs=[vmem] * 6 + [hbm] * 6,
        out_specs=[hbm] * 6 + [vmem] * 2,
        scratch_shapes=scratch,
        compiler_params=pltpu.CompilerParams(
            collective_id=0, has_side_effects=True, vmem_limit_bytes=62 << 20
        ),
        cost_estimate=pl.CostEstimate(
            flops=24 * 10**9, bytes_accessed=30 * 2**20, transcendentals=4 * 10**6
        ),
    )(seg, route, g1, b1, g2, b2, tok, wqkv, wout, win, wbk, cot)


def outer_kernel(x_ref, dpre_ref, hid_ref, g_ref, win_out, wback_out):
    def outer(lhs, rhs, out):
        a = lhs[...].reshape(T, 256)
        b = rhs[...].reshape(T, D)
        out[0] = lax.dot_general(a, b, (((0,), (0,)), ((), ())), preferred_element_type=f32)

    outer(x_ref, dpre_ref, win_out)
    outer(hid_ref, g_ref, wback_out)


def expert_weight_grads(x, dpre, hid, g):
    lhs = pl.BlockSpec((4, 1, Q, 256), lambda e, c: (0, e, 0, c))
    rhs = pl.BlockSpec((4, 1, Q, D), lambda e, c: (0, e, 0, 0))
    out = pl.BlockSpec((1, 256, D), lambda e, c: (e, c, 0))
    shape = jax.ShapeDtypeStruct((2, D, D), f32)
    return pl.pallas_call(
        outer_kernel,
        name="expert_weight_grads",
        grid=(2, 4),
        out_shape=[shape, shape],
        in_specs=[lhs, rhs, lhs, rhs],
        out_specs=[out, out],
        compiler_params=pltpu.CompilerParams(vmem_limit_bytes=40 << 20),
        cost_estimate=pl.CostEstimate(
            flops=8 * 2**30, bytes_accessed=24 * 2**20, transcendentals=0
        ),
    )(x, dpre, hid, g)


def per_device(
    tokens, segment_ids, expert_of, norm1_gain, norm1_bias, norm2_gain, norm2_bias,
    w_qkv, w_out, w_in, w_back, cotangent,
):
    row = lambda v: v.reshape(1, D)
    x, g, hid, dpre, u, gt, w, nrm = layer(
        segment_ids, expert_of, row(norm1_gain), row(norm1_bias), row(norm2_gain), row(norm2_bias),
        tokens, w_qkv, w_out, w_in, w_back, cotangent,
    )
    grad_w_in, grad_w_back = expert_weight_grads(x, dpre, hid, g)
    output = tokens.astype(f32) + u.astype(f32)
    grad_tokens = gt.astype(f32)
    w = w.astype(f32)
    grad_w_qkv = jnp.moveaxis(w[:, :768].reshape(D, 3, 256), 1, 0)
    grad_w_out = jnp.moveaxis(w[:, 768:].reshape(4, 256, 256), 0, 1).reshape(256, D)
    vectors = nrm.reshape(4, D)
    return (
        output, grad_tokens, vectors[0], vectors[1], vectors[2], vectors[3],
        grad_w_qkv, grad_w_out, grad_w_in, grad_w_back,
    )


def solution(mesh):
    return jax.shard_map(
        per_device,
        mesh=mesh,
        in_specs=(
            P("expert", None),
            P("expert", None),
            P("expert", None),
            P(),
            P(),
            P(),
            P(),
            P(None, None, "head"),
            P("head", None),
            P("expert", None, "head"),
            P("expert", "head", None),
            P("expert", None),
        ),
        out_specs=(
            P("expert", None),
            P("expert", None),
            P(),
            P(),
            P(),
            P(),
            P(None, None, "head"),
            P("head", None),
            P("expert", None, "head"),
            P("expert", "head", None),
        ),
        check_vma=False,
    )
```

```python
import functools

import jax
import jax.numpy as jnp
from jax import lax
from jax.experimental import pallas as pl
from jax.experimental.pallas import tpu as pltpu
from jax.sharding import PartitionSpec as P

f32 = jnp.float32
bf16 = jnp.bfloat16
i32 = jnp.int32
MESH = pl.DeviceIdType.MESH

T = 512
D = 1024
G = 32
H = 4
Q = T // H
HALF = D // 2
EPS = 1e-5


def mm(a, b):
    return lax.dot_general(a, b, (((1,), (0,)), ((), ())), preferred_element_type=f32)


def mm_nt(a, b):
    return lax.dot_general(a, b, (((1,), (1,)), ((), ())), preferred_element_type=f32)


def iota(shape, dim):
    return lax.broadcasted_iota(i32, shape, dim)


def hot(cond):
    return jnp.where(cond, 1.0, 0.0).astype(bf16)


def rem4(v):
    return lax.rem(v, 4)


def remote(src, dst, send_sem, recv_sem, device):
    return pltpu.make_async_remote_copy(
        src_ref=src,
        dst_ref=dst,
        send_sem=send_sem,
        recv_sem=recv_sem,
        device_id=device,
        device_id_type=MESH,
    )


def columns(ref, rows):
    half = ref.shape[1] // 2
    return lambda b, hf: ref.at[pl.ds(pl.multiple_of(b * rows, rows), rows), pl.ds(hf * half, half)]


class ReduceScatter:
    def __init__(self, ring, whole, rows, relay, total, arrived, sems):
        self.me, right, left = ring
        self.right, self.left = rem4(self.me + 1), rem4(self.me + 3)
        far = rem4(self.me + 2)
        self.part = part = columns(whole, rows)
        self.relay, self.total, self.arrived = relay, total, arrived
        self.three, self.two = whole.at[pl.ds(0, 3 * rows), :], whole.at[pl.ds(0, 2 * rows), :]
        self.sems, self.left_device = sems, left
        send, rest = sems.at[0], sems.at[3]
        self.far = [
            remote(part(far, 0), relay.at[0], send, sems.at[1], left),
            remote(part(far, 1), relay.at[1], send, sems.at[2], right),
        ]
        self.near = [
            remote(part(self.left, 1), arrived.at[1, 1], send, rest, left),
            remote(part(self.right, 0), arrived.at[0, 0], send, rest, right),
        ]
        self.last = [
            remote(total.at[0], arrived.at[1, 0], send, rest, left),
            remote(total.at[1], arrived.at[0, 1], send, rest, right),
        ]

    def send_all(self):
        for copy in self.far + self.near:
            copy.start()

    def pass_on(self):
        for hf, owner in ((0, self.left), (1, self.right)):
            self.far[hf].wait_recv()
            mine = self.part(owner, hf)[...].astype(f32)
            self.total[hf] = (mine + self.relay[hf].astype(f32)).astype(bf16)
            self.last[hf].start()

    def wait(self):
        all_of(self.two, self.sems.at[0], self.sems.at[3], self.left_device).wait_recv()

    def value(self):
        def half(hf):
            mine = self.part(self.me, hf)[...].astype(f32)
            return mine + self.arrived[0, hf].astype(f32) + self.arrived[1, hf].astype(f32)

        return jnp.concatenate([half(0), half(1)], axis=1)

    def wait_sent(self):
        all_of(self.three, self.sems.at[0], self.sems.at[3], self.left_device).wait_send()


class Gather:
    def __init__(self, ring, whole, rows, sems):
        me, right, left = ring
        on_right, on_left = rem4(me + 1), rem4(me + 3)
        block = columns(whole, rows)
        self.three, self.two = whole.at[pl.ds(0, 3 * rows), :], whole.at[pl.ds(0, 2 * rows), :]
        self.sems, self.left_device = sems, left

        def copy(b, hf, i, device):
            return remote(block(b, hf), block(b, hf), sems.at[0], sems.at[i], device)

        self.first = [copy(me, 0, 1, right), copy(me, 1, 2, left)]
        self.second = [copy(me, 0, 3, left), copy(me, 1, 3, right)]
        self.third = [copy(on_left, 0, 3, right), copy(on_right, 1, 3, left)]

    def start(self):
        for copy in self.first + self.second:
            copy.start()

    def pass_on(self):
        for hf in range(2):
            self.first[hf].wait_recv()
            self.third[hf].start()

    def wait_rest(self):
        all_of(self.two, self.sems.at[0], self.sems.at[3], self.left_device).wait_recv()

    def finish(self):
        self.pass_on()
        self.wait_rest()

    def wait_sent(self):
        all_of(self.three, self.sems.at[0], self.sems.at[3], self.left_device).wait_send()


class Exchange:
    def __init__(self, me, src, dst, sems):
        self.me, self.src, self.dst, self.sems = me, src, dst, sems
        rows = pl.ds(0, 16 * (G - 1))
        index = (slice(None),) * (len(src.shape) - 2) + (rows, slice(None))
        other = {"expert": lax.rem(me + 1, G)}
        self.all = remote(src.at[index], dst.at[index], sems.at[0], sems.at[1], other)

    def block(self, ref, d):
        rows = pl.ds(pl.multiple_of(d * 16, 16), 16)
        return ref.at[(slice(None),) * (len(ref.shape) - 2) + (rows, slice(None))]

    def start_chunk(self, chunk):
        @pl.loop(0, 8)
        def _(k):
            d = chunk * 8 + lax.rem(self.me + k, 8)

            @pl.when(d != self.me)
            def _():
                remote(
                    self.block(self.src, d), self.block(self.dst, self.me),
                    self.sems.at[0], self.sems.at[1], {"expert": d},
                ).start()

    def keep_own(self):
        self.block(self.dst, self.me)[...] = self.block(self.src, self.me)[...]


def all_of(view, send_sem, recv_sem, device):
    return remote(view, view, send_sem, recv_sem, device)


def norm_parts(x):
    center = x - jnp.mean(x, axis=-1, keepdims=True)
    r = lax.rsqrt(jnp.mean(center * center, axis=-1, keepdims=True) + EPS)
    return center * r, r


def norm_back(g, xhat, r):
    return r * (
        g - jnp.mean(g, axis=-1, keepdims=True) - xhat * jnp.mean(g * xhat, axis=-1, keepdims=True)
    )


def gelu_parts(v):
    c = 0.7978845608028654
    v2 = v * v
    t = jnp.tanh(c * v * (1.0 + 0.044715 * v2))
    half = 0.5 * (1.0 + t)
    grad = half + 0.5 * v * (1.0 - t * t) * c * (1.0 + 3.0 * 0.044715 * v2)
    return v * half, grad


def as_tile(row):
    return jnp.concatenate([row[:, i * 128 : (i + 1) * 128] for i in range(8)], axis=0)


def layer_kernel(
    seg_ref, route_ref, g1_ref, b1_ref, g2_ref, b2_ref,
    tok_hbm, wqkv_hbm, wout_hbm, win_hbm, wbk_hbm, cot_hbm,
    x_out, g_out, hid_out, dpre_out, u_out, gt_out, w_out, nrm_out,
    tok, wqkv, wout, win, wbk, cotw, cot_low,
    pm, pmt, code_c, code_r, slot_c, slot_r,
    csend, crecv, gal,
    xp, normed, normed_t, qkv, q_t, chs, mixed, mixed_t,
    apart, a_rel, a_sum, a_arr,
    norm2, nsend, nrecv, xall, hid, dpre, n2p,
    e_rel, e_sum, e_arr, esend, erecv,
    o_rel, o_sum, o_arr, osend, orecv, outall,
    datt, dmx, dm_t, dqkv,
    d_rel, d_sum, d_arr, gtall,
    wx,
    w0, w0_rel, w0_sum, w0_arr, w1, w1_rel, w1_sum, w1_arr,
    w2_rel, w2_sum, w2_arr, w3_rel, w3_sum, w3_arr,
    nv, nrx, nye,
    loc, cs, ns, es, os_, rss, ags, xs, vs,
):
    me = lax.axis_index("expert")
    h = lax.axis_index("head")
    core = lax.rem(me, 2)
    chip = me // 2
    y = lax.rem(chip, 4)
    z = chip // 4

    def at_yz(yy, zz, cc):
        return {"expert": (rem4(zz) * 4 + rem4(yy)) * 2 + cc}

    ring_x = (h, {"head": rem4(h + 1)}, {"head": rem4(h + 3)})
    ring_y = (y, at_yz(y + 1, z, core), at_yz(y + 3, z, core))
    ring_z = (z, at_yz(y, z + 1, core), at_yz(y, z + 3, core))
    sibling = {"expert": chip * 2 + 1 - core}
    left, right, far = rem4(h + 3), rem4(h + 1), rem4(h + 2)

    att_q, dres = cotw.at[pl.ds(0, Q), :], cotw.at[pl.ds(Q, Q), :]
    npart = tok
    ws = cot_low
    wpart = gal
    dss = [tok.at[:, pl.ds(0, T)], tok.at[:, pl.ds(T, T)]]
    outp = csend

    loads = {}
    for i, (name, src, dst) in enumerate(
        (
            ("cot", cot_hbm, cotw),
            ("tok", tok_hbm, tok),
            ("wqkv", wqkv_hbm, wqkv),
            ("wout", wout_hbm, wout),
            ("win", win_hbm, win),
            ("wbk", wbk_hbm, wbk),
        )
    ):
        loads[name] = pltpu.make_async_copy(src, dst, loc.at[i])
        loads[name].start()

    barrier = pltpu.get_barrier_semaphore()

    @pl.loop(1, G)
    def _(k):
        pl.semaphore_signal(
            barrier, inc=1, device_id={"expert": lax.rem(me + k, G)}, device_id_type=MESH
        )

    for k in range(1, H):
        pl.semaphore_signal(barrier, inc=1, device_id={"head": rem4(h + k)}, device_id_type=MESH)

    eye = iota((T, T), 0) == iota((T, T), 1)
    route_row = route_ref[...].astype(f32)
    route_c = jnp.sum(jnp.where(eye, route_row, 0.0), axis=1, keepdims=True).astype(i32)

    def to_row(col):
        return jnp.sum(jnp.where(eye, col.astype(f32), 0.0), axis=0, keepdims=True)

    onehot = jnp.where(iota((T, 128), 1) == route_c, 1.0, 0.0)
    before = hot(iota((T, T), 1) < iota((T, T), 0))
    rank = jnp.sum(mm(before, onehot.astype(bf16)) * onehot, axis=1, keepdims=True)
    count = jnp.broadcast_to(jnp.sum(onehot, axis=0, keepdims=True), (8, 128)).astype(bf16)
    first = mm(count, hot(iota((128, 128), 0) < iota((128, 128), 1)))[0:1]
    place = (jnp.sum(onehot * first, axis=1, keepdims=True) + rank).astype(i32)
    rank4 = rank.astype(i32) >> 2
    quarter = place & 3
    pos_c = quarter * Q + (place >> 2)
    slot4 = route_c * 4 + rank4
    key = (route_c & 1) * T + (route_c >> 1) * 16 + quarter * 4 + rank4
    pos_r = to_row(pos_c).astype(i32)
    key_r = to_row(key).astype(i32)
    perm = iota((T, T), 0) == pos_r
    perm_t = iota((T, T), 1) == pos_c
    pm[...] = hot(perm)
    pmt[...] = hot(perm_t)
    code = (seg_ref[...] * 1024 + iota((1, T), 1)).astype(f32)
    code_pc = jnp.sum(jnp.where(perm, code, 0.0), axis=1, keepdims=True)
    code_c[...] = code_pc.astype(i32)
    code_r[...] = to_row(code_pc).astype(i32)
    own_t = iota((T, Q), 1) + h * Q == pos_c
    slot_row = jnp.sum(jnp.where(own_t, slot4.astype(f32), 0.0), axis=0, keepdims=True)
    slot_r[...] = slot_row.astype(i32)
    eye_q = iota((Q, Q), 0) == iota((Q, Q), 1)
    slot_c[...] = jnp.sum(jnp.where(eye_q, slot_row, 0.0), axis=1, keepdims=True).astype(i32)

    pl.semaphore_wait(barrier, G - 1 + H - 1)

    loads["cot"].wait()
    cot_low[...] = cotw[...].astype(bf16)

    def others(act):
        @pl.loop(1, G)
        def _(k):
            act(lax.rem(me + k, G))

    def exchange(src, dst, sems):
        return [Exchange(me, src.at[e], dst.at[e], sems.at[e]) for e in range(2)]

    cot_x = Exchange(me, csend, crecv, cs)

    @pl.loop(0, 4)
    def _(c):
        chunk = rem4(me // 8 + c)
        row0 = pl.multiple_of(chunk * 128, 128)
        r = iota((256, T), 0)
        sel = hot(row0 + (r & 127) + (r >> 7) * T == key_r)
        rows = mm(sel, cot_low[...]).astype(bf16)
        for e in range(2):
            csend[e, pl.ds(row0, 128), :] = rows[e * 128 : e * 128 + 128]
        cot_x.start_chunk(chunk)

    cot_x.keep_own()

    loads["tok"].wait()

    @pl.loop(0, 4)
    def _(rb):
        rows = pl.ds(pl.multiple_of(rb * Q, Q), Q)
        x = mm(pm[rows, :], tok[...])
        xp[rows, :] = x.astype(bf16)
        xhat, _r = norm_parts(x)
        normed[rows, :] = (xhat * g1_ref[...] + b1_ref[...]).astype(bf16)

    loads["wqkv"].wait()

    @pl.loop(0, 3)
    def _(c):
        qkv[c] = mm(normed[...], wqkv[c]).astype(bf16)

    for hp in range(2):
        pair = slice(hp * 128, hp * 128 + 128)

        @pl.loop(0, 4)
        def _(rb):
            rows = pl.ds(pl.multiple_of(rb * Q, Q), Q)
            codes = code_c[rows, :]
            keys = code_r[...]
            allowed = (keys <= codes) & (keys >= ((codes >> 10) << 10))
            outs = []
            for hh in range(2):
                lanes = slice(hp * 128 + hh * 64, hp * 128 + hh * 64 + 64)
                s = mm_nt(qkv[0, rows, lanes], qkv[1, :, lanes]) * 0.125
                s = jnp.where(allowed, s, -1e30)
                e = jnp.exp(s - jnp.max(s, axis=-1, keepdims=True))
                ch = (e * (1.0 / jnp.sum(e, axis=-1, keepdims=True))).astype(bf16)
                chs[hp * 2 + hh, rows, :] = ch
                outs.append(mm(ch, qkv[2, :, lanes]))
            mixed[rows, pair] = jnp.concatenate(outs, axis=1).astype(bf16)

    loads["wout"].wait()
    rs_a = ReduceScatter(ring_x, apart, Q, a_rel, a_sum, a_arr, rss.at[0])

    def project(b):
        rows = pl.ds(pl.multiple_of(b * Q, Q), Q)
        apart[rows, :] = mm(mixed[rows, :], wout[...]).astype(bf16)

    project(far)
    for copy in rs_a.far:
        copy.start()
    project(left)
    rs_a.near[0].start()
    project(right)
    rs_a.near[1].start()
    project(h)
    own_rows = pl.ds(pl.multiple_of(h * Q, Q), Q)

    rs_a.pass_on()
    q_t[...] = qkv[0].astype(f32).T.astype(bf16)
    mixed_t[...] = mixed[...].astype(f32).T.astype(bf16)

    @pl.loop(0, 4)
    def _(c):
        cols = pl.ds(pl.multiple_of(c * 256, 256), 256)
        normed_t[cols, :] = normed[:, cols].astype(f32).T.astype(bf16)

    rs_a.wait()
    att_q[...] = rs_a.value()

    def resid_norm():
        return norm_parts(xp[own_rows, :].astype(f32) + att_q[...])

    xhat2, _r2 = resid_norm()
    norm2[...] = (xhat2 * g2_ref[...] + b2_ref[...]).astype(bf16)
    n_x = exchange(nsend, nrecv, ns)

    def pick_quarter(full):
        cq = (iota((128, 256), 0) >> 2) & 3
        out = full[:, :256]
        for k in (1, 2, 3):
            out = jnp.where(cq == k, full[:, k * 256 : (k + 1) * 256], out)
        return out.astype(bf16)

    for e in range(2):

        @pl.loop(0, 4)
        def _(c):
            chunk = rem4(me // 8 + c)
            row0 = pl.multiple_of(chunk * 128, 128)
            r = iota((128, Q), 0) + row0
            sel = hot((r >> 4) * 8 + e * 4 + (r & 3) == slot_r[...])
            nsend[e, pl.ds(row0, 128), :] = pick_quarter(mm(sel, norm2[...]))
            n_x[e].start_chunk(chunk)

        n_x[e].keep_own()

    cot_x.all.wait_recv()

    i = iota((T, T), 0)
    reorder = hot(((i & 127) >> 2) * 16 + (i >> 7) * 4 + (i & 3) == iota((T, T), 1))
    for e in range(2):

        @pl.loop(0, 4)
        def _(c):
            cols = pl.ds(pl.multiple_of(c * 256, 256), 256)
            gal[e, :, cols] = mm(reorder, crecv[e, :, cols]).astype(bf16)

    ag_x = [Gather(ring_x, xall.at[e], Q, ags.at[e]) for e in range(2)]

    def compact(e):
        n_x[e].all.wait_recv()
        i = iota((Q, T), 0)
        target = (i >> 2) * 16 + (i & 3)
        for cq in range(4):
            sel = hot(iota((Q, T), 1) == target + cq * 4)
            xall[e, own_rows, cq * 256 : (cq + 1) * 256] = mm(sel, nrecv[e]).astype(bf16)

    compact(0)
    ag_x[0].start()
    compact(1)
    ag_x[0].pass_on()
    ag_x[1].start()

    loads["win"].wait()
    loads["wbk"].wait()
    cot_x.all.wait_send()

    def unit(e):
        @pl.loop(0, 2)
        def _(c):
            cols = pl.ds(pl.multiple_of(c * 512, 512), 512)
            act, slope = gelu_parts(mm(xall[e], win[e, :, cols]))
            hid[e, :, cols] = act.astype(bf16)
            dpre[e, :, cols] = (mm_nt(gal[e], wbk[e, cols, :]) * slope).astype(bf16)

    def unit_n2(e):
        @pl.loop(0, 2)
        def _(c):
            cols = pl.ds(pl.multiple_of(c * 512, 512), 512)
            n2p[e, :, cols] = mm_nt(dpre[e], win[e, cols, :]).astype(bf16)

    def unit_out(e):
        @pl.loop(0, 2)
        def _(c):
            cols = pl.ds(pl.multiple_of(c * 512, 512), 512)
            outp[e, :, cols] = mm(hid[e], wbk[e, :, cols]).astype(bf16)

    def scatter(part, bufs, e, at):
        rel, tot, arr = bufs
        return ReduceScatter(
            ring_x, part.at[e], Q, rel.at[e], tot.at[e], arr.at[e], rss.at[at]
        )

    rs_e = [scatter(n2p, (e_rel, e_sum, e_arr), e, 1 + e) for e in range(2)]
    rs_o = [scatter(outp, (o_rel, o_sum, o_arr), e, 3 + e) for e in range(2)]

    ag_x[0].wait_rest()
    unit(0)
    ag_x[1].pass_on()
    unit_n2(0)
    rs_e[0].send_all()
    unit_out(0)
    ag_x[1].wait_rest()
    unit(1)
    rs_e[0].pass_on()
    unit_n2(1)
    rs_e[1].send_all()
    unit_out(1)

    outs = [(xall, x_out), (gal, g_out), (hid, hid_out), (dpre, dpre_out)]
    stores = [pltpu.make_async_copy(a, b, loc.at[6 + i]) for i, (a, b) in enumerate(outs)]
    for copy in stores:
        copy.start()

    def send_back(rs, e, buf, x):
        value = rs.value().astype(bf16)
        for c in range(4):
            chunk = rem4(me // 8 + c)
            row0 = pl.multiple_of(chunk * 128, 128)
            r = iota((128, Q), 0) + row0
            sel = hot((r >> 4) * 4 + (r & 3) == iota((128, Q), 1))
            buf[e, pl.ds(row0, 128), :] = pick_quarter(mm(sel, value))
            x[e].start_chunk(chunk)
        x[e].keep_own()

    def to_tokens(buf, e):
        slots = slot_c[...]
        target = jnp.where(((slots >> 2) & 1) == e, (slots >> 3) * 16 + (slots & 3), -T)
        lanes = iota((Q, T), 1)
        return jnp.concatenate(
            [mm(hot(lanes == target + cq * 4), buf[e]) for cq in range(4)], axis=1
        )

    e_x = exchange(esend, erecv, es)
    o_x = exchange(osend, orecv, os_)

    rs_e[0].wait()
    send_back(rs_e[0], 0, esend, e_x)
    rs_e[1].pass_on()
    rs_o[0].send_all()
    rs_e[1].wait()
    send_back(rs_e[1], 1, esend, e_x)

    sel_own = hot(iota((Q, T), 0) + h * Q == iota((Q, T), 1))
    cot_q = mm(mm(sel_own, pm[...]).astype(bf16), cot_low[...])
    e_x[0].all.wait_recv()
    dn2 = to_tokens(erecv, 0)
    rs_o[0].pass_on()
    e_x[1].all.wait_recv()
    dn2 = dn2 + to_tokens(erecv, 1)
    xhat2, r2 = resid_norm()
    nv[2] = as_tile(jnp.sum(dn2 * xhat2, axis=0, keepdims=True))
    nv[3] = as_tile(jnp.sum(dn2, axis=0, keepdims=True))
    d_resid = cot_q + norm_back(dn2 * g2_ref[...], xhat2, r2)
    dres[...] = d_resid
    datt[own_rows, :] = d_resid.astype(bf16)
    ag_d = Gather(ring_x, datt, Q, ags.at[2])
    ag_d.start()
    ag_d.pass_on()
    rs_o[1].send_all()
    ag_d.wait_rest()

    stores[1].wait()
    dmx[...] = mm_nt(datt[...], wout[...]).astype(bf16)
    dm_t[...] = dmx[...].astype(f32).T.astype(bf16)

    @pl.loop(0, 4)
    def _(c):
        cols = pl.ds(pl.multiple_of(c * 256, 256), 256)
        rows = pl.ds(pl.multiple_of(lax.rem(c, 2) * 256, 256), 256)
        wpart[c // 2, rows, 768:1024] = mm(mixed_t[...], datt[:, cols]).astype(bf16)

    for hp in range(2):
        pair = slice(hp * 128, hp * 128 + 128)

        @pl.loop(0, 4)
        def _(rb):
            rows = pl.ds(pl.multiple_of(rb * Q, Q), Q)
            dqs = []
            for hh in range(2):
                lanes = slice(hp * 128 + hh * 64, hp * 128 + hh * 64 + 64)
                dch = mm_nt(dmx[rows, lanes], qkv[2, :, lanes])
                ch = chs[hp * 2 + hh, rows, :].astype(f32)
                inner = jnp.sum(ch * dch, axis=-1, keepdims=True)
                ds = (ch * (dch - inner)).astype(bf16)
                dss[hh][rows, :] = ds
                dqs.append(mm(ds, qkv[1, :, lanes]) * 0.125)
            dqkv[0, rows, pair] = jnp.concatenate(dqs, axis=1).astype(bf16)

        if hp == 0:
            rs_o[1].pass_on()
            rs_o[0].wait()
            send_back(rs_o[0], 0, osend, o_x)
        dks, dvs = [], []
        for hh in range(2):
            lanes = slice(hp * 128 + hh * 64, hp * 128 + hh * 64 + 64)
            dks.append(mm(q_t[lanes, :], dss[hh][...]) * 0.125)
            dvs.append(mm(dm_t[lanes, :], chs[hp * 2 + hh]))
        dqkv[1, :, pair] = jnp.concatenate(dks, axis=0).T.astype(bf16)
        dqkv[2, :, pair] = jnp.concatenate(dvs, axis=0).T.astype(bf16)

    rs_d = ReduceScatter(ring_x, npart, Q, d_rel, d_sum, d_arr, rss.at[5])

    def input_grad(b):
        rows = pl.ds(pl.multiple_of(b * Q, Q), Q)
        total = mm_nt(dqkv[0, rows, :], wqkv[0])
        for c in (1, 2):
            total += mm_nt(dqkv[c, rows, :], wqkv[c])
        npart[rows, :] = total.astype(bf16)

    input_grad(far)
    for copy in rs_d.far:
        copy.start()
    input_grad(left)
    rs_d.near[0].start()
    input_grad(right)
    rs_d.near[1].start()
    input_grad(h)

    for c in range(3):
        for k in range(2):
            rows = normed_t[k * T : (k + 1) * T, :]
            wpart[k, :, c * 256 : (c + 1) * 256] = mm(rows, dqkv[c]).astype(bf16)

    core_rows = pl.ds(pl.multiple_of(core * T, T), T)
    other_rows = pl.ds(pl.multiple_of((1 - core) * T, T), T)
    swap = remote(wpart.at[1 - core], wx, xs.at[0], xs.at[1], sibling)
    swap.start()
    rs_d.pass_on()
    rs_o[1].wait()
    send_back(rs_o[1], 1, osend, o_x)
    swap.wait_recv()
    ws[...] = (wpart[core].astype(f32) + wx[...].astype(f32)).astype(bf16)
    ws0, ws1 = ws.at[pl.ds(0, 256), :], ws.at[pl.ds(256, 256), :]

    def reduce(ring, part, rows, rel, tot, arr, at):
        return ReduceScatter(ring, part, rows, rel, tot, arr, rss.at[at])

    rs_w0 = reduce(ring_y, ws0, 64, w0_rel, w0_sum, w0_arr, 6)
    rs_w1 = reduce(ring_z, ws1, 64, w1_rel, w1_sum, w1_arr, 7)
    rs_w2 = reduce(ring_z, w0, 16, w2_rel, w2_sum, w2_arr, 8)
    rs_w3 = reduce(ring_y, w1, 16, w3_rel, w3_sum, w3_arr, 9)
    rs_w0.send_all()
    rs_w1.send_all()

    rs_d.wait()
    dn1 = rs_d.value()
    xhat1, r1 = norm_parts(xp[own_rows, :].astype(f32))
    gtall[own_rows, :] = (dres[...] + norm_back(dn1 * g1_ref[...], xhat1, r1)).astype(bf16)
    ag_g = Gather(ring_x, gtall, Q, ags.at[3])
    ag_g.start()
    nv[0] = as_tile(jnp.sum(dn1 * xhat1, axis=0, keepdims=True))
    nv[1] = as_tile(jnp.sum(dn1, axis=0, keepdims=True))

    def to_x(src, dst, mine, at):
        copies = [
            remote(src(rem4(h + k)), dst.at[mine], vs.at[at], vs.at[at + 1], {"head": rem4(h + k)})
            for k in (1, 2, 3)
        ]
        three = dst.at[pl.ds(0, 3)]
        for copy in copies:
            copy.start()
        return remote(three, three, vs.at[at], vs.at[at + 1], {"head": rem4(h + 1)})

    nx = to_x(lambda k: nv.at[k], nrx, h, 0)

    rs_w0.pass_on()
    rs_w1.pass_on()
    rs_w0.wait()
    w0[...] = rs_w0.value().astype(bf16)
    rs_w2.send_all()
    rs_w1.wait()
    w1[...] = rs_w1.value().astype(bf16)
    rs_w3.send_all()

    for e in range(2):
        o_x[e].all.wait_recv()
    outall[own_rows, :] = (att_q[...] + to_tokens(orecv, 0) + to_tokens(orecv, 1)).astype(bf16)
    ag_o = Gather(ring_x, outall, Q, ags.at[4])
    ag_g.pass_on()
    ag_o.start()
    rs_w2.pass_on()
    rs_w3.pass_on()

    nx.wait_recv()
    nye[me] = nv[h] + nrx[rem4(h + 1)] + nrx[rem4(h + 2)] + nrx[rem4(h + 3)]

    def n_all(d):
        return remote(nye.at[me], nye.at[me], vs.at[2], vs.at[3], {"expert": d})

    n_rows = nye.at[pl.ds(0, G - 1)]
    n_every = remote(n_rows, n_rows, vs.at[2], vs.at[3], {"expert": lax.rem(me + 1, G)})

    base = core * T
    row_y = pl.multiple_of(base + y * 64, 64)
    row_z = pl.multiple_of(base + 256 + z * 64, 64)

    def spread(ring, row0, rows, at):
        view = w_out.at[pl.ds(pl.multiple_of(row0, rows), 4 * rows), :]
        return Gather(ring, view, rows, ags.at[at])

    ag_w2 = spread(ring_z, row_y, 16, 5)
    ag_w3 = spread(ring_y, row_z, 16, 6)
    ag_w0 = spread(ring_y, base, 64, 7)
    ag_w1 = spread(ring_z, base + 256, 64, 8)
    rs_w2.wait()
    w_out[pl.ds(pl.multiple_of(row_y + z * 16, 16), 16), :] = rs_w2.value().astype(bf16)
    ag_w2.start()
    rs_w3.wait()
    w_out[pl.ds(pl.multiple_of(row_z + y * 16, 16), 16), :] = rs_w3.value().astype(bf16)
    ag_w3.start()
    others(lambda d: n_all(d).start())
    ag_w2.finish()
    ag_w0.start()
    ag_w3.finish()
    ag_w1.start()

    def restore(dst, src):
        @pl.loop(0, 4)
        def _(c):
            cols = pl.ds(pl.multiple_of(c * 256, 256), 256)
            dst[:, cols] = mm(pmt[...], src[:, cols]).astype(bf16)

    ag_o.pass_on()
    ag_w0.pass_on()
    ag_w1.pass_on()
    ag_g.wait_rest()
    restore(xp, gtall)
    gt_store = pltpu.make_async_copy(xp, gt_out, loc.at[10])
    gt_store.start()

    n_every.wait_recv()
    nrm_out[h] = jnp.sum(nye[...], axis=0)
    nf = to_x(lambda k: nrm_out.at[h], nrm_out, h, 4)

    ag_w0.wait_rest()
    ag_w1.wait_rest()
    both = remote(w_out.at[core_rows, :], w_out.at[core_rows, :], xs.at[2], xs.at[3], sibling)
    both_in = remote(w_out.at[core_rows, :], w_out.at[other_rows, :], xs.at[2], xs.at[3], sibling)
    both.start()
    ag_o.wait_rest()
    restore(normed, outall)
    u_store = pltpu.make_async_copy(normed, u_out, loc.at[11])
    u_store.start()
    both_in.wait_recv()
    nf.wait_recv()

    for x in n_x + e_x + o_x:
        x.all.wait_send()
    n_every.wait_send()
    for group in (rs_a, *rs_e, *rs_o, rs_d, rs_w0, rs_w1, rs_w2, rs_w3,
                  *ag_x, ag_d, ag_o, ag_g, ag_w0, ag_w1, ag_w2, ag_w3):
        group.wait_sent()
    swap.wait_send()
    both.wait_send()
    nx.wait_send()
    nf.wait_send()
    for copy in [stores[0], *stores[2:], gt_store, u_store]:
        copy.wait()


def layer(seg, route, g1, b1, g2, b2, tok, wqkv, wout, win, wbk, cot):
    vmem = pl.BlockSpec(memory_space=pltpu.VMEM)
    hbm = pl.BlockSpec(memory_space=pl.ANY)
    V = pltpu.VMEM
    DMA = pltpu.SemaphoreType.DMA

    def rs_bufs(rows, cols):
        return [V((2, rows, cols), bf16), V((2, rows, cols), bf16), V((2, 2, rows, cols), bf16)]

    pair_bufs = [V((2, *buf.shape), bf16) for buf in rs_bufs(Q, HALF)]
    scratch = [
        V((T, D), bf16), V((3, D, 256), bf16), V((256, D), bf16), V((2, D, D), bf16),
        V((2, D, D), bf16), V((T, D), f32), V((T, D), bf16),
        V((T, T), bf16), V((T, T), bf16), V((T, 1), i32), V((1, T), i32), V((Q, 1), i32),
        V((1, Q), i32),
        V((2, T, D), bf16), V((2, T, D), bf16), V((2, T, D), bf16),
        V((T, D), bf16), V((T, D), bf16), V((D, T), bf16), V((3, T, 256), bf16),
        V((256, T), bf16), V((4, T, T), bf16), V((T, 256), bf16), V((256, T), bf16),
        V((T, D), bf16), *rs_bufs(Q, HALF),
        V((Q, D), bf16), V((2, T, 256), bf16), V((2, T, 256), bf16), *[V((2, T, D), bf16)] * 4,
        *pair_bufs, V((2, T, 256), bf16), V((2, T, 256), bf16),
        *pair_bufs, V((2, T, 256), bf16), V((2, T, 256), bf16), V((T, D), bf16),
        V((T, D), bf16), V((T, 256), bf16), V((256, T), bf16), V((3, T, 256), bf16),
        *rs_bufs(Q, HALF), V((T, D), bf16),
        V((T, D), bf16),
        V((64, D), bf16), *rs_bufs(64, HALF), V((64, D), bf16), *rs_bufs(64, HALF),
        *rs_bufs(16, HALF), *rs_bufs(16, HALF),
        V((4, 8, 128), f32), V((4, 8, 128), f32), V((G, 8, 128), f32),
        DMA((12,)), DMA((2,)), *[DMA((2, 2))] * 3, DMA((10, 4)), DMA((9, 4)), DMA((4,)), DMA((6,)),
    ]
    S = jax.ShapeDtypeStruct
    quarters = S((2, T, D), bf16)
    return pl.pallas_call(
        layer_kernel,
        name="layer",
        out_shape=[quarters] * 4
        + [S((T, D), bf16), S((T, D), bf16), S((D, D), bf16), S((4, 8, 128), f32)],
        in_specs=[vmem] * 6 + [hbm] * 6,
        out_specs=[hbm] * 6 + [vmem] * 2,
        scratch_shapes=scratch,
        compiler_params=pltpu.CompilerParams(
            collective_id=0, has_side_effects=True, vmem_limit_bytes=62 << 20
        ),
        cost_estimate=pl.CostEstimate(
            flops=24 * 10**9, bytes_accessed=30 * 2**20, transcendentals=4 * 10**6
        ),
    )(seg, route, g1, b1, g2, b2, tok, wqkv, wout, win, wbk, cot)


def finish_kernel(
    x_ref, dpre_ref, hid_ref, g_ref, w_ref, u_ref, gt_ref, tok_ref,
    win_out, wback_out, wqkv_out, wout_out, out_out, gt_out,
):
    def outer(lhs, rhs, out):
        out[0] = lax.dot_general(
            lhs[0], rhs[0], (((0,), (0,)), ((), ())), preferred_element_type=f32
        )

    outer(x_ref, dpre_ref, win_out)
    outer(hid_ref, g_ref, wback_out)
    for c in range(3):
        wqkv_out[c] = w_ref[:, c * 256 : (c + 1) * 256].astype(f32)
    wout_out[...] = w_ref[:, 768:].astype(f32)
    out_out[...] = tok_ref[...].astype(f32) + u_ref[...].astype(f32)
    gt_out[...] = gt_ref[...].astype(f32)


def finish(x, dpre, hid, g, w, u, gt, tokens):
    lhs = pl.BlockSpec((1, T, 256), lambda e, c: (e, 0, c))
    rhs = pl.BlockSpec((1, T, D), lambda e, c: (e, 0, 0))
    out = pl.BlockSpec((1, 256, D), lambda e, c: (e, c, 0))
    rows = pl.BlockSpec((64, D), lambda e, c: (e * 4 + c, 0))
    S = jax.ShapeDtypeStruct
    return pl.pallas_call(
        finish_kernel,
        name="finish",
        grid=(2, 4),
        out_shape=[
            S((2, D, D), f32), S((2, D, D), f32), S((3, D, 256), f32), S((256, D), f32),
            S((T, D), f32), S((T, D), f32),
        ],
        in_specs=[lhs, rhs, lhs, rhs, pl.BlockSpec((128, D), lambda e, c: (e * 4 + c, 0)),
                  rows, rows, rows],
        out_specs=[
            out, out,
            pl.BlockSpec((3, 128, 256), lambda e, c: (0, e * 4 + c, 0)),
            pl.BlockSpec((128, 256), lambda e, c: (c % 2, e * 2 + c // 2)),
            rows, rows,
        ],
        compiler_params=pltpu.CompilerParams(vmem_limit_bytes=60 << 20),
        cost_estimate=pl.CostEstimate(
            flops=8 * 2**30, bytes_accessed=37 * 2**20, transcendentals=0
        ),
    )(x, dpre, hid, g, w, u, gt, tokens)


def per_device(
    tokens, segment_ids, expert_of, norm1_gain, norm1_bias, norm2_gain, norm2_bias,
    w_qkv, w_out, w_in, w_back, cotangent,
):
    row = lambda v: v.reshape(1, D)
    x, g, hid, dpre, u, gt, w, nrm = layer(
        segment_ids, expert_of.reshape(1, T), row(norm1_gain), row(norm1_bias), row(norm2_gain), row(norm2_bias),
        tokens, w_qkv, w_out, w_in, w_back, cotangent,
    )
    grad_w_in, grad_w_back, grad_w_qkv, grad_w_out, output, grad_tokens = finish(
        x, dpre, hid, g, w, u, gt, tokens
    )
    vectors = nrm.reshape(4, D)
    return (
        output, grad_tokens, vectors[0], vectors[1], vectors[2], vectors[3],
        grad_w_qkv, grad_w_out, grad_w_in, grad_w_back,
    )


def solution(mesh):
    return jax.shard_map(
        per_device,
        mesh=mesh,
        in_specs=(
            P("expert", None),
            P("expert", None),
            P("expert", None),
            P(),
            P(),
            P(),
            P(),
            P(None, None, "head"),
            P("head", None),
            P("expert", None, "head"),
            P("expert", "head", None),
            P("expert", None),
        ),
        out_specs=(
            P("expert", None),
            P("expert", None),
            P(),
            P(),
            P(),
            P(),
            P(None, None, "head"),
            P("head", None),
            P("expert", None, "head"),
            P("expert", "head", None),
        ),
        check_vma=False,
    )
```

```python
import functools

import jax
import jax.numpy as jnp
from jax import lax
from jax.experimental import pallas as pl
from jax.experimental.pallas import tpu as pltpu
from jax.sharding import PartitionSpec as P

f32 = jnp.float32
bf16 = jnp.bfloat16
i32 = jnp.int32
MESH = pl.DeviceIdType.MESH

T = 512
D = 1024
G = 32
H = 4
Q = T // H
HALF = D // 2
EPS = 1e-5


def mm(a, b):
    return lax.dot_general(a, b, (((1,), (0,)), ((), ())), preferred_element_type=f32)


def mm_nt(a, b):
    return lax.dot_general(a, b, (((1,), (1,)), ((), ())), preferred_element_type=f32)


def iota(shape, dim):
    return lax.broadcasted_iota(i32, shape, dim)


def hot(cond):
    return jnp.where(cond, 1.0, 0.0).astype(bf16)


def rem4(v):
    return lax.rem(v, 4)


def remote(src, dst, send_sem, recv_sem, device):
    return pltpu.make_async_remote_copy(
        src_ref=src,
        dst_ref=dst,
        send_sem=send_sem,
        recv_sem=recv_sem,
        device_id=device,
        device_id_type=MESH,
    )


def columns(ref, rows):
    half = ref.shape[1] // 2
    return lambda b, hf: ref.at[pl.ds(pl.multiple_of(b * rows, rows), rows), pl.ds(hf * half, half)]


class ReduceScatter:
    def __init__(self, ring, whole, rows, relay, total, arrived, sems):
        self.me, right, left = ring
        self.right, self.left = rem4(self.me + 1), rem4(self.me + 3)
        far = rem4(self.me + 2)
        self.part = part = columns(whole, rows)
        self.relay, self.total, self.arrived = relay, total, arrived
        self.three, self.two = whole.at[pl.ds(0, 3 * rows), :], whole.at[pl.ds(0, 2 * rows), :]
        self.sems, self.left_device = sems, left
        send, rest = sems.at[0], sems.at[3]
        self.far = [
            remote(part(far, 0), relay.at[0], send, sems.at[1], left),
            remote(part(far, 1), relay.at[1], send, sems.at[2], right),
        ]
        self.near = [
            remote(part(self.left, 1), arrived.at[1, 1], send, rest, left),
            remote(part(self.right, 0), arrived.at[0, 0], send, rest, right),
        ]
        self.last = [
            remote(total.at[0], arrived.at[1, 0], send, rest, left),
            remote(total.at[1], arrived.at[0, 1], send, rest, right),
        ]

    def send_all(self):
        for copy in self.far + self.near:
            copy.start()

    def pass_on(self):
        for hf, owner in ((0, self.left), (1, self.right)):
            self.far[hf].wait_recv()
            mine = self.part(owner, hf)[...].astype(f32)
            self.total[hf] = (mine + self.relay[hf].astype(f32)).astype(bf16)
            self.last[hf].start()

    def wait(self):
        all_of(self.two, self.sems.at[0], self.sems.at[3], self.left_device).wait_recv()

    def value(self):
        def half(hf):
            mine = self.part(self.me, hf)[...].astype(f32)
            return mine + self.arrived[0, hf].astype(f32) + self.arrived[1, hf].astype(f32)

        return jnp.concatenate([half(0), half(1)], axis=1)

    def wait_sent(self):
        all_of(self.three, self.sems.at[0], self.sems.at[3], self.left_device).wait_send()


class Gather:
    def __init__(self, ring, whole, rows, sems):
        me, right, left = ring
        on_right, on_left = rem4(me + 1), rem4(me + 3)
        block = columns(whole, rows)
        self.three, self.two = whole.at[pl.ds(0, 3 * rows), :], whole.at[pl.ds(0, 2 * rows), :]
        self.sems, self.left_device = sems, left

        def copy(b, hf, i, device):
            return remote(block(b, hf), block(b, hf), sems.at[0], sems.at[i], device)

        self.first = [copy(me, 0, 1, right), copy(me, 1, 2, left)]
        self.second = [copy(me, 0, 3, left), copy(me, 1, 3, right)]
        self.third = [copy(on_left, 0, 3, right), copy(on_right, 1, 3, left)]

    def start(self):
        for copy in self.first + self.second:
            copy.start()

    def pass_on(self):
        for hf in range(2):
            self.first[hf].wait_recv()
            self.third[hf].start()

    def wait_rest(self):
        all_of(self.two, self.sems.at[0], self.sems.at[3], self.left_device).wait_recv()

    def finish(self):
        self.pass_on()
        self.wait_rest()

    def wait_sent(self):
        all_of(self.three, self.sems.at[0], self.sems.at[3], self.left_device).wait_send()


class Exchange:
    def __init__(self, me, src, dst, sems):
        self.me, self.src, self.dst, self.sems = me, src, dst, sems
        rows = pl.ds(0, 16 * (G - 1))
        index = (slice(None),) * (len(src.shape) - 2) + (rows, slice(None))
        other = {"expert": lax.rem(me + 1, G)}
        self.all = remote(src.at[index], dst.at[index], sems.at[0], sems.at[1], other)

    def block(self, ref, d):
        rows = pl.ds(pl.multiple_of(d * 16, 16), 16)
        return ref.at[(slice(None),) * (len(ref.shape) - 2) + (rows, slice(None))]

    def start_chunk(self, chunk):
        @pl.loop(0, 8)
        def _(k):
            d = chunk * 8 + lax.rem(self.me + k, 8)

            @pl.when(d != self.me)
            def _():
                remote(
                    self.block(self.src, d), self.block(self.dst, self.me),
                    self.sems.at[0], self.sems.at[1], {"expert": d},
                ).start()

    def keep_own(self):
        self.block(self.dst, self.me)[...] = self.block(self.src, self.me)[...]


def all_of(view, send_sem, recv_sem, device):
    return remote(view, view, send_sem, recv_sem, device)


def norm_parts(x):
    center = x - jnp.mean(x, axis=-1, keepdims=True)
    r = lax.rsqrt(jnp.mean(center * center, axis=-1, keepdims=True) + EPS)
    return center * r, r


def norm_back(g, xhat, r):
    return r * (
        g - jnp.mean(g, axis=-1, keepdims=True) - xhat * jnp.mean(g * xhat, axis=-1, keepdims=True)
    )


def gelu_parts(v):
    c = 0.7978845608028654
    v2 = v * v
    t = jnp.tanh(c * v * (1.0 + 0.044715 * v2))
    half = 0.5 * (1.0 + t)
    grad = half + 0.5 * v * (1.0 - t * t) * c * (1.0 + 3.0 * 0.044715 * v2)
    return v * half, grad


def as_tile(row):
    return jnp.concatenate([row[:, i * 128 : (i + 1) * 128] for i in range(8)], axis=0)


def layer_kernel(
    seg_ref, route_ref, g1_ref, b1_ref, g2_ref, b2_ref,
    tok_hbm, wqkv_hbm, wout_hbm, win_hbm, wbk_hbm, cot_hbm,
    x_out, g_out, hid_out, dpre_out, u_out, gt_out, pmt_out, w_out, nrm_out,
    tok, wqkv, wout, win, wbk, cotw, cot_low,
    pm, pmt, code_c, code_r, slot_c, slot_r,
    csend, crecv, gal,
    xp, normed, normed_t, qkv, k_t, chs, mixed, mixed_t,
    apart, a_rel, a_sum, a_arr,
    norm2, nsend, nrecv, xall, hid, dpre, n2p,
    e_rel, e_sum, e_arr, esend, erecv,
    o_rel, o_sum, o_arr, osend, orecv, outall,
    datt, dmx, v_t, dqkv,
    d_rel, d_sum, d_arr, gtall,
    wx, wfin,
    w0, w0_rel, w0_sum, w0_arr, w1, w1_rel, w1_sum, w1_arr,
    w2_rel, w2_sum, w2_arr, w3_rel, w3_sum, w3_arr,
    nv, nrx, nye,
    loc, cs, ns, es, os_, rss, ags, xs, vs,
):
    me = lax.axis_index("expert")
    h = lax.axis_index("head")
    core = lax.rem(me, 2)
    chip = me // 2
    y = lax.rem(chip, 4)
    z = chip // 4

    def at_yz(yy, zz, cc):
        return {"expert": (rem4(zz) * 4 + rem4(yy)) * 2 + cc}

    ring_x = (h, {"head": rem4(h + 1)}, {"head": rem4(h + 3)})
    ring_y = (y, at_yz(y + 1, z, core), at_yz(y + 3, z, core))
    ring_z = (z, at_yz(y, z + 1, core), at_yz(y, z + 3, core))
    sibling = {"expert": chip * 2 + 1 - core}
    left, right, far = rem4(h + 3), rem4(h + 1), rem4(h + 2)

    att_q, dres, cot_q = (cotw.at[pl.ds(k * Q, Q), :] for k in range(3))
    npart = tok
    ws = cot_low
    wpart = gal
    dss = [buf.at[:, pl.ds(k * T, T)] for buf in (tok, apart) for k in range(2)]
    outp = csend

    loads = {}
    for i, (name, src, dst) in enumerate(
        (
            ("cot", cot_hbm, cotw),
            ("tok", tok_hbm, tok),
            ("wqkv", wqkv_hbm, wqkv),
            ("wout", wout_hbm, wout),
            ("win", win_hbm, win),
            ("wbk", wbk_hbm, wbk),
        )
    ):
        loads[name] = pltpu.make_async_copy(src, dst, loc.at[i])
        loads[name].start()

    barrier = pltpu.get_barrier_semaphore()

    @pl.loop(1, G)
    def _(k):
        pl.semaphore_signal(
            barrier, inc=1, device_id={"expert": lax.rem(me + k, G)}, device_id_type=MESH
        )

    for k in range(1, H):
        pl.semaphore_signal(barrier, inc=1, device_id={"head": rem4(h + k)}, device_id_type=MESH)

    eye = iota((T, T), 0) == iota((T, T), 1)
    route_row = route_ref[...].astype(f32)
    route_c = jnp.sum(jnp.where(eye, route_row, 0.0), axis=1, keepdims=True).astype(i32)

    def to_row(col):
        return jnp.sum(jnp.where(eye, col.astype(f32), 0.0), axis=0, keepdims=True)

    onehot = jnp.where(iota((T, 128), 1) == route_c, 1.0, 0.0)
    before = hot(iota((T, T), 1) < iota((T, T), 0))
    rank = jnp.sum(mm(before, onehot.astype(bf16)) * onehot, axis=1, keepdims=True)
    count = jnp.broadcast_to(jnp.sum(onehot, axis=0, keepdims=True), (8, 128)).astype(bf16)
    first = mm(count, hot(iota((128, 128), 0) < iota((128, 128), 1)))[0:1]
    place = (jnp.sum(onehot * first, axis=1, keepdims=True) + rank).astype(i32)
    rank4 = rank.astype(i32) >> 2
    quarter = place & 3
    pos_c = quarter * Q + (place >> 2)
    slot4 = route_c * 4 + rank4
    key = (route_c & 1) * T + (route_c >> 1) * 16 + quarter * 4 + rank4
    pos_r = to_row(pos_c).astype(i32)
    key_r = to_row(key).astype(i32)
    perm = iota((T, T), 0) == pos_r
    perm_t = iota((T, T), 1) == pos_c
    pm[...] = hot(perm)
    pmt[...] = hot(perm_t)
    code = (seg_ref[...] * 1024 + iota((1, T), 1)).astype(f32)
    code_pc = jnp.sum(jnp.where(perm, code, 0.0), axis=1, keepdims=True)
    code_c[...] = code_pc.astype(i32)
    code_r[...] = to_row(code_pc).astype(i32)
    own_t = iota((T, Q), 1) + h * Q == pos_c
    slot_row = jnp.sum(jnp.where(own_t, slot4.astype(f32), 0.0), axis=0, keepdims=True)
    slot_r[...] = slot_row.astype(i32)
    eye_q = iota((Q, Q), 0) == iota((Q, Q), 1)
    slot_c[...] = jnp.sum(jnp.where(eye_q, slot_row, 0.0), axis=1, keepdims=True).astype(i32)

    pl.semaphore_wait(barrier, G - 1 + H - 1)

    loads["cot"].wait()
    cot_low[...] = cotw[...].astype(bf16)

    def others(act):
        @pl.loop(1, G)
        def _(k):
            act(lax.rem(me + k, G))

    def exchange(src, dst, sems):
        return [Exchange(me, src.at[e], dst.at[e], sems.at[e]) for e in range(2)]

    cot_x = exchange(csend, crecv, cs)

    def send_cot(e):
        @pl.loop(0, 4)
        def _(c):
            cot_x[e].start_chunk(rem4(me // 8 + c))

        cot_x[e].keep_own()

    @pl.loop(0, 4)
    def _(c):
        chunk = rem4(me // 8 + c)
        row0 = pl.multiple_of(chunk * 128, 128)
        r = iota((256, T), 0)
        sel = hot(row0 + (r & 127) + (r >> 7) * T == key_r)
        rows = mm(sel, cot_low[...]).astype(bf16)
        for e in range(2):
            csend[e, pl.ds(row0, 128), :] = rows[e * 128 : e * 128 + 128]
        cot_x[0].start_chunk(chunk)

    cot_x[0].keep_own()

    loads["tok"].wait()

    @pl.loop(0, 4)
    def _(rb):
        rows = pl.ds(pl.multiple_of(rb * Q, Q), Q)
        x = mm(pm[rows, :], tok[...])
        xp[rows, :] = x.astype(bf16)
        xhat, _r = norm_parts(x)
        normed[rows, :] = (xhat * g1_ref[...] + b1_ref[...]).astype(bf16)

    loads["wqkv"].wait()

    @pl.loop(0, 3)
    def _(c):
        qkv[c] = (mm(normed[...], wqkv[c]) * jnp.where(c == 0, 0.125, 1.0)).astype(bf16)

    v_t[...] = qkv[2].astype(f32).T.astype(bf16)

    def head(hd):
        return slice(hd * 64, hd * 64 + 64)

    @pl.loop(0, 4)
    def _(rb):
        rows = pl.ds(pl.multiple_of(rb * Q, Q), Q)
        keys, queries = code_c[...], code_r[:, rows]
        allowed = (keys <= queries) & (keys >= ((queries >> 10) << 10))
        bias = jnp.where(allowed, 0.0, -1e30)
        outs = []
        for hd in range(4):
            s = mm_nt(qkv[1, :, head(hd)], qkv[0, rows, head(hd)]) + bias
            e = jnp.exp(s - jnp.max(s, axis=0, keepdims=True))
            ch = (e * (1.0 / jnp.sum(e, axis=0, keepdims=True))).astype(bf16)
            chs[hd, :, rows] = ch
            outs.append(mm(v_t[head(hd), :], ch))
        heads = jnp.concatenate(outs, axis=0)
        mixed_t[:, rows] = heads.astype(bf16)
        mixed[rows, :] = heads.T.astype(bf16)

    loads["wout"].wait()
    rs_a = ReduceScatter(ring_x, apart, Q, a_rel, a_sum, a_arr, rss.at[0])

    def project(b):
        rows = pl.ds(pl.multiple_of(b * Q, Q), Q)
        apart[rows, :] = mm(mixed[rows, :], wout[...]).astype(bf16)

    project(far)
    for copy in rs_a.far:
        copy.start()
    project(left)
    rs_a.near[0].start()
    project(right)
    rs_a.near[1].start()
    project(h)
    own_rows = pl.ds(pl.multiple_of(h * Q, Q), Q)

    rs_a.pass_on()
    k_t[...] = qkv[1].astype(f32).T.astype(bf16)

    @pl.loop(0, 4)
    def _(c):
        cols = pl.ds(pl.multiple_of(c * 256, 256), 256)
        normed_t[cols, :] = normed[:, cols].astype(f32).T.astype(bf16)

    rs_a.wait()
    att_q[...] = rs_a.value()

    def resid_norm():
        return norm_parts(xp[own_rows, :].astype(f32) + att_q[...])

    xhat2, _r2 = resid_norm()
    norm2[...] = (xhat2 * g2_ref[...] + b2_ref[...]).astype(bf16)
    n_x = exchange(nsend, nrecv, ns)

    def pick_quarter(full):
        cq = (iota((128, 256), 0) >> 2) & 3
        out = full[:, :256]
        for k in (1, 2, 3):
            out = jnp.where(cq == k, full[:, k * 256 : (k + 1) * 256], out)
        return out.astype(bf16)

    for e in range(2):

        @pl.loop(0, 4)
        def _(c):
            chunk = rem4(me // 8 + c)
            row0 = pl.multiple_of(chunk * 128, 128)
            r = iota((128, Q), 0) + row0
            sel = hot((r >> 4) * 8 + e * 4 + (r & 3) == slot_r[...])
            nsend[e, pl.ds(row0, 128), :] = pick_quarter(mm(sel, norm2[...]))
            n_x[e].start_chunk(chunk)

        n_x[e].keep_own()

    sel_own = hot(iota((Q, T), 0) + h * Q == iota((Q, T), 1))
    cot_q[...] = mm(mm(sel_own, pm[...]).astype(bf16), cot_low[...])
    i = iota((T, T), 0)
    pm[...] = hot(((i & 127) >> 2) * 16 + (i >> 7) * 4 + (i & 3) == iota((T, T), 1))

    def regroup(e):
        cot_x[e].all.wait_recv()

        @pl.loop(0, 4)
        def _(c):
            cols = pl.ds(pl.multiple_of(c * 256, 256), 256)
            gal[e, :, cols] = mm(pm[...], crecv[e, :, cols]).astype(bf16)

    regroup(0)
    ag_x = [Gather(ring_x, xall.at[e], Q, ags.at[e]) for e in range(2)]

    def compact(e):
        n_x[e].all.wait_recv()
        i = iota((Q, T), 0)
        target = (i >> 2) * 16 + (i & 3)
        for cq in range(4):
            sel = hot(iota((Q, T), 1) == target + cq * 4)
            xall[e, own_rows, cq * 256 : (cq + 1) * 256] = mm(sel, nrecv[e]).astype(bf16)

    compact(0)
    ag_x[0].start()
    compact(1)
    send_cot(1)
    ag_x[0].pass_on()
    ag_x[1].start()

    loads["win"].wait()
    loads["wbk"].wait()

    def unit(e):
        @pl.loop(0, 2)
        def _(c):
            cols = pl.ds(pl.multiple_of(c * 512, 512), 512)
            act, slope = gelu_parts(mm(xall[e], win[e, :, cols]))
            hid[e, :, cols] = act.astype(bf16)
            dpre[e, :, cols] = (mm_nt(gal[e], wbk[e, cols, :]) * slope).astype(bf16)

    def unit_n2(e):
        @pl.loop(0, 2)
        def _(c):
            cols = pl.ds(pl.multiple_of(c * 512, 512), 512)
            n2p[e, :, cols] = mm_nt(dpre[e], win[e, cols, :]).astype(bf16)

    def unit_out(e):
        @pl.loop(0, 2)
        def _(c):
            cols = pl.ds(pl.multiple_of(c * 512, 512), 512)
            outp[e, :, cols] = mm(hid[e], wbk[e, :, cols]).astype(bf16)

    def scatter(part, bufs, e, at):
        rel, tot, arr = bufs
        return ReduceScatter(
            ring_x, part.at[e], Q, rel.at[e], tot.at[e], arr.at[e], rss.at[at]
        )

    rs_e = [scatter(n2p, (e_rel, e_sum, e_arr), e, 1 + e) for e in range(2)]
    rs_o = [scatter(outp, (o_rel, o_sum, o_arr), e, 3 + e) for e in range(2)]

    ag_x[0].wait_rest()
    unit(0)
    ag_x[1].pass_on()
    unit_n2(0)
    rs_e[0].send_all()
    for x in cot_x:
        x.all.wait_send()
    unit_out(0)
    regroup(1)
    ag_x[1].wait_rest()
    unit(1)
    rs_e[0].pass_on()
    unit_n2(1)
    rs_e[1].send_all()
    unit_out(1)

    outs = [(xall, x_out), (gal, g_out), (hid, hid_out), (dpre, dpre_out), (pmt, pmt_out)]
    stores = [pltpu.make_async_copy(a, b, loc.at[6 + i]) for i, (a, b) in enumerate(outs)]
    for copy in stores:
        copy.start()

    def send_back(rs, e, buf, x):
        value = rs.value().astype(bf16)
        for c in range(4):
            chunk = rem4(me // 8 + c)
            row0 = pl.multiple_of(chunk * 128, 128)
            r = iota((128, Q), 0) + row0
            sel = hot((r >> 4) * 4 + (r & 3) == iota((128, Q), 1))
            buf[e, pl.ds(row0, 128), :] = pick_quarter(mm(sel, value))
            x[e].start_chunk(chunk)
        x[e].keep_own()

    def to_tokens(buf, e):
        slots = slot_c[...]
        target = jnp.where(((slots >> 2) & 1) == e, (slots >> 3) * 16 + (slots & 3), -T)
        lanes = iota((Q, T), 1)
        return jnp.concatenate(
            [mm(hot(lanes == target + cq * 4), buf[e]) for cq in range(4)], axis=1
        )

    e_x = exchange(esend, erecv, es)
    o_x = exchange(osend, orecv, os_)

    rs_e[0].wait()
    send_back(rs_e[0], 0, esend, e_x)
    rs_e[1].pass_on()
    rs_o[0].send_all()
    rs_e[1].wait()
    send_back(rs_e[1], 1, esend, e_x)

    e_x[0].all.wait_recv()
    dn2 = to_tokens(erecv, 0)
    rs_o[0].pass_on()
    e_x[1].all.wait_recv()
    dn2 = dn2 + to_tokens(erecv, 1)
    xhat2, r2 = resid_norm()
    nv[2] = as_tile(jnp.sum(dn2 * xhat2, axis=0, keepdims=True))
    nv[3] = as_tile(jnp.sum(dn2, axis=0, keepdims=True))
    d_resid = cot_q[...] + norm_back(dn2 * g2_ref[...], xhat2, r2)
    dres[...] = d_resid
    datt[own_rows, :] = d_resid.astype(bf16)
    ag_d = Gather(ring_x, datt, Q, ags.at[2])
    ag_d.start()
    ag_d.pass_on()
    rs_o[1].send_all()
    ag_d.wait_rest()

    stores[1].wait()
    dmx[...] = mm_nt(datt[...], wout[...]).astype(bf16)
    for hp in range(2):
        pair = slice(hp * 128, hp * 128 + 128)
        dvs = [mm(chs[hd], dmx[:, head(hd)]) for hd in (2 * hp, 2 * hp + 1)]
        dqkv[2, :, pair] = jnp.concatenate(dvs, axis=1).astype(bf16)

    def weight_part(c, lanes):
        for k in range(2):
            rows = normed_t[k * T : (k + 1) * T, :]
            wpart[k, :, lanes] = mm(rows, dqkv[c]).astype(bf16)

    for k in range(4):
        block = mm(mixed_t[...], datt[:, k * 256 : (k + 1) * 256]).astype(bf16)
        wpart[k // 2, (k % 2) * 256 : (k % 2) * 256 + 256, 0:256] = block
    weight_part(2, slice(256, 512))

    class WeightSum:
        def __init__(self, k):
            cols, thin = pl.ds(k * T, T), pl.ds(k * 256, 256)
            both = pl.ds(0, 2)
            core_rows = pl.ds(pl.multiple_of(core * T, T), T)
            other_rows = pl.ds(pl.multiple_of((1 - core) * T, T), T)
            base = core * T
            self.mine, self.got, self.ws = wpart.at[core, :, cols], wx.at[:, cols], ws.at[:, cols]
            self.w0, self.w1 = w0.at[:, cols], w1.at[:, cols]
            sem = xs.at[k]
            self.swap = remote(
                wpart.at[1 - core, :, cols], self.got, sem.at[0], sem.at[1], sibling
            )

            def scatter(ring, part, rows, bufs, at):
                rel, tot, arr = bufs
                return ReduceScatter(
                    ring, part, rows, rel.at[both, :, thin], tot.at[both, :, thin],
                    arr.at[both, both, :, thin], rss.at[6 + 4 * k + at],
                )

            def spread(ring, row0, rows, at):
                view = wfin.at[pl.ds(pl.multiple_of(row0, rows), 4 * rows), cols]
                return Gather(ring, view, rows, ags.at[5 + 4 * k + at])

            self.rs0 = scatter(ring_y, ws.at[pl.ds(0, 256), cols], 64, (w0_rel, w0_sum, w0_arr), 0)
            self.rs1 = scatter(ring_z, ws.at[pl.ds(256, 256), cols], 64, (w1_rel, w1_sum, w1_arr), 1)
            self.rs2 = scatter(ring_z, self.w0, 16, (w2_rel, w2_sum, w2_arr), 2)
            self.rs3 = scatter(ring_y, self.w1, 16, (w3_rel, w3_sum, w3_arr), 3)
            row_y, row_z = base + y * 64, base + 256 + z * 64
            self.last = [
                wfin.at[pl.ds(pl.multiple_of(row_y + z * 16, 16), 16), cols],
                wfin.at[pl.ds(pl.multiple_of(row_z + y * 16, 16), 16), cols],
            ]
            self.ag0, self.ag1 = spread(ring_y, base, 64, 0), spread(ring_z, base + 256, 64, 1)
            self.ag2, self.ag3 = spread(ring_z, row_y, 16, 2), spread(ring_y, row_z, 16, 3)
            done = wfin.at[core_rows, cols]
            self.give = remote(done, done, sem.at[2], sem.at[3], sibling)
            self.take = remote(done, wfin.at[other_rows, cols], sem.at[2], sem.at[3], sibling)
            self.store = pltpu.make_async_copy(
                wfin.at[:, cols], w_out.at[:, cols], loc.at[12 + k]
            )

        def step(self, n):
            if n == 0:
                self.swap.start()
            elif n == 1:
                self.swap.wait_recv()
                self.ws[...] = (self.mine[...].astype(f32) + self.got[...].astype(f32)).astype(bf16)
                self.rs0.send_all()
                self.rs1.send_all()
            elif n == 2:
                self.rs0.pass_on()
                self.rs1.pass_on()
            elif n == 3:
                self.rs0.wait()
                self.w0[...] = self.rs0.value().astype(bf16)
                self.rs2.send_all()
                self.rs1.wait()
                self.w1[...] = self.rs1.value().astype(bf16)
                self.rs3.send_all()
            elif n == 4:
                self.rs2.pass_on()
                self.rs3.pass_on()
            elif n == 5:
                self.rs2.wait()
                self.last[0][...] = self.rs2.value().astype(bf16)
                self.ag2.start()
                self.rs3.wait()
                self.last[1][...] = self.rs3.value().astype(bf16)
                self.ag3.start()
            elif n == 6:
                self.ag2.pass_on()
                self.ag3.pass_on()
            elif n == 7:
                self.ag2.wait_rest()
                self.ag0.start()
                self.ag3.wait_rest()
                self.ag1.start()
            elif n == 8:
                self.ag0.pass_on()
                self.ag1.pass_on()
            elif n == 9:
                self.ag0.wait_rest()
                self.ag1.wait_rest()
                self.give.start()
            else:
                self.take.wait_recv()
                self.store.start()

        def wait_sent(self):
            self.swap.wait_send()
            self.give.wait_send()
            for group in (self.rs0, self.rs1, self.rs2, self.rs3,
                          self.ag0, self.ag1, self.ag2, self.ag3):
                group.wait_sent()
            self.store.wait()

    sum_a = WeightSum(0)
    sum_a.step(0)
    rs_a.wait_sent()

    def backward(rb):
        rows = pl.ds(pl.multiple_of(rb * Q, Q), Q)
        dqs = []
        for hd in range(4):
            dch = mm_nt(qkv[2, :, head(hd)], dmx[rows, head(hd)])
            ch = chs[hd, :, rows].astype(f32)
            inner = jnp.sum(ch * dch, axis=0, keepdims=True)
            ds = (ch * (dch - inner)).astype(bf16)
            dss[hd][:, rows] = ds
            dqs.append(mm(k_t[head(hd), :], ds) * 0.125)
        dqkv[0, rows, :] = jnp.concatenate(dqs, axis=0).T.astype(bf16)

    pl.loop(0, 2)(backward)
    sum_a.step(1)
    rs_o[1].pass_on()
    pl.loop(2, 4)(backward)
    sum_a.step(2)
    rs_o[0].wait()
    send_back(rs_o[0], 0, osend, o_x)
    for hp in range(2):
        pair = slice(hp * 128, hp * 128 + 128)
        dks = [mm(dss[hd][...], qkv[0, :, head(hd)]) for hd in (2 * hp, 2 * hp + 1)]
        dqkv[1, :, pair] = jnp.concatenate(dks, axis=1).astype(bf16)
    sum_a.step(3)

    rs_d = ReduceScatter(ring_x, npart, Q, d_rel, d_sum, d_arr, rss.at[5])

    def input_grad(b):
        rows = pl.ds(pl.multiple_of(b * Q, Q), Q)
        total = mm_nt(dqkv[0, rows, :], wqkv[0])
        for c in (1, 2):
            total += mm_nt(dqkv[c, rows, :], wqkv[c])
        npart[rows, :] = total.astype(bf16)

    input_grad(far)
    for copy in rs_d.far:
        copy.start()
    input_grad(left)
    rs_d.near[0].start()
    input_grad(right)
    rs_d.near[1].start()
    input_grad(h)

    weight_part(0, slice(512, 768))
    weight_part(1, slice(768, 1024))
    sum_b = WeightSum(1)
    sum_b.step(0)
    sum_a.step(4)
    rs_d.pass_on()
    sum_a.step(5)
    rs_o[1].wait()
    send_back(rs_o[1], 1, osend, o_x)
    sum_b.step(1)
    sum_a.step(6)

    xhat1, r1 = norm_parts(xp[own_rows, :].astype(f32))
    rs_d.wait()
    dn1 = rs_d.value()
    gtall[own_rows, :] = (dres[...] + norm_back(dn1 * g1_ref[...], xhat1, r1)).astype(bf16)
    ag_g = Gather(ring_x, gtall, Q, ags.at[3])
    ag_g.start()
    nv[0] = as_tile(jnp.sum(dn1 * xhat1, axis=0, keepdims=True))
    nv[1] = as_tile(jnp.sum(dn1, axis=0, keepdims=True))

    def to_x(src, dst, mine, at):
        copies = [
            remote(src(rem4(h + k)), dst.at[mine], vs.at[at], vs.at[at + 1], {"head": rem4(h + k)})
            for k in (1, 2, 3)
        ]
        three = dst.at[pl.ds(0, 3)]
        for copy in copies:
            copy.start()
        return remote(three, three, vs.at[at], vs.at[at + 1], {"head": rem4(h + 1)})

    nx = to_x(lambda k: nv.at[k], nrx, h, 0)
    sum_b.step(2)
    sum_a.step(7)
    sum_b.step(3)
    nx.wait_recv()
    nye[me] = nv[h] + nrx[rem4(h + 1)] + nrx[rem4(h + 2)] + nrx[rem4(h + 3)]

    def n_all(d):
        return remote(nye.at[me], nye.at[me], vs.at[2], vs.at[3], {"expert": d})

    n_rows = nye.at[pl.ds(0, G - 1)]
    n_every = remote(n_rows, n_rows, vs.at[2], vs.at[3], {"expert": lax.rem(me + 1, G)})
    others(lambda d: n_all(d).start())
    sum_a.step(8)
    ag_g.pass_on()
    sum_b.step(4)

    for e in range(2):
        o_x[e].all.wait_recv()
    outall[own_rows, :] = (att_q[...] + to_tokens(orecv, 0) + to_tokens(orecv, 1)).astype(bf16)
    ag_o = Gather(ring_x, outall, Q, ags.at[4])
    ag_o.start()
    sum_b.step(5)
    sum_a.step(9)
    sum_b.step(6)
    n_every.wait_recv()
    nrm_out[h] = jnp.sum(nye[...], axis=0)
    nf = to_x(lambda k: nrm_out.at[h], nrm_out, h, 4)
    sum_b.step(7)
    sum_a.step(10)
    ag_o.pass_on()
    sum_b.step(8)
    ag_g.wait_rest()
    gt_store = pltpu.make_async_copy(gtall, gt_out, loc.at[14])
    gt_store.start()
    sum_b.step(9)
    ag_o.wait_rest()
    u_store = pltpu.make_async_copy(outall, u_out, loc.at[11])
    u_store.start()
    nf.wait_recv()
    sum_b.step(10)

    for x in n_x + e_x + o_x:
        x.all.wait_send()
    n_every.wait_send()
    for group in (*rs_e, *rs_o, rs_d, *ag_x, ag_d, ag_o, ag_g, sum_a, sum_b):
        group.wait_sent()
    nx.wait_send()
    nf.wait_send()
    for copy in [stores[0], *stores[2:], gt_store, u_store]:
        copy.wait()


def layer(seg, route, g1, b1, g2, b2, tok, wqkv, wout, win, wbk, cot):
    vmem = pl.BlockSpec(memory_space=pltpu.VMEM)
    hbm = pl.BlockSpec(memory_space=pl.ANY)
    V = pltpu.VMEM
    DMA = pltpu.SemaphoreType.DMA

    def rs_bufs(rows, cols):
        return [V((2, rows, cols), bf16), V((2, rows, cols), bf16), V((2, 2, rows, cols), bf16)]

    pair_bufs = [V((2, *buf.shape), bf16) for buf in rs_bufs(Q, HALF)]
    scratch = [
        V((T, D), bf16), V((3, D, 256), bf16), V((256, D), bf16), V((2, D, D), bf16),
        V((2, D, D), bf16), V((T, D), f32), V((T, D), bf16),
        V((T, T), bf16), V((T, T), bf16), V((T, 1), i32), V((1, T), i32), V((Q, 1), i32),
        V((1, Q), i32),
        V((2, T, D), bf16), V((2, T, D), bf16), V((2, T, D), bf16),
        V((T, D), bf16), V((T, D), bf16), V((D, T), bf16), V((3, T, 256), bf16),
        V((256, T), bf16), V((4, T, T), bf16), V((T, 256), bf16), V((256, T), bf16),
        V((T, D), bf16), *rs_bufs(Q, HALF),
        V((Q, D), bf16), V((2, T, 256), bf16), V((2, T, 256), bf16), *[V((2, T, D), bf16)] * 4,
        *pair_bufs, V((2, T, 256), bf16), V((2, T, 256), bf16),
        *pair_bufs, V((2, T, 256), bf16), V((2, T, 256), bf16), V((T, D), bf16),
        V((T, D), bf16), V((T, 256), bf16), V((256, T), bf16), V((3, T, 256), bf16),
        *rs_bufs(Q, HALF), V((T, D), bf16),
        V((T, D), bf16), V((D, D), bf16),
        V((64, D), bf16), *rs_bufs(64, HALF), V((64, D), bf16), *rs_bufs(64, HALF),
        *rs_bufs(16, HALF), *rs_bufs(16, HALF),
        V((4, 8, 128), f32), V((4, 8, 128), f32), V((G, 8, 128), f32),
        DMA((15,)), *[DMA((2, 2))] * 4, DMA((14, 4)), DMA((13, 4)), DMA((2, 4)), DMA((6,)),
    ]
    S = jax.ShapeDtypeStruct
    quarters = S((2, T, D), bf16)
    return pl.pallas_call(
        layer_kernel,
        name="layer",
        out_shape=[quarters] * 4
        + [S((T, D), bf16), S((T, D), bf16), S((T, T), bf16), S((D, D), bf16), S((4, 8, 128), f32)],
        in_specs=[vmem] * 6 + [hbm] * 6,
        out_specs=[hbm] * 8 + [vmem],
        scratch_shapes=scratch,
        compiler_params=pltpu.CompilerParams(
            collective_id=0, has_side_effects=True, vmem_limit_bytes=62 << 20
        ),
        cost_estimate=pl.CostEstimate(
            flops=24 * 10**9, bytes_accessed=30 * 2**20, transcendentals=4 * 10**6
        ),
    )(seg, route, g1, b1, g2, b2, tok, wqkv, wout, win, wbk, cot)


def finish_kernel(
    x_hbm, dpre_hbm, hid_hbm, g_hbm, w_hbm, u_hbm, gt_hbm, pmt_hbm, tok_hbm,
    win_out, wback_out, wqkv_out, wout_out, out_out, gt_out,
    x, dpre, hid, g, w, u, gt, pmt, tok, win, wback, wqkv, wout, out, gtok, load, store,
):
    pairs = [(x_hbm, x), (dpre_hbm, dpre), (hid_hbm, hid), (g_hbm, g)]
    loads = []
    for e in range(2):
        for i, (src, dst) in enumerate(pairs):
            loads.append(pltpu.make_async_copy(src.at[e], dst.at[e], load.at[e * 4 + i]))
    rest = [(w_hbm, w), (u_hbm, u), (gt_hbm, gt), (pmt_hbm, pmt), (tok_hbm, tok)]
    for i, (src, dst) in enumerate(rest):
        loads.append(pltpu.make_async_copy(src, dst, load.at[8 + i]))
    for copy in loads:
        copy.start()

    def outer(e, lhs, rhs, buf, dst, sem):
        @pl.loop(0, 4)
        def _(c):
            rows = pl.ds(pl.multiple_of(c * 256, 256), 256)
            buf[e, rows, :] = lax.dot_general(
                lhs[e, :, rows], rhs[e], (((0,), (0,)), ((), ())), preferred_element_type=f32
            )
            pltpu.make_async_copy(buf.at[e, rows, :], dst.at[e, rows, :], sem).start()

    for e in range(2):
        loads[e * 4].wait()
        loads[e * 4 + 1].wait()
        outer(e, x, dpre, win, win_out, store.at[0])
        loads[e * 4 + 2].wait()
        loads[e * 4 + 3].wait()
        outer(e, hid, g, wback, wback_out, store.at[1])
    loads[8].wait()
    for c, k in ((0, 2), (1, 3), (2, 1)):
        wqkv[c] = w[:, k * 256 : (k + 1) * 256].astype(f32)
    for k in range(4):
        wout[:, k * 256 : (k + 1) * 256] = w[k * 256 : (k + 1) * 256, :256].astype(f32)
    wq_store = pltpu.make_async_copy(wqkv, wqkv_out, store.at[2])
    wo_store = pltpu.make_async_copy(wout, wout_out, store.at[3])
    wq_store.start()
    wo_store.start()
    for copy in loads[9:]:
        copy.wait()

    @pl.loop(0, 2)
    def _(c):
        rows = pl.ds(pl.multiple_of(c * 256, 256), 256)
        out[rows, :] = tok[rows, :].astype(f32) + mm(pmt[rows, :], u[...])
        pltpu.make_async_copy(out.at[rows, :], out_out.at[rows, :], store.at[4]).start()
        gtok[rows, :] = mm(pmt[rows, :], gt[...])
        pltpu.make_async_copy(gtok.at[rows, :], gt_out.at[rows, :], store.at[5]).start()

    pltpu.make_async_copy(win, win_out, store.at[0]).wait()
    pltpu.make_async_copy(wback, wback_out, store.at[1]).wait()
    wq_store.wait()
    wo_store.wait()
    pltpu.make_async_copy(out, out_out, store.at[4]).wait()
    pltpu.make_async_copy(gtok, gt_out, store.at[5]).wait()


def finish(*operands):
    S = jax.ShapeDtypeStruct
    hbm = pl.BlockSpec(memory_space=pl.ANY)
    results = [
        S((2, D, D), f32), S((2, D, D), f32), S((3, D, 256), f32), S((256, D), f32),
        S((T, D), f32), S((T, D), f32),
    ]
    DMA = pltpu.SemaphoreType.DMA
    return pl.pallas_call(
        finish_kernel,
        name="finish",
        out_shape=results,
        in_specs=[hbm] * len(operands),
        out_specs=[hbm] * len(results),
        scratch_shapes=[pltpu.VMEM(a.shape, a.dtype) for a in (*operands, *results)]
        + [DMA((13,)), DMA((6,))],
        compiler_params=pltpu.CompilerParams(vmem_limit_bytes=60 << 20),
        cost_estimate=pl.CostEstimate(
            flops=8 * 2**30, bytes_accessed=37 * 2**20, transcendentals=0
        ),
    )(*operands)


def per_device(
    tokens, segment_ids, expert_of, norm1_gain, norm1_bias, norm2_gain, norm2_bias,
    w_qkv, w_out, w_in, w_back, cotangent,
):
    row = lambda v: v.reshape(1, D)
    x, g, hid, dpre, u, gt, pmt, w, nrm = layer(
        segment_ids, expert_of.reshape(1, T), row(norm1_gain), row(norm1_bias), row(norm2_gain), row(norm2_bias),
        tokens, w_qkv, w_out, w_in, w_back, cotangent,
    )
    grad_w_in, grad_w_back, grad_w_qkv, grad_w_out, output, grad_tokens = finish(
        x, dpre, hid, g, w, u, gt, pmt, tokens
    )
    vectors = nrm.reshape(4, D)
    return (
        output, grad_tokens, vectors[0], vectors[1], vectors[2], vectors[3],
        grad_w_qkv, grad_w_out, grad_w_in, grad_w_back,
    )


def solution(mesh):
    return jax.shard_map(
        per_device,
        mesh=mesh,
        in_specs=(
            P("expert", None),
            P("expert", None),
            P("expert", None),
            P(),
            P(),
            P(),
            P(),
            P(None, None, "head"),
            P("head", None),
            P("expert", None, "head"),
            P("expert", "head", None),
            P("expert", None),
        ),
        out_specs=(
            P("expert", None),
            P("expert", None),
            P(),
            P(),
            P(),
            P(),
            P(None, None, "head"),
            P("head", None),
            P("expert", None, "head"),
            P("expert", "head", None),
        ),
        check_vma=False,
    )
```

```python
import functools

import jax
import jax.numpy as jnp
from jax import lax
from jax.experimental import pallas as pl
from jax.experimental.pallas import tpu as pltpu
from jax.sharding import PartitionSpec as P

f32 = jnp.float32
bf16 = jnp.bfloat16
i32 = jnp.int32
MESH = pl.DeviceIdType.MESH

T = 512
D = 1024
G = 32
H = 4
Q = T // H
HALF = D // 2
EPS = 1e-5


def mm(a, b):
    return lax.dot_general(a, b, (((1,), (0,)), ((), ())), preferred_element_type=f32)


def mm_nt(a, b):
    return lax.dot_general(a, b, (((1,), (1,)), ((), ())), preferred_element_type=f32)


def iota(shape, dim):
    return lax.broadcasted_iota(i32, shape, dim)


def hot(cond):
    return jnp.where(cond, 1.0, 0.0).astype(bf16)


def rem4(v):
    return lax.rem(v, 4)


def remote(src, dst, send_sem, recv_sem, device):
    return pltpu.make_async_remote_copy(
        src_ref=src,
        dst_ref=dst,
        send_sem=send_sem,
        recv_sem=recv_sem,
        device_id=device,
        device_id_type=MESH,
    )


def columns(ref, rows):
    half = ref.shape[1] // 2
    return lambda b, hf: ref.at[pl.ds(pl.multiple_of(b * rows, rows), rows), pl.ds(hf * half, half)]


class ReduceScatter:
    def __init__(self, ring, whole, rows, relay, total, arrived, sems):
        self.me, right, left = ring
        self.right, self.left = rem4(self.me + 1), rem4(self.me + 3)
        far = rem4(self.me + 2)
        self.part = part = columns(whole, rows)
        self.relay, self.total, self.arrived = relay, total, arrived
        self.three, self.two = whole.at[pl.ds(0, 3 * rows), :], whole.at[pl.ds(0, 2 * rows), :]
        self.sems, self.left_device = sems, left
        send, rest = sems.at[0], sems.at[3]
        self.far = [
            remote(part(far, 0), relay.at[0], send, sems.at[1], left),
            remote(part(far, 1), relay.at[1], send, sems.at[2], right),
        ]
        self.near = [
            remote(part(self.left, 1), arrived.at[1, 1], send, rest, left),
            remote(part(self.right, 0), arrived.at[0, 0], send, rest, right),
        ]
        self.last = [
            remote(total.at[0], arrived.at[1, 0], send, rest, left),
            remote(total.at[1], arrived.at[0, 1], send, rest, right),
        ]

    def send_all(self):
        for copy in self.far + self.near:
            copy.start()

    def pass_on(self):
        for hf, owner in ((0, self.left), (1, self.right)):
            self.far[hf].wait_recv()
            mine = self.part(owner, hf)[...].astype(f32)
            self.total[hf] = (mine + self.relay[hf].astype(f32)).astype(bf16)
            self.last[hf].start()

    def wait(self):
        all_of(self.two, self.sems.at[0], self.sems.at[3], self.left_device).wait_recv()

    def value(self):
        def half(hf):
            mine = self.part(self.me, hf)[...].astype(f32)
            return mine + self.arrived[0, hf].astype(f32) + self.arrived[1, hf].astype(f32)

        return jnp.concatenate([half(0), half(1)], axis=1)

    def wait_sent(self):
        all_of(self.three, self.sems.at[0], self.sems.at[3], self.left_device).wait_send()


class Gather:
    def __init__(self, ring, whole, rows, sems):
        me, right, left = ring
        on_right, on_left = rem4(me + 1), rem4(me + 3)
        block = columns(whole, rows)
        self.three, self.two = whole.at[pl.ds(0, 3 * rows), :], whole.at[pl.ds(0, 2 * rows), :]
        self.sems, self.left_device = sems, left

        def copy(b, hf, i, device):
            return remote(block(b, hf), block(b, hf), sems.at[0], sems.at[i], device)

        self.first = [copy(me, 0, 1, right), copy(me, 1, 2, left)]
        self.second = [copy(me, 0, 3, left), copy(me, 1, 3, right)]
        self.third = [copy(on_left, 0, 3, right), copy(on_right, 1, 3, left)]

    def start(self):
        for copy in self.first + self.second:
            copy.start()

    def pass_on(self):
        for hf in range(2):
            self.first[hf].wait_recv()
            self.third[hf].start()

    def wait_rest(self):
        all_of(self.two, self.sems.at[0], self.sems.at[3], self.left_device).wait_recv()

    def finish(self):
        self.pass_on()
        self.wait_rest()

    def wait_sent(self):
        all_of(self.three, self.sems.at[0], self.sems.at[3], self.left_device).wait_send()


class Exchange:
    def __init__(self, me, src, dst, sems):
        self.me, self.src, self.dst, self.sems = me, src, dst, sems
        rows = pl.ds(0, 16 * (G - 1))
        index = (slice(None),) * (len(src.shape) - 2) + (rows, slice(None))
        other = {"expert": lax.rem(me + 1, G)}
        self.all = remote(src.at[index], dst.at[index], sems.at[0], sems.at[1], other)

    def block(self, ref, d):
        rows = pl.ds(pl.multiple_of(d * 16, 16), 16)
        return ref.at[(slice(None),) * (len(ref.shape) - 2) + (rows, slice(None))]

    def start_chunk(self, chunk):
        @pl.loop(0, 8)
        def _(k):
            d = chunk * 8 + lax.rem(self.me + k, 8)

            @pl.when(d != self.me)
            def _():
                remote(
                    self.block(self.src, d), self.block(self.dst, self.me),
                    self.sems.at[0], self.sems.at[1], {"expert": d},
                ).start()

    def keep_own(self):
        self.block(self.dst, self.me)[...] = self.block(self.src, self.me)[...]


def all_of(view, send_sem, recv_sem, device):
    return remote(view, view, send_sem, recv_sem, device)


def norm_parts(x):
    center = x - jnp.mean(x, axis=-1, keepdims=True)
    r = lax.rsqrt(jnp.mean(center * center, axis=-1, keepdims=True) + EPS)
    return center * r, r


def norm_back(g, xhat, r):
    return r * (
        g - jnp.mean(g, axis=-1, keepdims=True) - xhat * jnp.mean(g * xhat, axis=-1, keepdims=True)
    )


def gelu_parts(v):
    c = 0.7978845608028654
    v2 = v * v
    t = jnp.tanh(c * v * (1.0 + 0.044715 * v2))
    half = 0.5 * (1.0 + t)
    grad = half + 0.5 * v * (1.0 - t * t) * c * (1.0 + 3.0 * 0.044715 * v2)
    return v * half, grad


def as_tile(row):
    return jnp.concatenate([row[:, i * 128 : (i + 1) * 128] for i in range(8)], axis=0)


def layer_kernel(
    seg_ref, route_ref, g1_ref, b1_ref, g2_ref, b2_ref,
    tok_hbm, wqkv_hbm, wout_hbm, win_hbm, wbk_hbm, cot_hbm,
    x_out, g_out, hid_out, dpre_out, u_out, gt_out, pmt_out, w_out, nrm_out,
    tok, wqkv, wout, win, wbk, cotw, cot_low,
    pm, pmt, code_c, code_r, slot_c, slot_r,
    csend, crecv, gal,
    xp, normed, normed_t, qkv, k_t, chs, mixed, mixed_t,
    apart, a_rel, a_sum, a_arr,
    norm2, nsend, nrecv, xall, hid, dpre, n2p,
    e_rel, e_sum, e_arr, esend, erecv,
    o_rel, o_sum, o_arr, osend, orecv, outall,
    datt, dmx, v_t, dqkv,
    d_rel, d_sum, d_arr, gtall,
    wx, wfin,
    wbox,
    nv, nrx, nye,
    loc, cs, ns, es, os_, rss, ags, xs, vs,
):
    me = lax.axis_index("expert")
    h = lax.axis_index("head")
    core = lax.rem(me, 2)
    chip = me // 2

    ring_x = (h, {"head": rem4(h + 1)}, {"head": rem4(h + 3)})
    sibling = {"expert": chip * 2 + 1 - core}
    left, right, far = rem4(h + 3), rem4(h + 1), rem4(h + 2)

    att_q, dres, cot_q = (cotw.at[pl.ds(k * Q, Q), :] for k in range(3))
    npart = tok
    ws = cot_low
    wpart = gal
    dss = [buf.at[:, pl.ds(k * T, T)] for buf in (tok, apart) for k in range(2)]
    outp = csend

    loads = {}
    for i, (name, src, dst) in enumerate(
        (
            ("cot", cot_hbm, cotw),
            ("tok", tok_hbm, tok),
            ("wqkv", wqkv_hbm, wqkv),
            ("wout", wout_hbm, wout),
            ("win", win_hbm, win),
            ("wbk", wbk_hbm, wbk),
        )
    ):
        loads[name] = pltpu.make_async_copy(src, dst, loc.at[i])
        loads[name].start()

    barrier = pltpu.get_barrier_semaphore()

    @pl.loop(1, G)
    def _(k):
        pl.semaphore_signal(
            barrier, inc=1, device_id={"expert": lax.rem(me + k, G)}, device_id_type=MESH
        )

    for k in range(1, H):
        pl.semaphore_signal(barrier, inc=1, device_id={"head": rem4(h + k)}, device_id_type=MESH)

    eye = iota((T, T), 0) == iota((T, T), 1)
    route_row = route_ref[...].astype(f32)
    route_c = jnp.sum(jnp.where(eye, route_row, 0.0), axis=1, keepdims=True).astype(i32)

    def to_row(col):
        return jnp.sum(jnp.where(eye, col.astype(f32), 0.0), axis=0, keepdims=True)

    onehot = jnp.where(iota((T, 128), 1) == route_c, 1.0, 0.0)
    before = hot(iota((T, T), 1) < iota((T, T), 0))
    rank = jnp.sum(mm(before, onehot.astype(bf16)) * onehot, axis=1, keepdims=True)
    count = jnp.broadcast_to(jnp.sum(onehot, axis=0, keepdims=True), (8, 128)).astype(bf16)
    first = mm(count, hot(iota((128, 128), 0) < iota((128, 128), 1)))[0:1]
    place = (jnp.sum(onehot * first, axis=1, keepdims=True) + rank).astype(i32)
    rank4 = rank.astype(i32) >> 2
    quarter = place & 3
    pos_c = quarter * Q + (place >> 2)
    slot4 = route_c * 4 + rank4
    key = (route_c & 1) * T + (route_c >> 1) * 16 + quarter * 4 + rank4
    pos_r = to_row(pos_c).astype(i32)
    key_r = to_row(key).astype(i32)
    perm = iota((T, T), 0) == pos_r
    perm_t = iota((T, T), 1) == pos_c
    pm[...] = hot(perm)
    pmt[...] = hot(perm_t)
    code = (seg_ref[...] * 1024 + iota((1, T), 1)).astype(f32)
    code_pc = jnp.sum(jnp.where(perm, code, 0.0), axis=1, keepdims=True)
    code_c[...] = code_pc.astype(i32)
    code_r[...] = to_row(code_pc).astype(i32)
    own_t = iota((T, Q), 1) + h * Q == pos_c
    slot_row = jnp.sum(jnp.where(own_t, slot4.astype(f32), 0.0), axis=0, keepdims=True)
    slot_r[...] = slot_row.astype(i32)
    eye_q = iota((Q, Q), 0) == iota((Q, Q), 1)
    slot_c[...] = jnp.sum(jnp.where(eye_q, slot_row, 0.0), axis=1, keepdims=True).astype(i32)

    pl.semaphore_wait(barrier, G - 1 + H - 1)

    loads["cot"].wait()
    cot_low[...] = cotw[...].astype(bf16)

    def others(act):
        @pl.loop(1, G)
        def _(k):
            act(lax.rem(me + k, G))

    def exchange(src, dst, sems):
        return [Exchange(me, src.at[e], dst.at[e], sems.at[e]) for e in range(2)]

    cot_x = exchange(csend, crecv, cs)

    def send_cot(e):
        @pl.loop(0, 4)
        def _(c):
            cot_x[e].start_chunk(rem4(me // 8 + c))

        cot_x[e].keep_own()

    @pl.loop(0, 4)
    def _(c):
        chunk = rem4(me // 8 + c)
        row0 = pl.multiple_of(chunk * 128, 128)
        r = iota((256, T), 0)
        sel = hot(row0 + (r & 127) + (r >> 7) * T == key_r)
        rows = mm(sel, cot_low[...]).astype(bf16)
        for e in range(2):
            csend[e, pl.ds(row0, 128), :] = rows[e * 128 : e * 128 + 128]
        cot_x[0].start_chunk(chunk)

    cot_x[0].keep_own()

    loads["tok"].wait()

    @pl.loop(0, 4)
    def _(rb):
        rows = pl.ds(pl.multiple_of(rb * Q, Q), Q)
        x = mm(pm[rows, :], tok[...])
        xp[rows, :] = x.astype(bf16)
        xhat, _r = norm_parts(x)
        normed[rows, :] = (xhat * g1_ref[...] + b1_ref[...]).astype(bf16)

    loads["wqkv"].wait()

    @pl.loop(0, 3)
    def _(c):
        qkv[c] = (mm(normed[...], wqkv[c]) * jnp.where(c == 0, 0.125, 1.0)).astype(bf16)

    v_t[...] = qkv[2].astype(f32).T.astype(bf16)

    def head(hd):
        return slice(hd * 64, hd * 64 + 64)

    @pl.loop(0, 4)
    def _(rb):
        rows = pl.ds(pl.multiple_of(rb * Q, Q), Q)
        keys, queries = code_c[...], code_r[:, rows]
        allowed = (keys <= queries) & (keys >= ((queries >> 10) << 10))
        bias = jnp.where(allowed, 0.0, -1e30)
        outs = []
        for hd in range(4):
            s = mm_nt(qkv[1, :, head(hd)], qkv[0, rows, head(hd)]) + bias
            e = jnp.exp(s - jnp.max(s, axis=0, keepdims=True))
            ch = (e * (1.0 / jnp.sum(e, axis=0, keepdims=True))).astype(bf16)
            chs[hd, :, rows] = ch
            outs.append(mm(v_t[head(hd), :], ch))
        heads = jnp.concatenate(outs, axis=0)
        mixed_t[:, rows] = heads.astype(bf16)
        mixed[rows, :] = heads.T.astype(bf16)

    loads["wout"].wait()
    rs_a = ReduceScatter(ring_x, apart, Q, a_rel, a_sum, a_arr, rss.at[0])

    def project(b):
        rows = pl.ds(pl.multiple_of(b * Q, Q), Q)
        apart[rows, :] = mm(mixed[rows, :], wout[...]).astype(bf16)

    project(far)
    for copy in rs_a.far:
        copy.start()
    project(left)
    rs_a.near[0].start()
    project(right)
    rs_a.near[1].start()
    project(h)
    own_rows = pl.ds(pl.multiple_of(h * Q, Q), Q)

    rs_a.pass_on()
    k_t[...] = qkv[1].astype(f32).T.astype(bf16)

    @pl.loop(0, 4)
    def _(c):
        cols = pl.ds(pl.multiple_of(c * 256, 256), 256)
        normed_t[cols, :] = normed[:, cols].astype(f32).T.astype(bf16)

    rs_a.wait()
    att_q[...] = rs_a.value()

    def resid_norm():
        return norm_parts(xp[own_rows, :].astype(f32) + att_q[...])

    xhat2, _r2 = resid_norm()
    norm2[...] = (xhat2 * g2_ref[...] + b2_ref[...]).astype(bf16)
    n_x = exchange(nsend, nrecv, ns)

    def pick_quarter(full):
        cq = (iota((128, 256), 0) >> 2) & 3
        out = full[:, :256]
        for k in (1, 2, 3):
            out = jnp.where(cq == k, full[:, k * 256 : (k + 1) * 256], out)
        return out.astype(bf16)

    for e in range(2):

        @pl.loop(0, 4)
        def _(c):
            chunk = rem4(me // 8 + c)
            row0 = pl.multiple_of(chunk * 128, 128)
            r = iota((128, Q), 0) + row0
            sel = hot((r >> 4) * 8 + e * 4 + (r & 3) == slot_r[...])
            nsend[e, pl.ds(row0, 128), :] = pick_quarter(mm(sel, norm2[...]))
            n_x[e].start_chunk(chunk)

        n_x[e].keep_own()

    sel_own = hot(iota((Q, T), 0) + h * Q == iota((Q, T), 1))
    cot_q[...] = mm(mm(sel_own, pm[...]).astype(bf16), cot_low[...])
    i = iota((T, T), 0)
    pm[...] = hot(((i & 127) >> 2) * 16 + (i >> 7) * 4 + (i & 3) == iota((T, T), 1))

    def regroup(e):
        cot_x[e].all.wait_recv()

        @pl.loop(0, 4)
        def _(c):
            cols = pl.ds(pl.multiple_of(c * 256, 256), 256)
            gal[e, :, cols] = mm(pm[...], crecv[e, :, cols]).astype(bf16)

    regroup(0)
    ag_x = [Gather(ring_x, xall.at[e], Q, ags.at[e]) for e in range(2)]

    def compact(e):
        n_x[e].all.wait_recv()
        i = iota((Q, T), 0)
        target = (i >> 2) * 16 + (i & 3)
        for cq in range(4):
            sel = hot(iota((Q, T), 1) == target + cq * 4)
            xall[e, own_rows, cq * 256 : (cq + 1) * 256] = mm(sel, nrecv[e]).astype(bf16)

    compact(0)
    ag_x[0].start()
    compact(1)
    send_cot(1)
    ag_x[0].pass_on()
    ag_x[1].start()

    loads["win"].wait()
    loads["wbk"].wait()

    def unit(e):
        @pl.loop(0, 2)
        def _(c):
            cols = pl.ds(pl.multiple_of(c * 512, 512), 512)
            act, slope = gelu_parts(mm(xall[e], win[e, :, cols]))
            hid[e, :, cols] = act.astype(bf16)
            dpre[e, :, cols] = (mm_nt(gal[e], wbk[e, cols, :]) * slope).astype(bf16)

    def unit_n2(e):
        @pl.loop(0, 2)
        def _(c):
            cols = pl.ds(pl.multiple_of(c * 512, 512), 512)
            n2p[e, :, cols] = mm_nt(dpre[e], win[e, cols, :]).astype(bf16)

    def unit_out(e):
        @pl.loop(0, 2)
        def _(c):
            cols = pl.ds(pl.multiple_of(c * 512, 512), 512)
            outp[e, :, cols] = mm(hid[e], wbk[e, :, cols]).astype(bf16)

    def scatter(part, bufs, e, at):
        rel, tot, arr = bufs
        return ReduceScatter(
            ring_x, part.at[e], Q, rel.at[e], tot.at[e], arr.at[e], rss.at[at]
        )

    rs_e = [scatter(n2p, (e_rel, e_sum, e_arr), e, 1 + e) for e in range(2)]
    rs_o = [scatter(outp, (o_rel, o_sum, o_arr), e, 3 + e) for e in range(2)]

    ag_x[0].wait_rest()
    unit(0)
    ag_x[1].pass_on()
    unit_n2(0)
    rs_e[0].send_all()
    for x in cot_x:
        x.all.wait_send()
    unit_out(0)
    regroup(1)
    ag_x[1].wait_rest()
    unit(1)
    rs_e[0].pass_on()
    unit_n2(1)
    rs_e[1].send_all()
    unit_out(1)

    outs = [(xall, x_out), (gal, g_out), (hid, hid_out), (dpre, dpre_out), (pmt, pmt_out)]
    stores = [pltpu.make_async_copy(a, b, loc.at[6 + i]) for i, (a, b) in enumerate(outs)]
    for copy in stores:
        copy.start()

    def send_back(rs, e, buf, x):
        value = rs.value().astype(bf16)
        for c in range(4):
            chunk = rem4(me // 8 + c)
            row0 = pl.multiple_of(chunk * 128, 128)
            r = iota((128, Q), 0) + row0
            sel = hot((r >> 4) * 4 + (r & 3) == iota((128, Q), 1))
            buf[e, pl.ds(row0, 128), :] = pick_quarter(mm(sel, value))
            x[e].start_chunk(chunk)
        x[e].keep_own()

    def to_tokens(buf, e):
        slots = slot_c[...]
        target = jnp.where(((slots >> 2) & 1) == e, (slots >> 3) * 16 + (slots & 3), -T)
        lanes = iota((Q, T), 1)
        return jnp.concatenate(
            [mm(hot(lanes == target + cq * 4), buf[e]) for cq in range(4)], axis=1
        )

    e_x = exchange(esend, erecv, es)
    o_x = exchange(osend, orecv, os_)

    rs_e[0].wait()
    send_back(rs_e[0], 0, esend, e_x)
    rs_e[1].pass_on()
    rs_o[0].send_all()
    rs_e[1].wait()
    send_back(rs_e[1], 1, esend, e_x)

    e_x[0].all.wait_recv()
    dn2 = to_tokens(erecv, 0)
    rs_o[0].pass_on()
    e_x[1].all.wait_recv()
    dn2 = dn2 + to_tokens(erecv, 1)
    xhat2, r2 = resid_norm()
    nv[2] = as_tile(jnp.sum(dn2 * xhat2, axis=0, keepdims=True))
    nv[3] = as_tile(jnp.sum(dn2, axis=0, keepdims=True))
    d_resid = cot_q[...] + norm_back(dn2 * g2_ref[...], xhat2, r2)
    dres[...] = d_resid
    datt[own_rows, :] = d_resid.astype(bf16)
    ag_d = Gather(ring_x, datt, Q, ags.at[2])
    ag_d.start()
    ag_d.pass_on()
    rs_o[1].send_all()
    ag_d.wait_rest()

    stores[1].wait()
    dmx[...] = mm_nt(datt[...], wout[...]).astype(bf16)
    for hp in range(2):
        pair = slice(hp * 128, hp * 128 + 128)
        dvs = [mm(chs[hd], dmx[:, head(hd)]) for hd in (2 * hp, 2 * hp + 1)]
        dqkv[2, :, pair] = jnp.concatenate(dvs, axis=1).astype(bf16)

    def weight_part(c, lanes):
        for k in range(2):
            rows = normed_t[k * T : (k + 1) * T, :]
            wpart[k, :, lanes] = mm(rows, dqkv[c]).astype(bf16)

    for k in range(4):
        block = mm(mixed_t[...], datt[:, k * 256 : (k + 1) * 256]).astype(bf16)
        wpart[k // 2, (k % 2) * 256 : (k % 2) * 256 + 256, 0:256] = block
    weight_part(2, slice(256, 512))

    class WeightSum:
        def __init__(self, k):
            cols, self.sem = pl.ds(k * T, T), xs.at[k]
            core_rows = pl.ds(pl.multiple_of(core * T, T), T)
            other_rows = pl.ds(pl.multiple_of((1 - core) * T, T), T)
            self.mine, self.got, self.ws = wpart.at[core, :, cols], wx.at[:, cols], ws.at[:, cols]
            self.box, self.full = wbox.at[:, cols], wfin.at[core_rows, cols]
            self.swap = self.copy(wpart.at[1 - core, :, cols], self.got, 0, sibling)
            first = pl.ds(0, 15 * 32)
            self.boxes = self.copy(self.ws.at[first, :], self.box.at[first, :], 2, sibling)
            self.rest = self.copy(self.full.at[first, :], self.full.at[first, :], 4, sibling)
            self.give = self.copy(self.full, self.full, 6, sibling)
            self.take = self.copy(self.full, wfin.at[other_rows, cols], 6, sibling)
            self.store = pltpu.make_async_copy(
                wfin.at[:, cols], w_out.at[:, cols], loc.at[12 + k]
            )

        def copy(self, src, dst, at, device):
            return remote(src, dst, self.sem.at[at], self.sem.at[at + 1], device)

        def block(self, ref, c):
            return ref.at[pl.ds(pl.multiple_of(c * 32, 32), 32), :]

        def to_chips(self, src, dst, at):
            @pl.loop(1, 16)
            def _(k):
                c = lax.rem(chip + k, 16)
                block = self.block(src, chip if src is dst else c)
                self.copy(block, self.block(dst, chip), at, {"expert": c * 2 + core}).start()

        def step(self, n):
            if n == 0:
                self.swap.start()
            elif n == 1:
                self.swap.wait_recv()
                self.ws[...] = (self.mine[...].astype(f32) + self.got[...].astype(f32)).astype(bf16)
                self.to_chips(self.ws, self.box, 2)
                self.block(self.box, chip)[...] = self.block(self.ws, chip)[...]
            elif n == 2:
                self.boxes.wait_recv()
                total = self.box[0:32, :].astype(f32)
                for c in range(1, 16):
                    total += self.box[c * 32 : c * 32 + 32, :].astype(f32)
                self.block(self.full, chip)[...] = total.astype(bf16)
                self.to_chips(self.full, self.full, 4)
            elif n == 3:
                self.rest.wait_recv()
                self.give.start()
            else:
                self.take.wait_recv()
                self.store.start()

        def wait_sent(self):
            for copy in (self.swap, self.boxes, self.rest, self.give):
                copy.wait_send()
            self.store.wait()

    sum_a = WeightSum(0)
    sum_a.step(0)
    rs_a.wait_sent()

    def backward(rb):
        rows = pl.ds(pl.multiple_of(rb * Q, Q), Q)
        dqs = []
        for hd in range(4):
            dch = mm_nt(qkv[2, :, head(hd)], dmx[rows, head(hd)])
            ch = chs[hd, :, rows].astype(f32)
            inner = jnp.sum(ch * dch, axis=0, keepdims=True)
            ds = (ch * (dch - inner)).astype(bf16)
            dss[hd][:, rows] = ds
            dqs.append(mm(k_t[head(hd), :], ds) * 0.125)
        dqkv[0, rows, :] = jnp.concatenate(dqs, axis=0).T.astype(bf16)

    pl.loop(0, 2)(backward)
    sum_a.step(1)
    rs_o[1].pass_on()
    pl.loop(2, 4)(backward)
    rs_o[0].wait()
    send_back(rs_o[0], 0, osend, o_x)
    for hp in range(2):
        pair = slice(hp * 128, hp * 128 + 128)
        dks = [mm(dss[hd][...], qkv[0, :, head(hd)]) for hd in (2 * hp, 2 * hp + 1)]
        dqkv[1, :, pair] = jnp.concatenate(dks, axis=1).astype(bf16)

    rs_d = ReduceScatter(ring_x, npart, Q, d_rel, d_sum, d_arr, rss.at[5])

    def input_grad(b):
        rows = pl.ds(pl.multiple_of(b * Q, Q), Q)
        total = mm_nt(dqkv[0, rows, :], wqkv[0])
        for c in (1, 2):
            total += mm_nt(dqkv[c, rows, :], wqkv[c])
        npart[rows, :] = total.astype(bf16)

    input_grad(far)
    for copy in rs_d.far:
        copy.start()
    input_grad(left)
    rs_d.near[0].start()
    input_grad(right)
    rs_d.near[1].start()
    input_grad(h)

    weight_part(0, slice(512, 768))
    weight_part(1, slice(768, 1024))
    sum_b = WeightSum(1)
    sum_b.step(0)
    sum_a.step(2)
    rs_d.pass_on()
    sum_b.step(1)
    rs_o[1].wait()
    send_back(rs_o[1], 1, osend, o_x)

    xhat1, r1 = norm_parts(xp[own_rows, :].astype(f32))
    rs_d.wait()
    dn1 = rs_d.value()
    gtall[own_rows, :] = (dres[...] + norm_back(dn1 * g1_ref[...], xhat1, r1)).astype(bf16)
    ag_g = Gather(ring_x, gtall, Q, ags.at[3])
    ag_g.start()
    nv[0] = as_tile(jnp.sum(dn1 * xhat1, axis=0, keepdims=True))
    nv[1] = as_tile(jnp.sum(dn1, axis=0, keepdims=True))

    def to_x(src, dst, mine, at):
        copies = [
            remote(src(rem4(h + k)), dst.at[mine], vs.at[at], vs.at[at + 1], {"head": rem4(h + k)})
            for k in (1, 2, 3)
        ]
        three = dst.at[pl.ds(0, 3)]
        for copy in copies:
            copy.start()
        return remote(three, three, vs.at[at], vs.at[at + 1], {"head": rem4(h + 1)})

    nx = to_x(lambda k: nv.at[k], nrx, h, 0)
    sum_a.step(3)
    sum_b.step(2)
    nx.wait_recv()
    nye[me] = nv[h] + nrx[rem4(h + 1)] + nrx[rem4(h + 2)] + nrx[rem4(h + 3)]

    def n_all(d):
        return remote(nye.at[me], nye.at[me], vs.at[2], vs.at[3], {"expert": d})

    n_rows = nye.at[pl.ds(0, G - 1)]
    n_every = remote(n_rows, n_rows, vs.at[2], vs.at[3], {"expert": lax.rem(me + 1, G)})
    others(lambda d: n_all(d).start())
    ag_g.pass_on()

    for e in range(2):
        o_x[e].all.wait_recv()
    outall[own_rows, :] = (att_q[...] + to_tokens(orecv, 0) + to_tokens(orecv, 1)).astype(bf16)
    ag_o = Gather(ring_x, outall, Q, ags.at[4])
    ag_o.start()
    sum_a.step(4)
    n_every.wait_recv()
    nrm_out[h] = jnp.sum(nye[...], axis=0)
    nf = to_x(lambda k: nrm_out.at[h], nrm_out, h, 4)
    sum_b.step(3)
    ag_o.pass_on()
    ag_g.wait_rest()
    gt_store = pltpu.make_async_copy(gtall, gt_out, loc.at[14])
    gt_store.start()
    nf.wait_recv()
    sum_b.step(4)
    ag_o.wait_rest()
    u_store = pltpu.make_async_copy(outall, u_out, loc.at[11])
    u_store.start()

    for x in n_x + e_x + o_x:
        x.all.wait_send()
    n_every.wait_send()
    for group in (*rs_e, *rs_o, rs_d, *ag_x, ag_d, ag_o, ag_g, sum_a, sum_b):
        group.wait_sent()
    nx.wait_send()
    nf.wait_send()
    for copy in [stores[0], *stores[2:], gt_store, u_store]:
        copy.wait()


def layer(seg, route, g1, b1, g2, b2, tok, wqkv, wout, win, wbk, cot):
    vmem = pl.BlockSpec(memory_space=pltpu.VMEM)
    hbm = pl.BlockSpec(memory_space=pl.ANY)
    V = pltpu.VMEM
    DMA = pltpu.SemaphoreType.DMA

    def rs_bufs(rows, cols):
        return [V((2, rows, cols), bf16), V((2, rows, cols), bf16), V((2, 2, rows, cols), bf16)]

    pair_bufs = [V((2, *buf.shape), bf16) for buf in rs_bufs(Q, HALF)]
    scratch = [
        V((T, D), bf16), V((3, D, 256), bf16), V((256, D), bf16), V((2, D, D), bf16),
        V((2, D, D), bf16), V((T, D), f32), V((T, D), bf16),
        V((T, T), bf16), V((T, T), bf16), V((T, 1), i32), V((1, T), i32), V((Q, 1), i32),
        V((1, Q), i32),
        V((2, T, D), bf16), V((2, T, D), bf16), V((2, T, D), bf16),
        V((T, D), bf16), V((T, D), bf16), V((D, T), bf16), V((3, T, 256), bf16),
        V((256, T), bf16), V((4, T, T), bf16), V((T, 256), bf16), V((256, T), bf16),
        V((T, D), bf16), *rs_bufs(Q, HALF),
        V((Q, D), bf16), V((2, T, 256), bf16), V((2, T, 256), bf16), *[V((2, T, D), bf16)] * 4,
        *pair_bufs, V((2, T, 256), bf16), V((2, T, 256), bf16),
        *pair_bufs, V((2, T, 256), bf16), V((2, T, 256), bf16), V((T, D), bf16),
        V((T, D), bf16), V((T, 256), bf16), V((256, T), bf16), V((3, T, 256), bf16),
        *rs_bufs(Q, HALF), V((T, D), bf16),
        V((T, D), bf16), V((D, D), bf16),
        V((T, D), bf16),
        V((4, 8, 128), f32), V((4, 8, 128), f32), V((G, 8, 128), f32),
        DMA((15,)), *[DMA((2, 2))] * 4, DMA((6, 4)), DMA((5, 4)), DMA((2, 8)), DMA((6,)),
    ]
    S = jax.ShapeDtypeStruct
    quarters = S((2, T, D), bf16)
    return pl.pallas_call(
        layer_kernel,
        name="layer",
        out_shape=[quarters] * 4
        + [S((T, D), bf16), S((T, D), bf16), S((T, T), bf16), S((D, D), bf16), S((4, 8, 128), f32)],
        in_specs=[vmem] * 6 + [hbm] * 6,
        out_specs=[hbm] * 8 + [vmem],
        scratch_shapes=scratch,
        compiler_params=pltpu.CompilerParams(
            collective_id=0, has_side_effects=True, vmem_limit_bytes=62 << 20
        ),
        cost_estimate=pl.CostEstimate(
            flops=24 * 10**9, bytes_accessed=30 * 2**20, transcendentals=4 * 10**6
        ),
    )(seg, route, g1, b1, g2, b2, tok, wqkv, wout, win, wbk, cot)


def finish_kernel(
    x_hbm, dpre_hbm, hid_hbm, g_hbm, w_hbm, u_hbm, gt_hbm, pmt_hbm, tok_hbm, nrm,
    win_out, wback_out, wqkv_out, wout_out, out_out, gt_out, n0, n1, n2, n3,
    x, dpre, hid, g, w, u, gt, pmt, tok, win, wback, wqkv, wout, out, gtok, load, store,
):
    for k, vector in enumerate((n0, n1, n2, n3)):
        vector[...] = nrm[k]
    pairs = [(x_hbm, x), (dpre_hbm, dpre), (hid_hbm, hid), (g_hbm, g)]
    loads = []
    for e in range(2):
        for i, (src, dst) in enumerate(pairs):
            loads.append(pltpu.make_async_copy(src.at[e], dst.at[e], load.at[e * 4 + i]))
    rest = [(w_hbm, w), (u_hbm, u), (gt_hbm, gt), (pmt_hbm, pmt), (tok_hbm, tok)]
    for i, (src, dst) in enumerate(rest):
        loads.append(pltpu.make_async_copy(src, dst, load.at[8 + i]))
    for copy in loads:
        copy.start()

    def outer(e, lhs, rhs, buf, dst, sem):
        @pl.loop(0, 4)
        def _(c):
            rows = pl.ds(pl.multiple_of(c * 256, 256), 256)
            buf[e, rows, :] = lax.dot_general(
                lhs[e, :, rows], rhs[e], (((0,), (0,)), ((), ())), preferred_element_type=f32
            )
            pltpu.make_async_copy(buf.at[e, rows, :], dst.at[e, rows, :], sem).start()

    for e in range(2):
        loads[e * 4].wait()
        loads[e * 4 + 1].wait()
        outer(e, x, dpre, win, win_out, store.at[0])
        loads[e * 4 + 2].wait()
        loads[e * 4 + 3].wait()
        outer(e, hid, g, wback, wback_out, store.at[1])
    loads[8].wait()
    for c, k in ((0, 2), (1, 3), (2, 1)):
        wqkv[c] = w[:, k * 256 : (k + 1) * 256].astype(f32)
    for k in range(4):
        wout[:, k * 256 : (k + 1) * 256] = w[k * 256 : (k + 1) * 256, :256].astype(f32)
    wq_store = pltpu.make_async_copy(wqkv, wqkv_out, store.at[2])
    wo_store = pltpu.make_async_copy(wout, wout_out, store.at[3])
    wq_store.start()
    wo_store.start()
    for copy in loads[9:]:
        copy.wait()

    @pl.loop(0, 2)
    def _(c):
        rows = pl.ds(pl.multiple_of(c * 256, 256), 256)
        out[rows, :] = tok[rows, :].astype(f32) + mm(pmt[rows, :], u[...])
        pltpu.make_async_copy(out.at[rows, :], out_out.at[rows, :], store.at[4]).start()
        gtok[rows, :] = mm(pmt[rows, :], gt[...])
        pltpu.make_async_copy(gtok.at[rows, :], gt_out.at[rows, :], store.at[5]).start()

    pltpu.make_async_copy(win, win_out, store.at[0]).wait()
    pltpu.make_async_copy(wback, wback_out, store.at[1]).wait()
    wq_store.wait()
    wo_store.wait()
    pltpu.make_async_copy(out, out_out, store.at[4]).wait()
    pltpu.make_async_copy(gtok, gt_out, store.at[5]).wait()


def finish(nrm, *operands):
    S = jax.ShapeDtypeStruct
    hbm = pl.BlockSpec(memory_space=pl.ANY)
    vmem = pl.BlockSpec(memory_space=pltpu.VMEM)
    results = [
        S((2, D, D), f32), S((2, D, D), f32), S((3, D, 256), f32), S((256, D), f32),
        S((T, D), f32), S((T, D), f32),
    ]
    DMA = pltpu.SemaphoreType.DMA
    return pl.pallas_call(
        finish_kernel,
        name="finish",
        out_shape=results + [S((8, 128), f32)] * 4,
        in_specs=[hbm] * len(operands) + [vmem],
        out_specs=[hbm] * len(results) + [vmem] * 4,
        scratch_shapes=[pltpu.VMEM(a.shape, a.dtype) for a in (*operands, *results)]
        + [DMA((13,)), DMA((6,))],
        compiler_params=pltpu.CompilerParams(vmem_limit_bytes=60 << 20),
        cost_estimate=pl.CostEstimate(
            flops=8 * 2**30, bytes_accessed=37 * 2**20, transcendentals=0
        ),
    )(*operands, nrm)


def per_device(
    tokens, segment_ids, expert_of, norm1_gain, norm1_bias, norm2_gain, norm2_bias,
    w_qkv, w_out, w_in, w_back, cotangent,
):
    row = lambda v: v.reshape(1, D)
    x, g, hid, dpre, u, gt, pmt, w, nrm = layer(
        segment_ids, expert_of.reshape(1, T), row(norm1_gain), row(norm1_bias), row(norm2_gain), row(norm2_bias),
        tokens, w_qkv, w_out, w_in, w_back, cotangent,
    )
    grad_w_in, grad_w_back, grad_w_qkv, grad_w_out, output, grad_tokens, *vectors = finish(
        nrm, x, dpre, hid, g, w, u, gt, pmt, tokens
    )
    vectors = [v.reshape(D) for v in vectors]
    return (
        output, grad_tokens, vectors[0], vectors[1], vectors[2], vectors[3],
        grad_w_qkv, grad_w_out, grad_w_in, grad_w_back,
    )


def solution(mesh):
    return jax.shard_map(
        per_device,
        mesh=mesh,
        in_specs=(
            P("expert", None),
            P("expert", None),
            P("expert", None),
            P(),
            P(),
            P(),
            P(),
            P(None, None, "head"),
            P("head", None),
            P("expert", None, "head"),
            P("expert", "head", None),
            P("expert", None),
        ),
        out_specs=(
            P("expert", None),
            P("expert", None),
            P(),
            P(),
            P(),
            P(),
            P(None, None, "head"),
            P("head", None),
            P("expert", None, "head"),
            P("expert", "head", None),
        ),
        check_vma=False,
    )
```

```python
import functools

import jax
import jax.numpy as jnp
from jax import lax
from jax.experimental import pallas as pl
from jax.experimental.pallas import tpu as pltpu
from jax.sharding import PartitionSpec as P

f32 = jnp.float32
bf16 = jnp.bfloat16
i32 = jnp.int32
MESH = pl.DeviceIdType.MESH

T = 512
D = 1024
G = 32
H = 4
Q = T // H
HALF = D // 2
EPS = 1e-5


def mm(a, b):
    return lax.dot_general(a, b, (((1,), (0,)), ((), ())), preferred_element_type=f32)


def mm_nt(a, b):
    return lax.dot_general(a, b, (((1,), (1,)), ((), ())), preferred_element_type=f32)


def iota(shape, dim):
    return lax.broadcasted_iota(i32, shape, dim)


def hot(cond):
    return jnp.where(cond, 1.0, 0.0).astype(bf16)


def rem4(v):
    return lax.rem(v, 4)


def remote(src, dst, send_sem, recv_sem, device):
    return pltpu.make_async_remote_copy(
        src_ref=src,
        dst_ref=dst,
        send_sem=send_sem,
        recv_sem=recv_sem,
        device_id=device,
        device_id_type=MESH,
    )


def columns(ref, rows):
    half = ref.shape[1] // 2
    return lambda b, hf: ref.at[pl.ds(pl.multiple_of(b * rows, rows), rows), pl.ds(hf * half, half)]


class ReduceScatter:
    def __init__(self, ring, whole, rows, relay, total, arrived, sems):
        self.me, right, left = ring
        self.right, self.left = rem4(self.me + 1), rem4(self.me + 3)
        far = rem4(self.me + 2)
        self.part = part = columns(whole, rows)
        self.relay, self.total, self.arrived = relay, total, arrived
        self.three, self.two = whole.at[pl.ds(0, 3 * rows), :], whole.at[pl.ds(0, 2 * rows), :]
        self.sems, self.left_device = sems, left
        send, rest = sems.at[0], sems.at[3]
        self.far = [
            remote(part(far, 0), relay.at[0], send, sems.at[1], left),
            remote(part(far, 1), relay.at[1], send, sems.at[2], right),
        ]
        self.near = [
            remote(part(self.left, 1), arrived.at[1, 1], send, rest, left),
            remote(part(self.right, 0), arrived.at[0, 0], send, rest, right),
        ]
        self.last = [
            remote(total.at[0], arrived.at[1, 0], send, rest, left),
            remote(total.at[1], arrived.at[0, 1], send, rest, right),
        ]

    def send_all(self):
        for copy in self.far + self.near:
            copy.start()

    def pass_on(self):
        for hf, owner in ((0, self.left), (1, self.right)):
            self.far[hf].wait_recv()
            mine = self.part(owner, hf)[...].astype(f32)
            self.total[hf] = (mine + self.relay[hf].astype(f32)).astype(bf16)
            self.last[hf].start()

    def wait(self):
        all_of(self.two, self.sems.at[0], self.sems.at[3], self.left_device).wait_recv()

    def value(self):
        def half(hf):
            mine = self.part(self.me, hf)[...].astype(f32)
            return mine + self.arrived[0, hf].astype(f32) + self.arrived[1, hf].astype(f32)

        return jnp.concatenate([half(0), half(1)], axis=1)

    def wait_sent(self):
        all_of(self.three, self.sems.at[0], self.sems.at[3], self.left_device).wait_send()


class Gather:
    def __init__(self, ring, whole, rows, sems):
        me, right, left = ring
        on_right, on_left = rem4(me + 1), rem4(me + 3)
        block = columns(whole, rows)
        self.three, self.two = whole.at[pl.ds(0, 3 * rows), :], whole.at[pl.ds(0, 2 * rows), :]
        self.sems, self.left_device = sems, left

        def copy(b, hf, i, device):
            return remote(block(b, hf), block(b, hf), sems.at[0], sems.at[i], device)

        self.first = [copy(me, 0, 1, right), copy(me, 1, 2, left)]
        self.second = [copy(me, 0, 3, left), copy(me, 1, 3, right)]
        self.third = [copy(on_left, 0, 3, right), copy(on_right, 1, 3, left)]

    def start(self):
        for copy in self.first + self.second:
            copy.start()

    def pass_on(self):
        for hf in range(2):
            self.first[hf].wait_recv()
            self.third[hf].start()

    def wait_rest(self):
        all_of(self.two, self.sems.at[0], self.sems.at[3], self.left_device).wait_recv()

    def finish(self):
        self.pass_on()
        self.wait_rest()

    def wait_sent(self):
        all_of(self.three, self.sems.at[0], self.sems.at[3], self.left_device).wait_send()


class Exchange:
    def __init__(self, me, src, dst, sems):
        self.me, self.src, self.dst, self.sems = me, src, dst, sems
        rows = pl.ds(0, 16 * (G - 1))
        index = (slice(None),) * (len(src.shape) - 2) + (rows, slice(None))
        other = {"expert": lax.rem(me + 1, G)}
        self.all = remote(src.at[index], dst.at[index], sems.at[0], sems.at[1], other)

    def block(self, ref, d):
        rows = pl.ds(pl.multiple_of(d * 16, 16), 16)
        return ref.at[(slice(None),) * (len(ref.shape) - 2) + (rows, slice(None))]

    def start_chunk(self, chunk):
        @pl.loop(0, 8)
        def _(k):
            d = chunk * 8 + lax.rem(self.me + k, 8)

            @pl.when(d != self.me)
            def _():
                remote(
                    self.block(self.src, d), self.block(self.dst, self.me),
                    self.sems.at[0], self.sems.at[1], {"expert": d},
                ).start()

    def keep_own(self):
        self.block(self.dst, self.me)[...] = self.block(self.src, self.me)[...]


def all_of(view, send_sem, recv_sem, device):
    return remote(view, view, send_sem, recv_sem, device)


def norm_parts(x):
    center = x - jnp.mean(x, axis=-1, keepdims=True)
    r = lax.rsqrt(jnp.mean(center * center, axis=-1, keepdims=True) + EPS)
    return center * r, r


def norm_back(g, xhat, r):
    return r * (
        g - jnp.mean(g, axis=-1, keepdims=True) - xhat * jnp.mean(g * xhat, axis=-1, keepdims=True)
    )


def gelu_parts(v):
    c = 0.7978845608028654
    v2 = v * v
    t = jnp.tanh(c * v * (1.0 + 0.044715 * v2))
    half = 0.5 * (1.0 + t)
    grad = half + 0.5 * v * (1.0 - t * t) * c * (1.0 + 3.0 * 0.044715 * v2)
    return v * half, grad


def as_tile(row):
    return jnp.concatenate([row[:, i * 128 : (i + 1) * 128] for i in range(8)], axis=0)


def layer_kernel(
    seg_ref, route_ref, g1_ref, b1_ref, g2_ref, b2_ref,
    tok_hbm, wqkv_hbm, wout_hbm, win_hbm, wbk_hbm, cot_hbm,
    x_out, g_out, hid_out, dpre_out, u_out, gt_out, pmt_out, w_out, nrm_out,
    tok, wqkv, wout, win, wbk, cotw, cot_low,
    pm, pmt, code_c, code_r, slot_c, slot_r,
    csend, crecv, gal,
    xp, normed, normed_t, qkv, k_t, chs, mixed, mixed_t,
    apart, a_rel, a_sum, a_arr,
    norm2, nsend, nrecv, xall, hid, dpre, n2p,
    e_rel, e_sum, e_arr, esend, erecv,
    o_rel, o_sum, o_arr, osend, orecv, outall,
    datt, dmx, v_t, dqkv,
    d_rel, d_sum, d_arr, gtall,
    wx, wfin,
    wbox,
    nv, nrx, nye,
    loc, cs, ns, es, os_, rss, ags, xs, vs,
):
    me = lax.axis_index("expert")
    h = lax.axis_index("head")
    core = lax.rem(me, 2)
    chip = me // 2

    ring_x = (h, {"head": rem4(h + 1)}, {"head": rem4(h + 3)})
    sibling = {"expert": chip * 2 + 1 - core}
    left, right, far = rem4(h + 3), rem4(h + 1), rem4(h + 2)

    att_q, dres, cot_q = (cotw.at[pl.ds(k * Q, Q), :] for k in range(3))
    npart = tok
    ws = cot_low
    wpart = gal
    dss = [buf.at[:, pl.ds(k * T, T)] for buf in (tok, apart) for k in range(2)]
    outp = csend

    loads = {}
    for i, (name, src, dst) in enumerate(
        (
            ("cot", cot_hbm, cotw),
            ("tok", tok_hbm, tok),
            ("wqkv", wqkv_hbm, wqkv),
            ("wout", wout_hbm, wout),
            ("win", win_hbm, win),
            ("wbk", wbk_hbm, wbk),
        )
    ):
        loads[name] = pltpu.make_async_copy(src, dst, loc.at[i])
        loads[name].start()

    barrier = pltpu.get_barrier_semaphore()

    @pl.loop(1, G)
    def _(k):
        pl.semaphore_signal(
            barrier, inc=1, device_id={"expert": lax.rem(me + k, G)}, device_id_type=MESH
        )

    for k in range(1, H):
        pl.semaphore_signal(barrier, inc=1, device_id={"head": rem4(h + k)}, device_id_type=MESH)

    eye = iota((T, T), 0) == iota((T, T), 1)
    route_row = route_ref[...].astype(f32)
    route_c = jnp.sum(jnp.where(eye, route_row, 0.0), axis=1, keepdims=True).astype(i32)

    def to_row(col):
        return jnp.sum(jnp.where(eye, col.astype(f32), 0.0), axis=0, keepdims=True)

    onehot = jnp.where(iota((T, 128), 1) == route_c, 1.0, 0.0)
    before = hot(iota((T, T), 1) < iota((T, T), 0))
    rank = jnp.sum(mm(before, onehot.astype(bf16)) * onehot, axis=1, keepdims=True)
    count = jnp.broadcast_to(jnp.sum(onehot, axis=0, keepdims=True), (8, 128)).astype(bf16)
    first = mm(count, hot(iota((128, 128), 0) < iota((128, 128), 1)))[0:1]
    place = (jnp.sum(onehot * first, axis=1, keepdims=True) + rank).astype(i32)
    rank4 = rank.astype(i32) >> 2
    quarter = place & 3
    pos_c = quarter * Q + (place >> 2)
    slot4 = route_c * 4 + rank4
    key = (route_c & 1) * T + (route_c >> 1) * 16 + quarter * 4 + rank4
    pos_r = to_row(pos_c).astype(i32)
    key_r = to_row(key).astype(i32)
    perm = iota((T, T), 0) == pos_r
    perm_t = iota((T, T), 1) == pos_c
    pm[...] = hot(perm)
    pmt[...] = hot(perm_t)
    code = (seg_ref[...] * 1024 + iota((1, T), 1)).astype(f32)
    code_pc = jnp.sum(jnp.where(perm, code, 0.0), axis=1, keepdims=True)
    code_c[...] = code_pc.astype(i32)
    code_r[...] = to_row(code_pc).astype(i32)
    own_t = iota((T, Q), 1) + h * Q == pos_c
    slot_row = jnp.sum(jnp.where(own_t, slot4.astype(f32), 0.0), axis=0, keepdims=True)
    slot_r[...] = slot_row.astype(i32)
    eye_q = iota((Q, Q), 0) == iota((Q, Q), 1)
    slot_c[...] = jnp.sum(jnp.where(eye_q, slot_row, 0.0), axis=1, keepdims=True).astype(i32)

    pl.semaphore_wait(barrier, G - 1 + H - 1)

    loads["cot"].wait()
    cot_low[...] = cotw[...].astype(bf16)

    def others(act):
        @pl.loop(1, G)
        def _(k):
            act(lax.rem(me + k, G))

    def exchange(src, dst, sems):
        return [Exchange(me, src.at[e], dst.at[e], sems.at[e]) for e in range(2)]

    cot_x = exchange(csend, crecv, cs)

    def send_cot(e):
        @pl.loop(0, 4)
        def _(c):
            cot_x[e].start_chunk(rem4(me // 8 + c))

        cot_x[e].keep_own()

    @pl.loop(0, 4)
    def _(c):
        chunk = rem4(me // 8 + c)
        row0 = pl.multiple_of(chunk * 128, 128)
        r = iota((256, T), 0)
        sel = hot(row0 + (r & 127) + (r >> 7) * T == key_r)
        rows = mm(sel, cot_low[...]).astype(bf16)
        for e in range(2):
            csend[e, pl.ds(row0, 128), :] = rows[e * 128 : e * 128 + 128]
        cot_x[0].start_chunk(chunk)

    cot_x[0].keep_own()

    loads["tok"].wait()

    @pl.loop(0, 4)
    def _(rb):
        rows = pl.ds(pl.multiple_of(rb * Q, Q), Q)
        x = mm(pm[rows, :], tok[...])
        xp[rows, :] = x.astype(bf16)
        xhat, _r = norm_parts(x)
        normed[rows, :] = (xhat * g1_ref[...] + b1_ref[...]).astype(bf16)

    loads["wqkv"].wait()

    @pl.loop(0, 3)
    def _(c):
        qkv[c] = (mm(normed[...], wqkv[c]) * jnp.where(c == 0, 0.125, 1.0)).astype(bf16)

    v_t[...] = qkv[2].astype(f32).T.astype(bf16)

    def head(hd):
        return slice(hd * 64, hd * 64 + 64)

    @pl.loop(0, 4)
    def _(rb):
        rows = pl.ds(pl.multiple_of(rb * Q, Q), Q)
        keys, queries = code_c[...], code_r[:, rows]
        allowed = (keys <= queries) & (keys >= ((queries >> 10) << 10))
        bias = jnp.where(allowed, 0.0, -1e30)
        outs = []
        for hd in range(4):
            s = mm_nt(qkv[1, :, head(hd)], qkv[0, rows, head(hd)]) + bias
            e = jnp.exp(s - jnp.max(s, axis=0, keepdims=True))
            ch = (e * (1.0 / jnp.sum(e, axis=0, keepdims=True))).astype(bf16)
            chs[hd, :, rows] = ch
            outs.append(mm(v_t[head(hd), :], ch))
        heads = jnp.concatenate(outs, axis=0)
        mixed_t[:, rows] = heads.astype(bf16)
        mixed[rows, :] = heads.T.astype(bf16)

    loads["wout"].wait()
    rs_a = ReduceScatter(ring_x, apart, Q, a_rel, a_sum, a_arr, rss.at[0])

    def project(b):
        rows = pl.ds(pl.multiple_of(b * Q, Q), Q)
        apart[rows, :] = mm(mixed[rows, :], wout[...]).astype(bf16)

    project(far)
    for copy in rs_a.far:
        copy.start()
    project(left)
    rs_a.near[0].start()
    project(right)
    rs_a.near[1].start()
    project(h)
    own_rows = pl.ds(pl.multiple_of(h * Q, Q), Q)

    rs_a.pass_on()
    k_t[...] = qkv[1].astype(f32).T.astype(bf16)

    @pl.loop(0, 4)
    def _(c):
        cols = pl.ds(pl.multiple_of(c * 256, 256), 256)
        normed_t[cols, :] = normed[:, cols].astype(f32).T.astype(bf16)

    rs_a.wait()
    att_q[...] = rs_a.value()

    def resid_norm():
        return norm_parts(xp[own_rows, :].astype(f32) + att_q[...])

    xhat2, _r2 = resid_norm()
    norm2[...] = (xhat2 * g2_ref[...] + b2_ref[...]).astype(bf16)
    n_x = exchange(nsend, nrecv, ns)

    def pick_quarter(full):
        cq = (iota((128, 256), 0) >> 2) & 3
        out = full[:, :256]
        for k in (1, 2, 3):
            out = jnp.where(cq == k, full[:, k * 256 : (k + 1) * 256], out)
        return out.astype(bf16)

    for e in range(2):

        @pl.loop(0, 4)
        def _(c):
            chunk = rem4(me // 8 + c)
            row0 = pl.multiple_of(chunk * 128, 128)
            r = iota((128, Q), 0) + row0
            sel = hot((r >> 4) * 8 + e * 4 + (r & 3) == slot_r[...])
            nsend[e, pl.ds(row0, 128), :] = pick_quarter(mm(sel, norm2[...]))
            n_x[e].start_chunk(chunk)

        n_x[e].keep_own()

    sel_own = hot(iota((Q, T), 0) + h * Q == iota((Q, T), 1))
    cot_q[...] = mm(mm(sel_own, pm[...]).astype(bf16), cot_low[...])
    i = iota((T, T), 0)
    pm[...] = hot(((i & 127) >> 2) * 16 + (i >> 7) * 4 + (i & 3) == iota((T, T), 1))

    def regroup(e):
        cot_x[e].all.wait_recv()

        @pl.loop(0, 4)
        def _(c):
            cols = pl.ds(pl.multiple_of(c * 256, 256), 256)
            gal[e, :, cols] = mm(pm[...], crecv[e, :, cols]).astype(bf16)

    regroup(0)
    ag_x = [Gather(ring_x, xall.at[e], Q, ags.at[e]) for e in range(2)]

    def compact(e):
        n_x[e].all.wait_recv()
        i = iota((Q, T), 0)
        target = (i >> 2) * 16 + (i & 3)
        for cq in range(4):
            sel = hot(iota((Q, T), 1) == target + cq * 4)
            xall[e, own_rows, cq * 256 : (cq + 1) * 256] = mm(sel, nrecv[e]).astype(bf16)

    compact(0)
    ag_x[0].start()
    compact(1)
    send_cot(1)
    ag_x[0].pass_on()
    ag_x[1].start()

    loads["win"].wait()
    loads["wbk"].wait()

    def unit(e, c):
        cols = pl.ds(c * 512, 512)
        act, slope = gelu_parts(mm(xall[e], win[e, :, cols]))
        hid[e, :, cols] = act.astype(bf16)
        dpre[e, :, cols] = (mm_nt(gal[e], wbk[e, cols, :]) * slope).astype(bf16)

    def unit_n2(e):
        @pl.loop(0, 2)
        def _(c):
            cols = pl.ds(pl.multiple_of(c * 512, 512), 512)
            n2p[e, :, cols] = mm_nt(dpre[e], win[e, cols, :]).astype(bf16)

    def unit_out(e):
        @pl.loop(0, 2)
        def _(c):
            cols = pl.ds(pl.multiple_of(c * 512, 512), 512)
            outp[e, :, cols] = mm(hid[e], wbk[e, :, cols]).astype(bf16)

    def scatter(part, bufs, e, at):
        rel, tot, arr = bufs
        return ReduceScatter(
            ring_x, part.at[e], Q, rel.at[e], tot.at[e], arr.at[e], rss.at[at]
        )

    rs_e = [scatter(n2p, (e_rel, e_sum, e_arr), e, 1 + e) for e in range(2)]
    rs_o = [scatter(outp, (o_rel, o_sum, o_arr), e, 3 + e) for e in range(2)]

    ag_x[0].wait_rest()
    unit(0, 0)
    ag_x[1].pass_on()
    unit(0, 1)
    unit_n2(0)
    rs_e[0].send_all()
    for x in cot_x:
        x.all.wait_send()
    unit_out(0)
    regroup(1)
    ag_x[1].wait_rest()
    unit(1, 0)
    rs_e[0].pass_on()
    unit(1, 1)
    unit_n2(1)
    rs_e[1].send_all()
    unit_out(1)

    outs = [(xall, x_out), (gal, g_out), (hid, hid_out), (dpre, dpre_out), (pmt, pmt_out)]
    stores = [pltpu.make_async_copy(a, b, loc.at[6 + i]) for i, (a, b) in enumerate(outs)]
    for copy in stores:
        copy.start()

    def send_back(rs, e, buf, x):
        value = rs.value().astype(bf16)
        for c in range(4):
            chunk = rem4(me // 8 + c)
            row0 = pl.multiple_of(chunk * 128, 128)
            r = iota((128, Q), 0) + row0
            sel = hot((r >> 4) * 4 + (r & 3) == iota((128, Q), 1))
            buf[e, pl.ds(row0, 128), :] = pick_quarter(mm(sel, value))
            x[e].start_chunk(chunk)
        x[e].keep_own()

    def to_tokens(buf, e):
        slots = slot_c[...]
        target = jnp.where(((slots >> 2) & 1) == e, (slots >> 3) * 16 + (slots & 3), -T)
        lanes = iota((Q, T), 1)
        return jnp.concatenate(
            [mm(hot(lanes == target + cq * 4), buf[e]) for cq in range(4)], axis=1
        )

    e_x = exchange(esend, erecv, es)
    o_x = exchange(osend, orecv, os_)

    rs_e[0].wait()
    send_back(rs_e[0], 0, esend, e_x)
    rs_e[1].pass_on()
    rs_o[0].send_all()
    rs_e[1].wait()
    send_back(rs_e[1], 1, esend, e_x)

    e_x[0].all.wait_recv()
    dn2 = to_tokens(erecv, 0)
    rs_o[0].pass_on()
    e_x[1].all.wait_recv()
    dn2 = dn2 + to_tokens(erecv, 1)
    xhat2, r2 = resid_norm()
    nv[2] = as_tile(jnp.sum(dn2 * xhat2, axis=0, keepdims=True))
    nv[3] = as_tile(jnp.sum(dn2, axis=0, keepdims=True))
    d_resid = cot_q[...] + norm_back(dn2 * g2_ref[...], xhat2, r2)
    dres[...] = d_resid
    datt[own_rows, :] = d_resid.astype(bf16)
    ag_d = Gather(ring_x, datt, Q, ags.at[2])
    ag_d.start()
    ag_d.pass_on()
    rs_o[1].send_all()
    ag_d.wait_rest()

    stores[1].wait()
    dmx[...] = mm_nt(datt[...], wout[...]).astype(bf16)
    for hp in range(2):
        pair = slice(hp * 128, hp * 128 + 128)
        dvs = [mm(chs[hd], dmx[:, head(hd)]) for hd in (2 * hp, 2 * hp + 1)]
        dqkv[2, :, pair] = jnp.concatenate(dvs, axis=1).astype(bf16)

    def weight_part(c, lanes):
        for k in range(2):
            rows = normed_t[k * T : (k + 1) * T, :]
            wpart[k, :, lanes] = mm(rows, dqkv[c]).astype(bf16)

    for k in range(4):
        block = mm(mixed_t[...], datt[:, k * 256 : (k + 1) * 256]).astype(bf16)
        wpart[k // 2, (k % 2) * 256 : (k % 2) * 256 + 256, 0:256] = block
    weight_part(2, slice(256, 512))

    class WeightSum:
        def __init__(self, k):
            cols, self.sem = pl.ds(k * T, T), xs.at[k]
            core_rows = pl.ds(pl.multiple_of(core * T, T), T)
            other_rows = pl.ds(pl.multiple_of((1 - core) * T, T), T)
            self.mine, self.got, self.ws = wpart.at[core, :, cols], wx.at[:, cols], ws.at[:, cols]
            self.box, self.full = wbox.at[:, cols], wfin.at[core_rows, cols]
            self.swap = self.copy(wpart.at[1 - core, :, cols], self.got, 0, sibling)
            first = pl.ds(0, 15 * 32)
            self.boxes = self.copy(self.ws.at[first, :], self.box.at[first, :], 2, sibling)
            self.rest = self.copy(self.full.at[first, :], self.full.at[first, :], 4, sibling)
            self.give = self.copy(self.full, self.full, 6, sibling)
            self.take = self.copy(self.full, wfin.at[other_rows, cols], 6, sibling)
            self.store = pltpu.make_async_copy(
                wfin.at[:, cols], w_out.at[:, cols], loc.at[12 + k]
            )

        def copy(self, src, dst, at, device):
            return remote(src, dst, self.sem.at[at], self.sem.at[at + 1], device)

        def block(self, ref, c):
            return ref.at[pl.ds(pl.multiple_of(c * 32, 32), 32), :]

        def to_chips(self, src, dst, at):
            @pl.loop(1, 16)
            def _(k):
                c = lax.rem(chip + k, 16)
                block = self.block(src, chip if src is dst else c)
                self.copy(block, self.block(dst, chip), at, {"expert": c * 2 + core}).start()

        def step(self, n):
            if n == 0:
                self.swap.start()
            elif n == 1:
                self.swap.wait_recv()
                self.ws[...] = (self.mine[...].astype(f32) + self.got[...].astype(f32)).astype(bf16)
                self.to_chips(self.ws, self.box, 2)
                self.block(self.box, chip)[...] = self.block(self.ws, chip)[...]
            elif n == 2:
                self.boxes.wait_recv()
                total = self.box[0:32, :].astype(f32)
                for c in range(1, 16):
                    total += self.box[c * 32 : c * 32 + 32, :].astype(f32)
                self.block(self.full, chip)[...] = total.astype(bf16)
                self.to_chips(self.full, self.full, 4)
            elif n == 3:
                self.rest.wait_recv()
                self.give.start()
            else:
                self.take.wait_recv()
                self.store.start()

        def wait_sent(self):
            for copy in (self.swap, self.boxes, self.rest, self.give):
                copy.wait_send()
            self.store.wait()

    sum_a = WeightSum(0)
    sum_a.step(0)
    rs_a.wait_sent()

    def backward(rb):
        rows = pl.ds(pl.multiple_of(rb * Q, Q), Q)
        dqs = []
        for hd in range(4):
            dch = mm_nt(qkv[2, :, head(hd)], dmx[rows, head(hd)])
            ch = chs[hd, :, rows].astype(f32)
            inner = jnp.sum(ch * dch, axis=0, keepdims=True)
            ds = (ch * (dch - inner)).astype(bf16)
            dss[hd][:, rows] = ds
            dqs.append(mm(k_t[head(hd), :], ds) * 0.125)
        dqkv[0, rows, :] = jnp.concatenate(dqs, axis=0).T.astype(bf16)

    pl.loop(0, 2)(backward)
    sum_a.step(1)
    rs_o[1].pass_on()
    pl.loop(2, 4)(backward)
    rs_o[0].wait()
    send_back(rs_o[0], 0, osend, o_x)
    for hp in range(2):
        pair = slice(hp * 128, hp * 128 + 128)
        dks = [mm(dss[hd][...], qkv[0, :, head(hd)]) for hd in (2 * hp, 2 * hp + 1)]
        dqkv[1, :, pair] = jnp.concatenate(dks, axis=1).astype(bf16)

    rs_d = ReduceScatter(ring_x, npart, Q, d_rel, d_sum, d_arr, rss.at[5])

    def input_grad(b):
        rows = pl.ds(pl.multiple_of(b * Q, Q), Q)
        total = mm_nt(dqkv[0, rows, :], wqkv[0])
        for c in (1, 2):
            total += mm_nt(dqkv[c, rows, :], wqkv[c])
        npart[rows, :] = total.astype(bf16)

    input_grad(far)
    for copy in rs_d.far:
        copy.start()
    input_grad(left)
    rs_d.near[0].start()
    input_grad(right)
    rs_d.near[1].start()
    input_grad(h)

    weight_part(0, slice(512, 768))
    weight_part(1, slice(768, 1024))
    sum_b = WeightSum(1)
    sum_b.step(0)
    sum_a.step(2)
    rs_d.pass_on()
    sum_b.step(1)
    rs_o[1].wait()
    send_back(rs_o[1], 1, osend, o_x)

    xhat1, r1 = norm_parts(xp[own_rows, :].astype(f32))
    rs_d.wait()
    dn1 = rs_d.value()
    gtall[own_rows, :] = (dres[...] + norm_back(dn1 * g1_ref[...], xhat1, r1)).astype(bf16)
    ag_g = Gather(ring_x, gtall, Q, ags.at[3])
    ag_g.start()
    nv[0] = as_tile(jnp.sum(dn1 * xhat1, axis=0, keepdims=True))
    nv[1] = as_tile(jnp.sum(dn1, axis=0, keepdims=True))

    def to_x(src, dst, mine, at):
        copies = [
            remote(src(rem4(h + k)), dst.at[mine], vs.at[at], vs.at[at + 1], {"head": rem4(h + k)})
            for k in (1, 2, 3)
        ]
        three = dst.at[pl.ds(0, 3)]
        for copy in copies:
            copy.start()
        return remote(three, three, vs.at[at], vs.at[at + 1], {"head": rem4(h + 1)})

    nx = to_x(lambda k: nv.at[k], nrx, h, 0)
    sum_a.step(3)
    sum_b.step(2)
    nx.wait_recv()
    nye[me] = nv[h] + nrx[rem4(h + 1)] + nrx[rem4(h + 2)] + nrx[rem4(h + 3)]

    def n_all(d):
        return remote(nye.at[me], nye.at[me], vs.at[2], vs.at[3], {"expert": d})

    n_rows = nye.at[pl.ds(0, G - 1)]
    n_every = remote(n_rows, n_rows, vs.at[2], vs.at[3], {"expert": lax.rem(me + 1, G)})
    others(lambda d: n_all(d).start())
    ag_g.pass_on()

    for e in range(2):
        o_x[e].all.wait_recv()
    outall[own_rows, :] = (att_q[...] + to_tokens(orecv, 0) + to_tokens(orecv, 1)).astype(bf16)
    ag_o = Gather(ring_x, outall, Q, ags.at[4])
    ag_o.start()
    sum_a.step(4)
    n_every.wait_recv()
    nrm_out[h] = jnp.sum(nye[...], axis=0)
    nf = to_x(lambda k: nrm_out.at[h], nrm_out, h, 4)
    sum_b.step(3)
    ag_o.pass_on()
    ag_g.wait_rest()
    gt_store = pltpu.make_async_copy(gtall, gt_out, loc.at[14])
    gt_store.start()
    nf.wait_recv()
    sum_b.step(4)
    ag_o.wait_rest()
    u_store = pltpu.make_async_copy(outall, u_out, loc.at[11])
    u_store.start()

    for x in n_x + e_x + o_x:
        x.all.wait_send()
    n_every.wait_send()
    for group in (*rs_e, *rs_o, rs_d, *ag_x, ag_d, ag_o, ag_g, sum_a, sum_b):
        group.wait_sent()
    nx.wait_send()
    nf.wait_send()
    for copy in [stores[0], *stores[2:], gt_store, u_store]:
        copy.wait()


def layer(seg, route, g1, b1, g2, b2, tok, wqkv, wout, win, wbk, cot):
    vmem = pl.BlockSpec(memory_space=pltpu.VMEM)
    hbm = pl.BlockSpec(memory_space=pl.ANY)
    V = pltpu.VMEM
    DMA = pltpu.SemaphoreType.DMA

    def rs_bufs(rows, cols):
        return [V((2, rows, cols), bf16), V((2, rows, cols), bf16), V((2, 2, rows, cols), bf16)]

    pair_bufs = [V((2, *buf.shape), bf16) for buf in rs_bufs(Q, HALF)]
    scratch = [
        V((T, D), bf16), V((3, D, 256), bf16), V((256, D), bf16), V((2, D, D), bf16),
        V((2, D, D), bf16), V((T, D), f32), V((T, D), bf16),
        V((T, T), bf16), V((T, T), bf16), V((T, 1), i32), V((1, T), i32), V((Q, 1), i32),
        V((1, Q), i32),
        V((2, T, D), bf16), V((2, T, D), bf16), V((2, T, D), bf16),
        V((T, D), bf16), V((T, D), bf16), V((D, T), bf16), V((3, T, 256), bf16),
        V((256, T), bf16), V((4, T, T), bf16), V((T, 256), bf16), V((256, T), bf16),
        V((T, D), bf16), *rs_bufs(Q, HALF),
        V((Q, D), bf16), V((2, T, 256), bf16), V((2, T, 256), bf16), *[V((2, T, D), bf16)] * 4,
        *pair_bufs, V((2, T, 256), bf16), V((2, T, 256), bf16),
        *pair_bufs, V((2, T, 256), bf16), V((2, T, 256), bf16), V((T, D), bf16),
        V((T, D), bf16), V((T, 256), bf16), V((256, T), bf16), V((3, T, 256), bf16),
        *rs_bufs(Q, HALF), V((T, D), bf16),
        V((T, D), bf16), V((D, D), bf16),
        V((T, D), bf16),
        V((4, 8, 128), f32), V((4, 8, 128), f32), V((G, 8, 128), f32),
        DMA((15,)), *[DMA((2, 2))] * 4, DMA((6, 4)), DMA((5, 4)), DMA((2, 8)), DMA((6,)),
    ]
    S = jax.ShapeDtypeStruct
    quarters = S((2, T, D), bf16)
    return pl.pallas_call(
        layer_kernel,
        name="layer",
        out_shape=[quarters] * 4
        + [S((T, D), bf16), S((T, D), bf16), S((T, T), bf16), S((D, D), bf16), S((4, 8, 128), f32)],
        in_specs=[vmem] * 6 + [hbm] * 6,
        out_specs=[hbm] * 8 + [vmem],
        scratch_shapes=scratch,
        compiler_params=pltpu.CompilerParams(
            collective_id=0, has_side_effects=True, vmem_limit_bytes=62 << 20
        ),
        cost_estimate=pl.CostEstimate(
            flops=24 * 10**9, bytes_accessed=30 * 2**20, transcendentals=4 * 10**6
        ),
    )(seg, route, g1, b1, g2, b2, tok, wqkv, wout, win, wbk, cot)


def finish_kernel(
    x_hbm, dpre_hbm, hid_hbm, g_hbm, w_hbm, u_hbm, gt_hbm, pmt_hbm, tok_hbm, nrm,
    win_out, wback_out, wqkv_out, wout_out, out_out, gt_out, n0, n1, n2, n3,
    x, dpre, hid, g, w, u, gt, pmt, tok, win, wback, wqkv, wout, out, gtok, load, store,
):
    vectors = [
        pltpu.make_async_copy(nrm.at[k], vector, store.at[6 + k])
        for k, vector in enumerate((n0, n1, n2, n3))
    ]
    pairs = [(x_hbm, x), (dpre_hbm, dpre), (hid_hbm, hid), (g_hbm, g)]
    loads = []
    for e in range(2):
        for i, (src, dst) in enumerate(pairs):
            loads.append(pltpu.make_async_copy(src.at[e], dst.at[e], load.at[e * 4 + i]))
    rest = [(w_hbm, w), (u_hbm, u), (gt_hbm, gt), (pmt_hbm, pmt), (tok_hbm, tok)]
    for i, (src, dst) in enumerate(rest):
        loads.append(pltpu.make_async_copy(src, dst, load.at[8 + i]))
    for copy in loads + vectors:
        copy.start()

    def outer(e, lhs, rhs, buf, dst, sem):
        @pl.loop(0, 4)
        def _(c):
            rows = pl.ds(pl.multiple_of(c * 256, 256), 256)
            buf[e, rows, :] = lax.dot_general(
                lhs[e, :, rows], rhs[e], (((0,), (0,)), ((), ())), preferred_element_type=f32
            )
            pltpu.make_async_copy(buf.at[e, rows, :], dst.at[e, rows, :], sem).start()

    for e in range(2):
        loads[e * 4].wait()
        loads[e * 4 + 1].wait()
        outer(e, x, dpre, win, win_out, store.at[0])
        loads[e * 4 + 2].wait()
        loads[e * 4 + 3].wait()
        outer(e, hid, g, wback, wback_out, store.at[1])
    loads[8].wait()
    for c, k in ((0, 2), (1, 3), (2, 1)):
        wqkv[c] = w[:, k * 256 : (k + 1) * 256].astype(f32)
    for k in range(4):
        wout[:, k * 256 : (k + 1) * 256] = w[k * 256 : (k + 1) * 256, :256].astype(f32)
    wq_store = pltpu.make_async_copy(wqkv, wqkv_out, store.at[2])
    wo_store = pltpu.make_async_copy(wout, wout_out, store.at[3])
    wq_store.start()
    wo_store.start()
    for copy in loads[9:]:
        copy.wait()

    @pl.loop(0, 2)
    def _(c):
        rows = pl.ds(pl.multiple_of(c * 256, 256), 256)
        out[rows, :] = tok[rows, :].astype(f32) + mm(pmt[rows, :], u[...])
        pltpu.make_async_copy(out.at[rows, :], out_out.at[rows, :], store.at[4]).start()
        gtok[rows, :] = mm(pmt[rows, :], gt[...])
        pltpu.make_async_copy(gtok.at[rows, :], gt_out.at[rows, :], store.at[5]).start()

    pltpu.make_async_copy(win, win_out, store.at[0]).wait()
    pltpu.make_async_copy(wback, wback_out, store.at[1]).wait()
    wq_store.wait()
    wo_store.wait()
    pltpu.make_async_copy(out, out_out, store.at[4]).wait()
    pltpu.make_async_copy(gtok, gt_out, store.at[5]).wait()
    for copy in vectors:
        copy.wait()


def finish(nrm, *operands):
    S = jax.ShapeDtypeStruct
    hbm = pl.BlockSpec(memory_space=pl.ANY)
    results = [
        S((2, D, D), f32), S((2, D, D), f32), S((3, D, 256), f32), S((256, D), f32),
        S((T, D), f32), S((T, D), f32),
    ]
    DMA = pltpu.SemaphoreType.DMA
    return pl.pallas_call(
        finish_kernel,
        name="finish",
        out_shape=results + [S((8, 128), f32)] * 4,
        in_specs=[hbm] * (len(operands) + 1),
        out_specs=[hbm] * (len(results) + 4),
        scratch_shapes=[pltpu.VMEM(a.shape, a.dtype) for a in (*operands, *results)]
        + [DMA((13,)), DMA((10,))],
        compiler_params=pltpu.CompilerParams(vmem_limit_bytes=60 << 20),
        cost_estimate=pl.CostEstimate(
            flops=8 * 2**30, bytes_accessed=37 * 2**20, transcendentals=0
        ),
    )(*operands, nrm)


def per_device(
    tokens, segment_ids, expert_of, norm1_gain, norm1_bias, norm2_gain, norm2_bias,
    w_qkv, w_out, w_in, w_back, cotangent,
):
    row = lambda v: v.reshape(1, D)
    x, g, hid, dpre, u, gt, pmt, w, nrm = layer(
        segment_ids, expert_of.reshape(1, T), row(norm1_gain), row(norm1_bias), row(norm2_gain), row(norm2_bias),
        tokens, w_qkv, w_out, w_in, w_back, cotangent,
    )
    grad_w_in, grad_w_back, grad_w_qkv, grad_w_out, output, grad_tokens, *vectors = finish(
        nrm, x, dpre, hid, g, w, u, gt, pmt, tokens
    )
    vectors = [v.reshape(D) for v in vectors]
    return (
        output, grad_tokens, vectors[0], vectors[1], vectors[2], vectors[3],
        grad_w_qkv, grad_w_out, grad_w_in, grad_w_back,
    )


def solution(mesh):
    return jax.shard_map(
        per_device,
        mesh=mesh,
        in_specs=(
            P("expert", None),
            P("expert", None),
            P("expert", None),
            P(),
            P(),
            P(),
            P(),
            P(None, None, "head"),
            P("head", None),
            P("expert", None, "head"),
            P("expert", "head", None),
            P("expert", None),
        ),
        out_specs=(
            P("expert", None),
            P("expert", None),
            P(),
            P(),
            P(),
            P(),
            P(None, None, "head"),
            P("head", None),
            P("expert", None, "head"),
            P("expert", "head", None),
        ),
        check_vma=False,
    )
```

```python
import functools

import jax
import jax.numpy as jnp
from jax import lax
from jax.experimental import pallas as pl
from jax.experimental.pallas import tpu as pltpu
from jax.sharding import PartitionSpec as P

f32 = jnp.float32
bf16 = jnp.bfloat16
i32 = jnp.int32
MESH = pl.DeviceIdType.MESH

T = 512
D = 1024
G = 32
H = 4
Q = T // H
HALF = D // 2
EPS = 1e-5


def mm(a, b):
    return lax.dot_general(a, b, (((1,), (0,)), ((), ())), preferred_element_type=f32)


def mm_nt(a, b):
    return lax.dot_general(a, b, (((1,), (1,)), ((), ())), preferred_element_type=f32)


def iota(shape, dim):
    return lax.broadcasted_iota(i32, shape, dim)


def hot(cond):
    return jnp.where(cond, 1.0, 0.0).astype(bf16)


def rem4(v):
    return lax.rem(v, 4)


def remote(src, dst, send_sem, recv_sem, device):
    return pltpu.make_async_remote_copy(
        src_ref=src,
        dst_ref=dst,
        send_sem=send_sem,
        recv_sem=recv_sem,
        device_id=device,
        device_id_type=MESH,
    )


def columns(ref, rows):
    half = ref.shape[1] // 2
    return lambda b, hf: ref.at[pl.ds(pl.multiple_of(b * rows, rows), rows), pl.ds(hf * half, half)]


class ReduceScatter:
    def __init__(self, ring, whole, rows, relay, total, arrived, sems):
        self.me, right, left = ring
        self.right, self.left = rem4(self.me + 1), rem4(self.me + 3)
        far = rem4(self.me + 2)
        self.part = part = columns(whole, rows)
        self.relay, self.total, self.arrived = relay, total, arrived
        self.three, self.two = whole.at[pl.ds(0, 3 * rows), :], whole.at[pl.ds(0, 2 * rows), :]
        self.sems, self.left_device = sems, left
        send, rest = sems.at[0], sems.at[3]
        self.far = [
            remote(part(far, 0), relay.at[0], send, sems.at[1], left),
            remote(part(far, 1), relay.at[1], send, sems.at[2], right),
        ]
        self.near = [
            remote(part(self.left, 1), arrived.at[1, 1], send, rest, left),
            remote(part(self.right, 0), arrived.at[0, 0], send, rest, right),
        ]
        self.last = [
            remote(total.at[0], arrived.at[1, 0], send, rest, left),
            remote(total.at[1], arrived.at[0, 1], send, rest, right),
        ]

    def send_all(self):
        for copy in self.far + self.near:
            copy.start()

    def pass_on(self):
        for hf, owner in ((0, self.left), (1, self.right)):
            self.far[hf].wait_recv()
            mine = self.part(owner, hf)[...].astype(f32)
            self.total[hf] = (mine + self.relay[hf].astype(f32)).astype(bf16)
            self.last[hf].start()

    def wait(self):
        all_of(self.two, self.sems.at[0], self.sems.at[3], self.left_device).wait_recv()

    def value(self):
        def half(hf):
            mine = self.part(self.me, hf)[...].astype(f32)
            return mine + self.arrived[0, hf].astype(f32) + self.arrived[1, hf].astype(f32)

        return jnp.concatenate([half(0), half(1)], axis=1)

    def wait_sent(self):
        all_of(self.three, self.sems.at[0], self.sems.at[3], self.left_device).wait_send()


class Gather:
    def __init__(self, ring, whole, rows, sems):
        me, right, left = ring
        on_right, on_left = rem4(me + 1), rem4(me + 3)
        block = columns(whole, rows)
        self.three, self.two = whole.at[pl.ds(0, 3 * rows), :], whole.at[pl.ds(0, 2 * rows), :]
        self.sems, self.left_device = sems, left

        def copy(b, hf, i, device):
            return remote(block(b, hf), block(b, hf), sems.at[0], sems.at[i], device)

        self.first = [copy(me, 0, 1, right), copy(me, 1, 2, left)]
        self.second = [copy(me, 0, 3, left), copy(me, 1, 3, right)]
        self.third = [copy(on_left, 0, 3, right), copy(on_right, 1, 3, left)]

    def start(self):
        for copy in self.first + self.second:
            copy.start()

    def pass_on(self):
        for hf in range(2):
            self.first[hf].wait_recv()
            self.third[hf].start()

    def wait_rest(self):
        all_of(self.two, self.sems.at[0], self.sems.at[3], self.left_device).wait_recv()

    def finish(self):
        self.pass_on()
        self.wait_rest()

    def wait_sent(self):
        all_of(self.three, self.sems.at[0], self.sems.at[3], self.left_device).wait_send()


class Exchange:
    def __init__(self, me, src, dst, sems):
        self.me, self.src, self.dst, self.sems = me, src, dst, sems
        rows = pl.ds(0, 16 * (G - 1))
        index = (slice(None),) * (len(src.shape) - 2) + (rows, slice(None))
        other = {"expert": lax.rem(me + 1, G)}
        self.all = remote(src.at[index], dst.at[index], sems.at[0], sems.at[1], other)

    def block(self, ref, d):
        rows = pl.ds(pl.multiple_of(d * 16, 16), 16)
        return ref.at[(slice(None),) * (len(ref.shape) - 2) + (rows, slice(None))]

    def start_chunk(self, chunk):
        @pl.loop(0, 8)
        def _(k):
            d = chunk * 8 + lax.rem(self.me + k, 8)

            @pl.when(d != self.me)
            def _():
                remote(
                    self.block(self.src, d), self.block(self.dst, self.me),
                    self.sems.at[0], self.sems.at[1], {"expert": d},
                ).start()

    def keep_own(self):
        self.block(self.dst, self.me)[...] = self.block(self.src, self.me)[...]


def all_of(view, send_sem, recv_sem, device):
    return remote(view, view, send_sem, recv_sem, device)


def norm_parts(x):
    center = x - jnp.mean(x, axis=-1, keepdims=True)
    r = lax.rsqrt(jnp.mean(center * center, axis=-1, keepdims=True) + EPS)
    return center * r, r


def norm_back(g, xhat, r):
    return r * (
        g - jnp.mean(g, axis=-1, keepdims=True) - xhat * jnp.mean(g * xhat, axis=-1, keepdims=True)
    )


def gelu_parts(v):
    c = 0.7978845608028654
    v2 = v * v
    t = jnp.tanh(c * v * (1.0 + 0.044715 * v2))
    half = 0.5 * (1.0 + t)
    grad = half + 0.5 * v * (1.0 - t * t) * c * (1.0 + 3.0 * 0.044715 * v2)
    return v * half, grad


def as_tile(row):
    return jnp.concatenate([row[:, i * 128 : (i + 1) * 128] for i in range(8)], axis=0)


def layer_kernel(
    seg_ref, route_ref, g1_ref, b1_ref, g2_ref, b2_ref,
    tok_hbm, wqkv_hbm, wout_hbm, win_hbm, wbk_hbm, cot_hbm,
    x_out, g_out, hid_out, dpre_out, u_out, gt_out, pmt_out, w_out, nrm_out,
    tok, wqkv, wout, win, wbk, cotw, cot_low,
    pm, pmt, code_c, code_r, slot_c, slot_r,
    csend, crecv, gal,
    xp, normed, normed_t, qkv, k_t, chs, mixed, mixed_t,
    apart, a_rel, a_sum, a_arr,
    norm2, nsend, nrecv, xall, hid, dpre, n2p,
    e_rel, e_sum, e_arr, esend, erecv,
    o_rel, o_sum, o_arr, osend, orecv, outall,
    datt, dmx, v_t, dqkv,
    d_rel, d_sum, d_arr, gtall,
    wx, wfin,
    wbox,
    nv, nrx, nye,
    loc, cs, ns, es, os_, rss, ags, xs, vs,
):
    me = lax.axis_index("expert")
    h = lax.axis_index("head")
    core = lax.rem(me, 2)
    chip = me // 2

    ring_x = (h, {"head": rem4(h + 1)}, {"head": rem4(h + 3)})
    sibling = {"expert": chip * 2 + 1 - core}
    left, right, far = rem4(h + 3), rem4(h + 1), rem4(h + 2)

    att_q, dres, cot_q = (cotw.at[pl.ds(k * Q, Q), :] for k in range(3))
    npart = tok
    ws = cot_low
    wpart = gal
    dss = [buf.at[:, pl.ds(k * T, T)] for buf in (tok, apart) for k in range(2)]
    outp = csend

    loads = {}
    for i, (name, src, dst) in enumerate(
        (
            ("cot", cot_hbm, cotw),
            ("tok", tok_hbm, tok),
            ("wqkv", wqkv_hbm, wqkv),
            ("wout", wout_hbm, wout),
            ("win", win_hbm, win),
            ("wbk", wbk_hbm, wbk),
        )
    ):
        loads[name] = pltpu.make_async_copy(src, dst, loc.at[i])
        loads[name].start()

    barrier = pltpu.get_barrier_semaphore()

    @pl.loop(1, G)
    def _(k):
        pl.semaphore_signal(
            barrier, inc=1, device_id={"expert": lax.rem(me + k, G)}, device_id_type=MESH
        )

    for k in range(1, H):
        pl.semaphore_signal(barrier, inc=1, device_id={"head": rem4(h + k)}, device_id_type=MESH)

    eye = iota((T, T), 0) == iota((T, T), 1)
    route_row = route_ref[...].astype(f32)
    route_c = jnp.sum(jnp.where(eye, route_row, 0.0), axis=1, keepdims=True).astype(i32)

    def to_row(col):
        return jnp.sum(jnp.where(eye, col.astype(f32), 0.0), axis=0, keepdims=True)

    onehot = jnp.where(iota((T, 128), 1) == route_c, 1.0, 0.0)
    before = hot(iota((T, T), 1) < iota((T, T), 0))
    rank = jnp.sum(mm(before, onehot.astype(bf16)) * onehot, axis=1, keepdims=True)
    count = jnp.broadcast_to(jnp.sum(onehot, axis=0, keepdims=True), (8, 128)).astype(bf16)
    first = mm(count, hot(iota((128, 128), 0) < iota((128, 128), 1)))[0:1]
    place = (jnp.sum(onehot * first, axis=1, keepdims=True) + rank).astype(i32)
    rank4 = rank.astype(i32) >> 2
    quarter = place & 3
    pos_c = quarter * Q + (place >> 2)
    slot4 = route_c * 4 + rank4
    key = (route_c & 1) * T + (route_c >> 1) * 16 + quarter * 4 + rank4
    pos_r = to_row(pos_c).astype(i32)
    key_r = to_row(key).astype(i32)
    perm = iota((T, T), 0) == pos_r
    perm_t = iota((T, T), 1) == pos_c
    pm[...] = hot(perm)
    pmt[...] = hot(perm_t)
    code = (seg_ref[...] * 1024 + iota((1, T), 1)).astype(f32)
    code_pc = jnp.sum(jnp.where(perm, code, 0.0), axis=1, keepdims=True)
    code_c[...] = code_pc.astype(i32)
    code_r[...] = to_row(code_pc).astype(i32)
    own_t = iota((T, Q), 1) + h * Q == pos_c
    slot_row = jnp.sum(jnp.where(own_t, slot4.astype(f32), 0.0), axis=0, keepdims=True)
    slot_r[...] = slot_row.astype(i32)
    eye_q = iota((Q, Q), 0) == iota((Q, Q), 1)
    slot_c[...] = jnp.sum(jnp.where(eye_q, slot_row, 0.0), axis=1, keepdims=True).astype(i32)

    pl.semaphore_wait(barrier, G - 1 + H - 1)

    loads["cot"].wait()
    cot_low[...] = cotw[...].astype(bf16)

    def others(act):
        @pl.loop(1, G)
        def _(k):
            act(lax.rem(me + k, G))

    def exchange(src, dst, sems):
        return [Exchange(me, src.at[e], dst.at[e], sems.at[e]) for e in range(2)]

    cot_x = exchange(csend, crecv, cs)

    def send_cot(e):
        @pl.loop(0, 4)
        def _(c):
            cot_x[e].start_chunk(rem4(me // 8 + c))

        cot_x[e].keep_own()

    @pl.loop(0, 4)
    def _(c):
        chunk = rem4(me // 8 + c)
        row0 = pl.multiple_of(chunk * 128, 128)
        r = iota((256, T), 0)
        sel = hot(row0 + (r & 127) + (r >> 7) * T == key_r)
        rows = mm(sel, cot_low[...]).astype(bf16)
        for e in range(2):
            csend[e, pl.ds(row0, 128), :] = rows[e * 128 : e * 128 + 128]
        cot_x[0].start_chunk(chunk)

    cot_x[0].keep_own()

    loads["tok"].wait()

    @pl.loop(0, 4)
    def _(rb):
        rows = pl.ds(pl.multiple_of(rb * Q, Q), Q)
        x = mm(pm[rows, :], tok[...])
        xp[rows, :] = x.astype(bf16)
        xhat, _r = norm_parts(x)
        normed[rows, :] = (xhat * g1_ref[...] + b1_ref[...]).astype(bf16)

    loads["wqkv"].wait()

    @pl.loop(0, 3)
    def _(c):
        qkv[c] = (mm(normed[...], wqkv[c]) * jnp.where(c == 0, 0.125, 1.0)).astype(bf16)

    v_t[...] = qkv[2].astype(f32).T.astype(bf16)

    def head(hd):
        return slice(hd * 64, hd * 64 + 64)

    @pl.loop(0, 4)
    def _(rb):
        rows = pl.ds(pl.multiple_of(rb * Q, Q), Q)
        keys, queries = code_c[...], code_r[:, rows]
        allowed = (keys <= queries) & (keys >= ((queries >> 10) << 10))
        bias = jnp.where(allowed, 0.0, -1e30)
        outs = []
        for hd in range(4):
            s = mm_nt(qkv[1, :, head(hd)], qkv[0, rows, head(hd)]) + bias
            e = jnp.exp(s - jnp.max(s, axis=0, keepdims=True))
            ch = (e * (1.0 / jnp.sum(e, axis=0, keepdims=True))).astype(bf16)
            chs[hd, :, rows] = ch
            outs.append(mm(v_t[head(hd), :], ch))
        heads = jnp.concatenate(outs, axis=0)
        mixed_t[:, rows] = heads.astype(bf16)
        mixed[rows, :] = heads.T.astype(bf16)

    loads["wout"].wait()
    rs_a = ReduceScatter(ring_x, apart, Q, a_rel, a_sum, a_arr, rss.at[0])

    def project(b):
        rows = pl.ds(pl.multiple_of(b * Q, Q), Q)
        apart[rows, :] = mm(mixed[rows, :], wout[...]).astype(bf16)

    project(far)
    for copy in rs_a.far:
        copy.start()
    project(left)
    rs_a.near[0].start()
    project(right)
    rs_a.near[1].start()
    project(h)
    own_rows = pl.ds(pl.multiple_of(h * Q, Q), Q)

    rs_a.pass_on()
    k_t[...] = qkv[1].astype(f32).T.astype(bf16)

    @pl.loop(0, 4)
    def _(c):
        cols = pl.ds(pl.multiple_of(c * 256, 256), 256)
        normed_t[cols, :] = normed[:, cols].astype(f32).T.astype(bf16)

    rs_a.wait()
    att_q[...] = rs_a.value()

    def resid_norm():
        return norm_parts(xp[own_rows, :].astype(f32) + att_q[...])

    xhat2, _r2 = resid_norm()
    norm2[...] = (xhat2 * g2_ref[...] + b2_ref[...]).astype(bf16)
    n_x = exchange(nsend, nrecv, ns)

    def pick_quarter(full):
        cq = (iota((128, 256), 0) >> 2) & 3
        out = full[:, :256]
        for k in (1, 2, 3):
            out = jnp.where(cq == k, full[:, k * 256 : (k + 1) * 256], out)
        return out.astype(bf16)

    for e in range(2):

        @pl.loop(0, 4)
        def _(c):
            chunk = rem4(me // 8 + c)
            row0 = pl.multiple_of(chunk * 128, 128)
            r = iota((128, Q), 0) + row0
            sel = hot((r >> 4) * 8 + e * 4 + (r & 3) == slot_r[...])
            nsend[e, pl.ds(row0, 128), :] = pick_quarter(mm(sel, norm2[...]))
            n_x[e].start_chunk(chunk)

        n_x[e].keep_own()

    sel_own = hot(iota((Q, T), 0) + h * Q == iota((Q, T), 1))
    cot_q[...] = mm(mm(sel_own, pm[...]).astype(bf16), cot_low[...])
    i = iota((T, T), 0)
    pm[...] = hot(((i & 127) >> 2) * 16 + (i >> 7) * 4 + (i & 3) == iota((T, T), 1))

    def regroup(e):
        cot_x[e].all.wait_recv()

        @pl.loop(0, 4)
        def _(c):
            cols = pl.ds(pl.multiple_of(c * 256, 256), 256)
            gal[e, :, cols] = mm(pm[...], crecv[e, :, cols]).astype(bf16)

    regroup(0)
    ag_x = [Gather(ring_x, xall.at[e], Q, ags.at[e]) for e in range(2)]

    def compact(e):
        n_x[e].all.wait_recv()
        i = iota((Q, T), 0)
        target = (i >> 2) * 16 + (i & 3)
        for cq in range(4):
            sel = hot(iota((Q, T), 1) == target + cq * 4)
            xall[e, own_rows, cq * 256 : (cq + 1) * 256] = mm(sel, nrecv[e]).astype(bf16)

    compact(0)
    ag_x[0].start()
    compact(1)
    send_cot(1)
    ag_x[0].pass_on()
    ag_x[1].start()

    loads["win"].wait()
    loads["wbk"].wait()

    def unit(e, c):
        cols = pl.ds(c * 512, 512)
        act, slope = gelu_parts(mm(xall[e], win[e, :, cols]))
        hid[e, :, cols] = act.astype(bf16)
        dpre[e, :, cols] = (mm_nt(gal[e], wbk[e, cols, :]) * slope).astype(bf16)

    def unit_n2(e):
        @pl.loop(0, 2)
        def _(c):
            cols = pl.ds(pl.multiple_of(c * 512, 512), 512)
            n2p[e, :, cols] = mm_nt(dpre[e], win[e, cols, :]).astype(bf16)

    def unit_out(e):
        @pl.loop(0, 2)
        def _(c):
            cols = pl.ds(pl.multiple_of(c * 512, 512), 512)
            outp[e, :, cols] = mm(hid[e], wbk[e, :, cols]).astype(bf16)

    def scatter(part, bufs, e, at):
        rel, tot, arr = bufs
        return ReduceScatter(
            ring_x, part.at[e], Q, rel.at[e], tot.at[e], arr.at[e], rss.at[at]
        )

    rs_e = [scatter(n2p, (e_rel, e_sum, e_arr), e, 1 + e) for e in range(2)]
    rs_o = [scatter(outp, (o_rel, o_sum, o_arr), e, 3 + e) for e in range(2)]

    ag_x[0].wait_rest()
    unit(0, 0)
    ag_x[1].pass_on()
    unit(0, 1)
    unit_n2(0)
    rs_e[0].send_all()
    for x in cot_x:
        x.all.wait_send()
    unit_out(0)
    regroup(1)
    ag_x[1].wait_rest()
    unit(1, 0)
    rs_e[0].pass_on()
    unit(1, 1)
    unit_n2(1)
    rs_e[1].send_all()
    unit_out(1)

    outs = [(xall, x_out), (gal, g_out), (hid, hid_out), (dpre, dpre_out), (pmt, pmt_out)]
    stores = [pltpu.make_async_copy(a, b, loc.at[6 + i]) for i, (a, b) in enumerate(outs)]
    for copy in stores:
        copy.start()

    def send_back(rs, e, buf, x):
        value = rs.value().astype(bf16)
        for c in range(4):
            chunk = rem4(me // 8 + c)
            row0 = pl.multiple_of(chunk * 128, 128)
            r = iota((128, Q), 0) + row0
            sel = hot((r >> 4) * 4 + (r & 3) == iota((128, Q), 1))
            buf[e, pl.ds(row0, 128), :] = pick_quarter(mm(sel, value))
            x[e].start_chunk(chunk)
        x[e].keep_own()

    def to_tokens(buf, e):
        slots = slot_c[...]
        target = jnp.where(((slots >> 2) & 1) == e, (slots >> 3) * 16 + (slots & 3), -T)
        lanes = iota((Q, T), 1)
        return jnp.concatenate(
            [mm(hot(lanes == target + cq * 4), buf[e]) for cq in range(4)], axis=1
        )

    e_x = exchange(esend, erecv, es)
    o_x = exchange(osend, orecv, os_)

    rs_e[0].wait()
    send_back(rs_e[0], 0, esend, e_x)
    rs_e[1].pass_on()
    rs_e[1].wait()
    rs_o[0].send_all()
    send_back(rs_e[1], 1, esend, e_x)

    e_x[0].all.wait_recv()
    dn2 = to_tokens(erecv, 0)
    e_x[1].all.wait_recv()
    dn2 = dn2 + to_tokens(erecv, 1)
    xhat2, r2 = resid_norm()
    nv[2] = as_tile(jnp.sum(dn2 * xhat2, axis=0, keepdims=True))
    nv[3] = as_tile(jnp.sum(dn2, axis=0, keepdims=True))
    d_resid = cot_q[...] + norm_back(dn2 * g2_ref[...], xhat2, r2)
    dres[...] = d_resid
    datt[own_rows, :] = d_resid.astype(bf16)
    ag_d = Gather(ring_x, datt, Q, ags.at[2])
    ag_d.start()
    ag_d.pass_on()
    rs_o[0].pass_on()
    rs_o[1].send_all()
    ag_d.wait_rest()

    stores[1].wait()
    dmx[...] = mm_nt(datt[...], wout[...]).astype(bf16)
    for hp in range(2):
        pair = slice(hp * 128, hp * 128 + 128)
        dvs = [mm(chs[hd], dmx[:, head(hd)]) for hd in (2 * hp, 2 * hp + 1)]
        dqkv[2, :, pair] = jnp.concatenate(dvs, axis=1).astype(bf16)

    def weight_part(c, lanes):
        for k in range(2):
            rows = normed_t[k * T : (k + 1) * T, :]
            wpart[k, :, lanes] = mm(rows, dqkv[c]).astype(bf16)

    for k in range(4):
        block = mm(mixed_t[...], datt[:, k * 256 : (k + 1) * 256]).astype(bf16)
        wpart[k // 2, (k % 2) * 256 : (k % 2) * 256 + 256, 0:256] = block
    weight_part(2, slice(256, 512))

    class WeightSum:
        def __init__(self, k):
            cols, self.sem = pl.ds(k * T, T), xs.at[k]
            core_rows = pl.ds(pl.multiple_of(core * T, T), T)
            other_rows = pl.ds(pl.multiple_of((1 - core) * T, T), T)
            self.mine, self.got, self.ws = wpart.at[core, :, cols], wx.at[:, cols], ws.at[:, cols]
            self.box, self.full = wbox.at[:, cols], wfin.at[core_rows, cols]
            self.swap = self.copy(wpart.at[1 - core, :, cols], self.got, 0, sibling)
            first = pl.ds(0, 15 * 32)
            self.boxes = self.copy(self.ws.at[first, :], self.box.at[first, :], 2, sibling)
            self.rest = self.copy(self.full.at[first, :], self.full.at[first, :], 4, sibling)
            self.give = self.copy(self.full, self.full, 6, sibling)
            self.take = self.copy(self.full, wfin.at[other_rows, cols], 6, sibling)
            self.store = pltpu.make_async_copy(
                wfin.at[:, cols], w_out.at[:, cols], loc.at[12 + k]
            )

        def copy(self, src, dst, at, device):
            return remote(src, dst, self.sem.at[at], self.sem.at[at + 1], device)

        def block(self, ref, c):
            return ref.at[pl.ds(pl.multiple_of(c * 32, 32), 32), :]

        def to_chips(self, src, dst, at):
            @pl.loop(1, 16)
            def _(k):
                c = lax.rem(chip + k, 16)
                block = self.block(src, chip if src is dst else c)
                self.copy(block, self.block(dst, chip), at, {"expert": c * 2 + core}).start()

        def step(self, n):
            if n == 0:
                self.swap.start()
            elif n == 1:
                self.swap.wait_recv()
                self.ws[...] = (self.mine[...].astype(f32) + self.got[...].astype(f32)).astype(bf16)
                self.to_chips(self.ws, self.box, 2)
                self.block(self.box, chip)[...] = self.block(self.ws, chip)[...]
            elif n == 2:
                self.boxes.wait_recv()
                total = self.box[0:32, :].astype(f32)
                for c in range(1, 16):
                    total += self.box[c * 32 : c * 32 + 32, :].astype(f32)
                self.block(self.full, chip)[...] = total.astype(bf16)
                self.to_chips(self.full, self.full, 4)
            elif n == 3:
                self.rest.wait_recv()
                self.give.start()
            else:
                self.take.wait_recv()
                self.store.start()

        def wait_sent(self):
            for copy in (self.swap, self.boxes, self.rest, self.give):
                copy.wait_send()
            self.store.wait()

    sum_a = WeightSum(0)
    sum_a.step(0)
    rs_a.wait_sent()

    def backward(rb):
        rows = pl.ds(pl.multiple_of(rb * Q, Q), Q)
        dqs = []
        for hd in range(4):
            dch = mm_nt(qkv[2, :, head(hd)], dmx[rows, head(hd)])
            ch = chs[hd, :, rows].astype(f32)
            inner = jnp.sum(ch * dch, axis=0, keepdims=True)
            ds = (ch * (dch - inner)).astype(bf16)
            dss[hd][:, rows] = ds
            dqs.append(mm(k_t[head(hd), :], ds) * 0.125)
        dqkv[0, rows, :] = jnp.concatenate(dqs, axis=0).T.astype(bf16)

    pl.loop(0, 2)(backward)
    sum_a.step(1)
    rs_o[1].pass_on()
    pl.loop(2, 4)(backward)
    rs_o[0].wait()
    send_back(rs_o[0], 0, osend, o_x)
    for hp in range(2):
        pair = slice(hp * 128, hp * 128 + 128)
        dks = [mm(dss[hd][...], qkv[0, :, head(hd)]) for hd in (2 * hp, 2 * hp + 1)]
        dqkv[1, :, pair] = jnp.concatenate(dks, axis=1).astype(bf16)

    rs_d = ReduceScatter(ring_x, npart, Q, d_rel, d_sum, d_arr, rss.at[5])

    def input_grad(b):
        rows = pl.ds(pl.multiple_of(b * Q, Q), Q)
        total = mm_nt(dqkv[0, rows, :], wqkv[0])
        for c in (1, 2):
            total += mm_nt(dqkv[c, rows, :], wqkv[c])
        npart[rows, :] = total.astype(bf16)

    input_grad(far)
    for copy in rs_d.far:
        copy.start()
    input_grad(left)
    rs_d.near[0].start()
    input_grad(right)
    rs_d.near[1].start()
    input_grad(h)

    weight_part(0, slice(512, 768))
    weight_part(1, slice(768, 1024))
    sum_b = WeightSum(1)
    sum_b.step(0)
    sum_a.step(2)
    rs_d.pass_on()
    sum_b.step(1)
    rs_o[1].wait()
    send_back(rs_o[1], 1, osend, o_x)

    xhat1, r1 = norm_parts(xp[own_rows, :].astype(f32))
    rs_d.wait()
    dn1 = rs_d.value()
    gtall[own_rows, :] = (dres[...] + norm_back(dn1 * g1_ref[...], xhat1, r1)).astype(bf16)
    ag_g = Gather(ring_x, gtall, Q, ags.at[3])
    ag_g.start()
    nv[0] = as_tile(jnp.sum(dn1 * xhat1, axis=0, keepdims=True))
    nv[1] = as_tile(jnp.sum(dn1, axis=0, keepdims=True))

    def to_x(src, dst, mine, at):
        copies = [
            remote(src(rem4(h + k)), dst.at[mine], vs.at[at], vs.at[at + 1], {"head": rem4(h + k)})
            for k in (1, 2, 3)
        ]
        three = dst.at[pl.ds(0, 3)]
        for copy in copies:
            copy.start()
        return remote(three, three, vs.at[at], vs.at[at + 1], {"head": rem4(h + 1)})

    nx = to_x(lambda k: nv.at[k], nrx, h, 0)
    sum_a.step(3)
    sum_b.step(2)
    nx.wait_recv()
    nye[me] = nv[h] + nrx[rem4(h + 1)] + nrx[rem4(h + 2)] + nrx[rem4(h + 3)]

    def n_all(d):
        return remote(nye.at[me], nye.at[me], vs.at[2], vs.at[3], {"expert": d})

    n_rows = nye.at[pl.ds(0, G - 1)]
    n_every = remote(n_rows, n_rows, vs.at[2], vs.at[3], {"expert": lax.rem(me + 1, G)})
    others(lambda d: n_all(d).start())
    ag_g.pass_on()

    for e in range(2):
        o_x[e].all.wait_recv()
    outall[own_rows, :] = (att_q[...] + to_tokens(orecv, 0) + to_tokens(orecv, 1)).astype(bf16)
    ag_o = Gather(ring_x, outall, Q, ags.at[4])
    ag_o.start()
    sum_a.step(4)
    n_every.wait_recv()
    nrm_out[h] = jnp.sum(nye[...], axis=0)
    nf = to_x(lambda k: nrm_out.at[h], nrm_out, h, 4)
    sum_b.step(3)
    ag_o.pass_on()
    ag_g.wait_rest()
    gt_store = pltpu.make_async_copy(gtall, gt_out, loc.at[14])
    gt_store.start()
    nf.wait_recv()
    sum_b.step(4)
    ag_o.wait_rest()
    u_store = pltpu.make_async_copy(outall, u_out, loc.at[11])
    u_store.start()

    for x in n_x + e_x + o_x:
        x.all.wait_send()
    n_every.wait_send()
    for group in (*rs_e, *rs_o, rs_d, *ag_x, ag_d, ag_o, ag_g, sum_a, sum_b):
        group.wait_sent()
    nx.wait_send()
    nf.wait_send()
    for copy in [stores[0], *stores[2:], gt_store, u_store]:
        copy.wait()


def layer(seg, route, g1, b1, g2, b2, tok, wqkv, wout, win, wbk, cot):
    vmem = pl.BlockSpec(memory_space=pltpu.VMEM)
    hbm = pl.BlockSpec(memory_space=pl.ANY)
    V = pltpu.VMEM
    DMA = pltpu.SemaphoreType.DMA

    def rs_bufs(rows, cols):
        return [V((2, rows, cols), bf16), V((2, rows, cols), bf16), V((2, 2, rows, cols), bf16)]

    pair_bufs = [V((2, *buf.shape), bf16) for buf in rs_bufs(Q, HALF)]
    scratch = [
        V((T, D), bf16), V((3, D, 256), bf16), V((256, D), bf16), V((2, D, D), bf16),
        V((2, D, D), bf16), V((T, D), f32), V((T, D), bf16),
        V((T, T), bf16), V((T, T), bf16), V((T, 1), i32), V((1, T), i32), V((Q, 1), i32),
        V((1, Q), i32),
        V((2, T, D), bf16), V((2, T, D), bf16), V((2, T, D), bf16),
        V((T, D), bf16), V((T, D), bf16), V((D, T), bf16), V((3, T, 256), bf16),
        V((256, T), bf16), V((4, T, T), bf16), V((T, 256), bf16), V((256, T), bf16),
        V((T, D), bf16), *rs_bufs(Q, HALF),
        V((Q, D), bf16), V((2, T, 256), bf16), V((2, T, 256), bf16), *[V((2, T, D), bf16)] * 4,
        *pair_bufs, V((2, T, 256), bf16), V((2, T, 256), bf16),
        *pair_bufs, V((2, T, 256), bf16), V((2, T, 256), bf16), V((T, D), bf16),
        V((T, D), bf16), V((T, 256), bf16), V((256, T), bf16), V((3, T, 256), bf16),
        *rs_bufs(Q, HALF), V((T, D), bf16),
        V((T, D), bf16), V((D, D), bf16),
        V((T, D), bf16),
        V((4, 8, 128), f32), V((4, 8, 128), f32), V((G, 8, 128), f32),
        DMA((15,)), *[DMA((2, 2))] * 4, DMA((6, 4)), DMA((5, 4)), DMA((2, 8)), DMA((6,)),
    ]
    S = jax.ShapeDtypeStruct
    quarters = S((2, T, D), bf16)
    return pl.pallas_call(
        layer_kernel,
        name="layer",
        out_shape=[quarters] * 4
        + [S((T, D), bf16), S((T, D), bf16), S((T, T), bf16), S((D, D), bf16), S((4, 8, 128), f32)],
        in_specs=[vmem] * 6 + [hbm] * 6,
        out_specs=[hbm] * 8 + [vmem],
        scratch_shapes=scratch,
        compiler_params=pltpu.CompilerParams(
            collective_id=0, has_side_effects=True, vmem_limit_bytes=62 << 20
        ),
        cost_estimate=pl.CostEstimate(
            flops=24 * 10**9, bytes_accessed=30 * 2**20, transcendentals=4 * 10**6
        ),
    )(seg, route, g1, b1, g2, b2, tok, wqkv, wout, win, wbk, cot)


def finish_kernel(
    x_hbm, dpre_hbm, hid_hbm, g_hbm, w_hbm, u_hbm, gt_hbm, pmt_hbm, tok_hbm, nrm,
    win_out, wback_out, wqkv_out, wout_out, out_out, gt_out, n0, n1, n2, n3,
    x, dpre, hid, g, w, u, gt, pmt, tok, win, wback, wqkv, wout, out, gtok, load, store,
):
    vectors = [
        pltpu.make_async_copy(nrm.at[k], vector, store.at[6 + k])
        for k, vector in enumerate((n0, n1, n2, n3))
    ]
    pairs = [(x_hbm, x), (dpre_hbm, dpre), (hid_hbm, hid), (g_hbm, g)]
    loads = []
    for e in range(2):
        for i, (src, dst) in enumerate(pairs):
            loads.append(pltpu.make_async_copy(src.at[e], dst.at[e], load.at[e * 4 + i]))
    rest = [(w_hbm, w), (u_hbm, u), (gt_hbm, gt), (pmt_hbm, pmt), (tok_hbm, tok)]
    for i, (src, dst) in enumerate(rest):
        loads.append(pltpu.make_async_copy(src, dst, load.at[8 + i]))
    for copy in loads + vectors:
        copy.start()

    def outer(e, lhs, rhs, buf, dst, sem):
        @pl.loop(0, 4)
        def _(c):
            rows = pl.ds(pl.multiple_of(c * 256, 256), 256)
            buf[e, rows, :] = lax.dot_general(
                lhs[e, :, rows], rhs[e], (((0,), (0,)), ((), ())), preferred_element_type=f32
            )
            pltpu.make_async_copy(buf.at[e, rows, :], dst.at[e, rows, :], sem).start()

    for e in range(2):
        loads[e * 4].wait()
        loads[e * 4 + 1].wait()
        outer(e, x, dpre, win, win_out, store.at[0])
        loads[e * 4 + 2].wait()
        loads[e * 4 + 3].wait()
        outer(e, hid, g, wback, wback_out, store.at[1])
    loads[8].wait()
    for c, k in ((0, 2), (1, 3), (2, 1)):
        wqkv[c] = w[:, k * 256 : (k + 1) * 256].astype(f32)
    for k in range(4):
        wout[:, k * 256 : (k + 1) * 256] = w[k * 256 : (k + 1) * 256, :256].astype(f32)
    wq_store = pltpu.make_async_copy(wqkv, wqkv_out, store.at[2])
    wo_store = pltpu.make_async_copy(wout, wout_out, store.at[3])
    wq_store.start()
    wo_store.start()
    for copy in loads[9:]:
        copy.wait()

    @pl.loop(0, 2)
    def _(c):
        rows = pl.ds(pl.multiple_of(c * 256, 256), 256)
        out[rows, :] = tok[rows, :].astype(f32) + mm(pmt[rows, :], u[...])
        pltpu.make_async_copy(out.at[rows, :], out_out.at[rows, :], store.at[4]).start()
        gtok[rows, :] = mm(pmt[rows, :], gt[...])
        pltpu.make_async_copy(gtok.at[rows, :], gt_out.at[rows, :], store.at[5]).start()

    pltpu.make_async_copy(win, win_out, store.at[0]).wait()
    pltpu.make_async_copy(wback, wback_out, store.at[1]).wait()
    wq_store.wait()
    wo_store.wait()
    pltpu.make_async_copy(out, out_out, store.at[4]).wait()
    pltpu.make_async_copy(gtok, gt_out, store.at[5]).wait()
    for copy in vectors:
        copy.wait()


def finish(nrm, *operands):
    S = jax.ShapeDtypeStruct
    hbm = pl.BlockSpec(memory_space=pl.ANY)
    results = [
        S((2, D, D), f32), S((2, D, D), f32), S((3, D, 256), f32), S((256, D), f32),
        S((T, D), f32), S((T, D), f32),
    ]
    DMA = pltpu.SemaphoreType.DMA
    return pl.pallas_call(
        finish_kernel,
        name="finish",
        out_shape=results + [S((8, 128), f32)] * 4,
        in_specs=[hbm] * (len(operands) + 1),
        out_specs=[hbm] * (len(results) + 4),
        scratch_shapes=[pltpu.VMEM(a.shape, a.dtype) for a in (*operands, *results)]
        + [DMA((13,)), DMA((10,))],
        compiler_params=pltpu.CompilerParams(vmem_limit_bytes=60 << 20),
        cost_estimate=pl.CostEstimate(
            flops=8 * 2**30, bytes_accessed=37 * 2**20, transcendentals=0
        ),
    )(*operands, nrm)


def per_device(
    tokens, segment_ids, expert_of, norm1_gain, norm1_bias, norm2_gain, norm2_bias,
    w_qkv, w_out, w_in, w_back, cotangent,
):
    row = lambda v: v.reshape(1, D)
    x, g, hid, dpre, u, gt, pmt, w, nrm = layer(
        segment_ids, expert_of.reshape(1, T), row(norm1_gain), row(norm1_bias), row(norm2_gain), row(norm2_bias),
        tokens, w_qkv, w_out, w_in, w_back, cotangent,
    )
    grad_w_in, grad_w_back, grad_w_qkv, grad_w_out, output, grad_tokens, *vectors = finish(
        nrm, x, dpre, hid, g, w, u, gt, pmt, tokens
    )
    vectors = [v.reshape(D) for v in vectors]
    return (
        output, grad_tokens, vectors[0], vectors[1], vectors[2], vectors[3],
        grad_w_qkv, grad_w_out, grad_w_in, grad_w_back,
    )


def solution(mesh):
    return jax.shard_map(
        per_device,
        mesh=mesh,
        in_specs=(
            P("expert", None),
            P("expert", None),
            P("expert", None),
            P(),
            P(),
            P(),
            P(),
            P(None, None, "head"),
            P("head", None),
            P("expert", None, "head"),
            P("expert", "head", None),
            P("expert", None),
        ),
        out_specs=(
            P("expert", None),
            P("expert", None),
            P(),
            P(),
            P(),
            P(),
            P(None, None, "head"),
            P("head", None),
            P("expert", None, "head"),
            P("expert", "head", None),
        ),
        check_vma=False,
    )
```
